32 devices in a mesh: lat: 4 (over z), lon: 8 (over y, x, core).
Axes of the slice: x: 2, y: 2, z: 4, core: 2. Of those that a mesh axis runs over, the one named last changes fastest.
Arguments:
- tokens: float32 [4, 8, 512, 1024], P('lat', 'lon')
- norm_gain: float32 [1024], replicated, may hold values from 0.5 to 6, as said below
- qkv_weight: bfloat16 [1024, 3072], replicated, may hold values from -0.1875 to 0.1875
- out_weight: bfloat16 [1024, 1024], replicated, may hold values from -0.1875 to 0.1875
- band_counts: int32 [4], P('lat'), may hold values from 256 to 512, as said below
- halo_rows: int32 [4, 2, 128], replicated, may hold values from 0 to 511, as said below
- window_mask: int32 [4, 8, 4, 5], P('lat', 'lon'), may hold values from 0 to 1, as said below
Outputs:
- updated: float32 [4, 8, 512, 1024], P('lat', 'lon')
The draws below stay inside these ranges and needn't reach their ends.
Inputs may be any that keep to these rules, and one draw needn't show every extreme that they name: `band_counts`: counts lie between 256 and 512; some band has exactly 512 and some band exactly 256. `halo_rows`: every entry names a live slot of the neighbour band it refers to (the band itself where that neighbour does not exist). `window_mask`: entries are 0 or 1; the middle entry (offset 0) is always 1. `norm_gain`: gains are positive.
All inputs are finite; a program needn't handle non-finite values.
Results may differ from the reference program's by a relative error of at most 0.002.
The reference program's roundings to bfloat16 on the way (of `normed`, `projected` and `attended`) count: a program that leaves them out, or rounds other values in their place, can miss the bound.
Values may be sent and summed in bfloat16 or wider, within the bound.
No kernel may reach another device: no remote copies, remote signals or barrier semaphores. Data moves between devices by JAX's collectives and lax.ppermute only.
A program may use at most 192 MiB of HBM per device.

```python
import jax
import jax.numpy as jnp
from jax import lax

D = 1024
HEADS = 16
HEAD_DIM = 64
CAP = 512
QROWS = 128
REACH = 2
HALO = 128
NBANDS = 4
NSECT = 8
QBLK = 4


def shared_counts(key):
    folded = jax.random.fold_in(key, 11)
    first, second = jax.random.split(folded)
    counts = jax.random.randint(first, (NBANDS,), CAP // 2, CAP + 1)
    order = jax.random.permutation(second, NBANDS)
    counts = counts.at[order[0]].set(CAP).at[order[1]].set(CAP // 2)
    return counts.astype(jnp.int32)


def draw_band_counts(key, part):
    return shared_counts(key)


def draw_halo_rows(key, part):
    counts = shared_counts(key)
    band_ids = jnp.arange(NBANDS)
    north_counts = counts[jnp.maximum(band_ids - 1, 0)]
    south_counts = counts[jnp.minimum(band_ids + 1, NBANDS - 1)]
    offsets = jax.random.randint(jax.random.fold_in(key, 23), (NBANDS, 2, HALO), 0, 2 * HALO)
    offsets = offsets.at[:, :, 0].set(0)
    offsets = offsets.at[:, :, 1].set(2 * HALO - 1)
    edges = jnp.stack([north_counts, south_counts], axis=1)[:, :, None]
    return (edges - 1 - offsets).astype(jnp.int32)


def draw_window_mask(key, part):
    picks = jax.random.randint(jax.random.fold_in(key, 31), (NBANDS, NSECT, QBLK, 2 * REACH + 1), 0, 4)
    flags = (picks > 0).astype(jnp.int32)
    return flags.at[:, :, :, REACH].set(1)


def draw_tokens(key, part):
    shape = (NBANDS, NSECT, CAP, D)
    return jnp.clip(jax.random.normal(key, shape, jnp.float32), -6.0, 6.0)


def draw_norm_gain(key, part):
    return jax.random.uniform(key, (D,), jnp.float32, 0.5, 1.5)


def noise(own_key, dims, spread, bound, dtype=jnp.bfloat16):
    values = spread * jax.random.normal(own_key, dims, jnp.float32)
    return jnp.clip(values, min=-bound, max=bound).astype(dtype)


def setup_inputs(seed: int = 0) -> dict:
    key_of = jax.random.split(jax.random.key(seed), 8)
    return {
        "tokens": draw_tokens(jax.random.fold_in(key_of[7], 71), 0),
        "norm_gain": draw_norm_gain(jax.random.fold_in(key_of[7], 71), 0),
        "qkv_weight": noise(key_of[2], (D, 3 * D), D ** -0.5, 0.1875),
        "out_weight": noise(key_of[3], (D, D), D ** -0.5, 0.1875),
        "band_counts": draw_band_counts(jax.random.fold_in(key_of[7], 71), 0),
        "halo_rows": draw_halo_rows(jax.random.fold_in(key_of[7], 71), 0),
        "window_mask": draw_window_mask(jax.random.fold_in(key_of[7], 71), 0),
    }


epsilon = 1e-05

def normalize(values, gain):
    average = lax.optimization_barrier(jnp.mean(values, axis=-1, keepdims=True))
    centered = values - average
    variance = lax.optimization_barrier(jnp.mean(centered * centered, axis=-1, keepdims=True))
    return (centered * lax.rsqrt(variance + epsilon) * gain).astype(jnp.bfloat16)

def attend(queries, key_rows, allowed):
    query_heads = queries.astype(jnp.float32).reshape(CAP, HEADS, HEAD_DIM)
    key_heads = key_rows[:, :D].astype(jnp.float32).reshape(-1, HEADS, HEAD_DIM)
    value_heads = key_rows[:, D:].astype(jnp.float32).reshape(-1, HEADS, HEAD_DIM)
    scores = jnp.einsum('qhd,khd->hqk', query_heads, key_heads) * HEAD_DIM ** (-0.5)
    scores = jnp.where(allowed[None], scores, -jnp.inf)
    row_max = lax.optimization_barrier(jnp.max(scores, axis=-1, keepdims=True))
    weights = jnp.exp(scores - row_max)
    row_sum = lax.optimization_barrier(jnp.sum(weights, axis=-1, keepdims=True))
    rounded = lax.optimization_barrier(weights.astype(jnp.bfloat16))
    weighted = jnp.einsum('hqk,khd->hqd', rounded.astype(jnp.float32), value_heads)
    attended = (weighted / row_sum).transpose(1, 0, 2).reshape(CAP, D)
    return attended.astype(jnp.bfloat16)

def reference(tokens, norm_gain, qkv_weight, out_weight, band_counts, halo_rows, window_mask):
    normed = normalize(tokens, norm_gain)
    projected = jnp.dot(normed.reshape(-1, D), qkv_weight, preferred_element_type=jnp.float32).astype(jnp.bfloat16)
    projected = projected.reshape(NBANDS, NSECT, CAP, 3 * D)
    position = jnp.arange(CAP)

    def one_device(device_index):
        band_index = device_index // NSECT
        sector = device_index % NSECT
        key_valid = position < band_counts[band_index]
        row_flags = jnp.repeat(window_mask[band_index, sector] > 0, QROWS, axis=0)
        key_blocks = []
        allowed_blocks = []
        for offset in range(-REACH, REACH + 1):
            key_blocks.append(projected[band_index, (sector + offset) % NSECT, :, D:])
            allowed_blocks.append(row_flags[:, offset + REACH][:, None] & key_valid[None, :])
        north_band = jnp.maximum(band_index - 1, 0)
        south_band = jnp.minimum(band_index + 1, NBANDS - 1)
        key_blocks.append(projected[north_band, sector, :, D:][halo_rows[band_index, 0]])
        key_blocks.append(projected[south_band, sector, :, D:][halo_rows[band_index, 1]])
        allowed_blocks.append(jnp.broadcast_to(band_index > 0, (CAP, HALO)))
        allowed_blocks.append(jnp.broadcast_to(band_index < NBANDS - 1, (CAP, HALO)))
        key_rows = jnp.concatenate(key_blocks, axis=0)
        allowed = jnp.concatenate(allowed_blocks, axis=1)
        attended = attend(projected[band_index, sector, :, :D], key_rows, allowed)
        result = tokens[band_index, sector] + jnp.dot(attended, out_weight, preferred_element_type=jnp.float32)
        return jnp.where(key_valid[:, None], result, 0.0)
    results = lax.map(one_device, jnp.arange(NBANDS * NSECT))
    return results.reshape(NBANDS, NSECT, CAP, D)
```

```python
import functools
import math

import jax
import jax.numpy as jnp
from jax import lax
from jax.experimental import pallas as pl
from jax.experimental.pallas import tpu as pltpu
from jax.sharding import PartitionSpec as P

HEADS = 16
LANES = 128
GROUP = 256
PARTS = 2
NEG = -1e30
FLOOR = -1e25
LOG2E = math.log2(math.e)
VMEM_LIMIT = 48 * 1024 * 1024

epsilon = 1e-05


def contract_last(a, b):
    return lax.dot_general(a, b, (((1,), (1,)), ((), ())), preferred_element_type=jnp.float32)


def matmul(a, b):
    return jnp.dot(a, b, preferred_element_type=jnp.float32)


def norm_kernel(bands, tokens_ref, gain_ref, halo_rows_ref, *outs):
    normed_refs, (north_ref, south_ref) = outs[:-2], outs[-2:]
    values = tokens_ref[...]
    average = jnp.mean(values, axis=-1, keepdims=True)
    centered = values - average
    variance = jnp.mean(centered * centered, axis=-1, keepdims=True)
    normed = (centered * lax.rsqrt(variance + epsilon) * gain_ref[...]).astype(jnp.bfloat16)
    rows = values.shape[0]
    part = rows // len(normed_refs)
    for i, ref in enumerate(normed_refs):
        ref[...] = normed[i * part : (i + 1) * part]
    band = lax.axis_index("lat")
    lists = ((jnp.maximum(band - 1, 0), 1, north_ref), (jnp.minimum(band + 1, bands - 1), 0, south_ref))
    for owner, side, out in lists:
        wanted = halo_rows_ref[pl.ds(owner, 1), side, :]
        slots = lax.broadcasted_iota(jnp.int32, (rows, wanted.shape[1]), 0)
        picks = (slots == wanted).astype(jnp.float32).astype(jnp.bfloat16)
        picked = lax.dot_general(
            picks, normed, (((0,), (0,)), ((), ())), preferred_element_type=jnp.float32
        )
        out[...] = picked.astype(jnp.bfloat16)


def norm_call(tokens, gain, halo_rows):
    rows, width = tokens.shape
    bands, _, halo = halo_rows.shape
    whole = pl.BlockSpec(memory_space=pltpu.VMEM)
    part = jax.ShapeDtypeStruct((rows // PARTS, width), jnp.bfloat16)
    edge = jax.ShapeDtypeStruct((halo, width), jnp.bfloat16)
    return pl.pallas_call(
        functools.partial(norm_kernel, bands),
        out_shape=[part] * PARTS + [edge] * 2,
        in_specs=[whole] * 3,
        out_specs=[whole] * (PARTS + 2),
        compiler_params=pltpu.CompilerParams(vmem_limit_bytes=VMEM_LIMIT),
        cost_estimate=pl.CostEstimate(flops=10 * rows * width, bytes_accessed=6 * rows * width, transcendentals=0),
        name="layer_norm",
    )(tokens, gain.reshape(1, width), halo_rows)


def pair_attention(query, tiles, head_size):
    rows = query.shape[0]
    low = lax.broadcasted_iota(jnp.int32, (rows, LANES), 1) < head_size
    ones = jnp.ones((tiles[0][1].shape[0], LANES), jnp.bfloat16)
    outs = []
    for head in range(2):
        own = jnp.where(low if head == 0 else ~low, query, jnp.zeros_like(query))
        scored = []
        peak = None
        for key, value, key_bias, row_bias in tiles:
            scores = contract_last(own, key) * (LOG2E * head_size**-0.5)
            chunks = []
            for c in range(key.shape[0] // LANES):
                chunk = scores[:, c * LANES : (c + 1) * LANES]
                if key_bias[c] is not None:
                    chunk = chunk + key_bias[c]
                chunks.append(chunk)
            tile_peak = functools.reduce(jnp.maximum, chunks)
            tile_peak = tile_peak + row_bias
            peak = tile_peak if peak is None else jnp.maximum(peak, tile_peak)
            scored.append(chunks)
        top = jnp.maximum(jnp.max(peak, axis=-1, keepdims=True), FLOOR)
        weights, values = [], []
        for chunks, (key, value, key_bias, row_bias) in zip(scored, tiles):
            shift = top - row_bias
            weights += [jnp.exp2(chunk - shift).astype(jnp.bfloat16) for chunk in chunks]
            values.append(jnp.concatenate([value, jnp.ones((value.shape[0], LANES), jnp.bfloat16)], axis=1))
        result = matmul(jnp.concatenate(weights, axis=1), jnp.concatenate(values, axis=0))
        outs.append((result[:, :LANES], result[:, LANES:], top))
    (acc0, sum0, top0), (acc1, sum1, top1) = outs
    return jnp.where(low, acc0, acc1), jnp.where(low, sum0, sum1), jnp.where(low, top0, top1)


def stage_kernel(spec, *refs):
    first, last, sectors, halos, head_size = spec
    refs = list(refs)

    def take(count):
        taken = refs[:count]
        del refs[:count]
        return taken

    counts_ref, mask_ref = take(2)
    sector_refs = [take(PARTS) for _ in sectors]
    halo_refs = take(2) if halos else []
    wq_ref = take(1)[0] if first else None
    wk_ref, wv_ref = take(2)
    query_in = take(1)[0] if not first else None
    state_in = take(3) if not first else None
    if last:
        tokens_ref, wo_ref, out_ref, res_ref = take(4)
    else:
        if first:
            query_out = take(1)[0]
        state_out = take(3)

    blocks, reach = mask_ref.shape[0], mask_ref.shape[1] // 2
    lon, lat = lax.axis_index("lon"), lax.axis_index("lat")
    bands = lax.axis_size("lat")
    core, odd = lon % 2, (lon // 2) % 2
    offsets = {"own": 0, "partner": 1 - 2 * core, "same": 2 - 4 * odd, "across": 4 * odd - 2, "near": 2 * core - 1}
    count = counts_ref[0]

    wk, wv = wk_ref[...], wv_ref[...]
    if first:
        query = jnp.concatenate([matmul(ref[...], wq_ref[...]).astype(jnp.bfloat16) for ref in sector_refs[0]], axis=0)
        query_out[...] = query
    else:
        query = query_in[...]
    rows = query.shape[0]
    width = query.shape[1]
    block_rows = rows // blocks
    part_rows = rows // PARTS

    tiles = []
    for name, parts in zip(sectors, sector_refs):
        column = reach + offsets[name]
        row_bias = jnp.concatenate(
            [
                jnp.full((block_rows, LANES), jnp.where(mask_ref[b, column] > 0, 0.0, NEG), jnp.float32)
                for b in range(blocks)
            ],
            axis=0,
        )
        for i, ref in enumerate(parts):
            key = matmul(ref[...], wk).astype(jnp.bfloat16)
            value = matmul(ref[...], wv).astype(jnp.bfloat16)
            bias = []
            for c in range(part_rows // LANES):
                start = i * part_rows + c * LANES
                if start + LANES <= rows // 2:
                    bias.append(None)
                else:
                    slot = start + lax.broadcasted_iota(jnp.int32, (1, LANES), 1)
                    bias.append(jnp.where(slot < count, 0.0, NEG))
            tiles.append((key, value, bias, row_bias))
    for ref, seen in zip(halo_refs, (lat > 0, lat < bands - 1)):
        key = matmul(ref[...], wk).astype(jnp.bfloat16)
        value = matmul(ref[...], wv).astype(jnp.bfloat16)
        row_bias = jnp.full((rows, LANES), jnp.where(seen, 0.0, NEG), jnp.float32)
        tiles.append((key, value, [None] * (key.shape[0] // LANES), row_bias))

    attended = []
    for pair in range(width // LANES):
        lanes = slice(pair * LANES, (pair + 1) * LANES)
        pair_tiles = [(key[:, lanes], value[:, lanes], kb, rb) for key, value, kb, rb in tiles]
        acc, total, top = pair_attention(query[:, lanes], pair_tiles, head_size)
        if not first:
            old_acc, old_total, old_top = [ref[:, lanes] for ref in state_in]
            new_top = jnp.maximum(old_top, top)
            old_scale, scale = jnp.exp2(old_top - new_top), jnp.exp2(top - new_top)
            acc = old_acc * old_scale + acc * scale
            total = old_total * old_scale + total * scale
            top = new_top
        if last:
            attended.append((acc / total).astype(jnp.bfloat16))
        else:
            for ref, value in zip(state_out, (acc, total, top)):
                ref[:, lanes] = value
    if last:
        step = pl.program_id(0)

        @pl.when(step == 0)
        def _():
            res_ref[...] = jnp.zeros_like(res_ref)

        columns = pl.ds(pl.multiple_of(step * width, width), width)
        res_ref[:, columns] += tokens_ref[...]
        res_ref[...] += matmul(jnp.concatenate(attended, axis=1), wo_ref[...])

        @pl.when(step == pl.num_programs(0) - 1)
        def _():
            slot = lax.broadcasted_iota(jnp.int32, res_ref.shape, 0)
            out_ref[...] = jnp.where(slot < count, res_ref[...], 0.0)


def stage_call(counts, mask, sectors, sector_parts, halos, qkv_weight, query=None, state=None, tokens=None, out_weight=None):
    first, last = query is None, tokens is not None
    model, width = qkv_weight.shape[0], qkv_weight.shape[1] // 3
    head_size = width // HEADS
    rows = sum(p.shape[0] for p in sector_parts[0])
    steps = width // GROUP
    smem = pl.BlockSpec(memory_space=pltpu.SMEM)

    def fixed(shape):
        return pl.BlockSpec(shape, lambda g: (0, 0), pipeline_mode=pl.Buffered(1))

    def weight(third):
        return pl.BlockSpec((model, GROUP), lambda g: (0, third * steps + g))

    columns = pl.BlockSpec((rows, GROUP), lambda g: (0, g))
    args, specs = [counts, mask], [smem, smem]
    for parts in sector_parts:
        args += parts
        specs += [fixed(p.shape) for p in parts]
    for halo in halos:
        args.append(halo)
        specs.append(fixed(halo.shape))
    for third in range(0 if first else 1, 3):
        args.append(qkv_weight)
        specs.append(weight(third))
    if not first:
        args += [query, *state]
        specs += [columns] * 4
    scratch = []
    state_shape = jax.ShapeDtypeStruct((rows, width), jnp.float32)
    if last:
        args += [tokens, out_weight]
        specs += [columns, pl.BlockSpec((GROUP, out_weight.shape[1]), lambda g: (g, 0))]
        out_shape = [state_shape]
        out_specs = [pl.BlockSpec((rows, width), lambda g: (0, 0), pipeline_mode=pl.Buffered(1))]
        scratch = [pltpu.VMEM((rows, width), jnp.float32)]
    else:
        out_shape = [state_shape] * 3
        out_specs = [columns] * 3
        if first:
            out_shape = [jax.ShapeDtypeStruct((rows, width), jnp.bfloat16)] + out_shape
            out_specs = [columns] + out_specs
    keys = sum(p.shape[0] for parts in sector_parts for p in parts) + sum(h.shape[0] for h in halos)
    flops = 2 * keys * model * 2 * width + 16 * rows * keys * width
    flops += 2 * rows * model * width * (int(first) + int(last))
    moved = sum(a.size * a.dtype.itemsize for a in args[2:] if a is not qkv_weight) + 3 * model * width * 2
    outs = pl.pallas_call(
        functools.partial(stage_kernel, (first, last, sectors, bool(halos), head_size)),
        out_shape=out_shape,
        grid=(steps,),
        in_specs=specs,
        out_specs=out_specs,
        scratch_shapes=scratch,
        compiler_params=pltpu.CompilerParams(vmem_limit_bytes=VMEM_LIMIT),
        cost_estimate=pl.CostEstimate(flops=flops, bytes_accessed=moved, transcendentals=rows * keys * HEADS),
        name="attend_" + "_".join(sectors),
    )(*args)
    if last:
        return outs[0]
    if first:
        return outs[0], outs[1:]
    return outs


def permuted(values, axis, target):
    size = lax.axis_size(axis)
    pairs = [(i, target(i)) for i in range(size) if 0 <= target(i) < size]
    return [lax.ppermute(v, axis, pairs) for v in values]


def on_device(tokens, norm_gain, qkv_weight, out_weight, band_counts, halo_rows, window_mask):
    mask = window_mask[0, 0]
    ring = lax.axis_size("lon")
    assert mask.shape[1] == 5 and ring % 4 == 0 and ring >= 8
    local = tokens[0, 0]
    outs = norm_call(local, norm_gain, halo_rows)
    own, north_rows, south_rows = outs[:PARTS], outs[PARTS], outs[PARTS + 1]

    partner = permuted(own, "lon", lambda i: i ^ 1)
    same = permuted(own, "lon", lambda i: i ^ 2)
    from_south = permuted([north_rows], "lat", lambda b: b - 1)[0]
    from_north = permuted([south_rows], "lat", lambda b: b + 1)[0]

    across = permuted(same, "lon", lambda i: (i + (4 if (i // 2) % 2 == 0 else -4)) % ring)
    lon = lax.axis_index("lon")
    gives_same = lon % 2 == (lon // 2) % 2
    near = permuted([jnp.where(gives_same, s, a) for s, a in zip(same, across)], "lon", lambda i: i ^ 1)

    query, state = stage_call(band_counts, mask, ["own"], [own], [], qkv_weight)
    state = stage_call(band_counts, mask, ["partner"], [partner], [from_north, from_south], qkv_weight, query, state)
    state = stage_call(band_counts, mask, ["same"], [same], [], qkv_weight, query, state)
    result = stage_call(
        band_counts, mask, ["across", "near"], [across, near], [], qkv_weight, query, state, local, out_weight
    )
    return result[None, None]


def solution(mesh):
    in_specs = (
        P("lat", "lon", None, None),
        P(),
        P(),
        P(),
        P("lat"),
        P(),
        P("lat", "lon", None, None),
    )
    out_specs = P("lat", "lon", None, None)
    return jax.shard_map(
        on_device, mesh=mesh, in_specs=in_specs, out_specs=out_specs, check_vma=False
    )
```

```python
import functools
import math

import jax
import jax.numpy as jnp
from jax import lax
from jax.experimental import pallas as pl
from jax.experimental.pallas import tpu as pltpu
from jax.sharding import PartitionSpec as P

HEADS = 16
LANES = 128
GROUP = 256
PARTS = 2
NEG = -1e30
FLOOR = -1e25
LOG2E = math.log2(math.e)
SUM_MIN, SUM_MAX = 2.0**-60, 2.0**100
VMEM_LIMIT = 32 * 1024 * 1024

epsilon = 1e-05


def contract_last(a, b):
    return lax.dot_general(a, b, (((1,), (1,)), ((), ())), preferred_element_type=jnp.float32)


def matmul(a, b):
    return jnp.dot(a, b, preferred_element_type=jnp.float32)


def norm_kernel(bands, tokens_ref, gain_ref, halo_rows_ref, *refs):
    part_refs, (north_ref, south_ref), picked_ref = refs[:PARTS], refs[PARTS : PARTS + 2], refs[PARTS + 2]
    step, steps = pl.program_id(0), pl.num_programs(0)
    values = tokens_ref[...]
    average = jnp.mean(values, axis=-1, keepdims=True)
    centered = values - average
    variance = jnp.mean(centered * centered, axis=-1, keepdims=True)
    normed = (centered * lax.rsqrt(variance + epsilon) * gain_ref[...]).astype(jnp.bfloat16)
    each = steps // PARTS
    for i, ref in enumerate(part_refs):

        @pl.when(step // each == i)
        def _(ref=ref):
            ref[...] = normed

    @pl.when(step == 0)
    def _():
        picked_ref[...] = jnp.zeros_like(picked_ref)

    band = lax.axis_index("lat")
    lists = ((jnp.maximum(band - 1, 0), 1, north_ref), (jnp.minimum(band + 1, bands - 1), 0, south_ref))
    rows = values.shape[0]
    for which, (owner, side, out) in enumerate(lists):
        wanted = halo_rows_ref[pl.ds(owner, 1), side, :]
        slots = step * rows + lax.broadcasted_iota(jnp.int32, (rows, wanted.shape[1]), 0)
        picks = (slots == wanted).astype(jnp.float32).astype(jnp.bfloat16)
        picked = lax.dot_general(
            picks, normed, (((0,), (0,)), ((), ())), preferred_element_type=jnp.float32
        )
        picked_ref[which] += picked

        @pl.when(step == steps - 1)
        def _(which=which, out=out):
            out[...] = picked_ref[which].astype(jnp.bfloat16)


def norm_call(tokens, gain, halo_rows):
    rows, width = tokens.shape
    bands, _, halo = halo_rows.shape
    each = 2
    steps = PARTS * each
    block = rows // steps
    part = jax.ShapeDtypeStruct((rows // PARTS, width), jnp.bfloat16)
    edge = jax.ShapeDtypeStruct((halo, width), jnp.bfloat16)

    def part_spec(i):
        return pl.BlockSpec((block, width), lambda g: (jnp.clip(g - i * each, 0, each - 1), 0))

    return pl.pallas_call(
        functools.partial(norm_kernel, bands),
        out_shape=[part] * PARTS + [edge] * 2,
        grid=(steps,),
        in_specs=[
            pl.BlockSpec((block, width), lambda g: (g, 0)),
            pl.BlockSpec((1, width), lambda g: (0, 0)),
            pl.BlockSpec(halo_rows.shape, lambda g: (0, 0, 0)),
        ],
        out_specs=[part_spec(i) for i in range(PARTS)] + [pl.BlockSpec((halo, width), lambda g: (0, 0))] * 2,
        scratch_shapes=[pltpu.VMEM((2, halo, width), jnp.float32)],
        compiler_params=pltpu.CompilerParams(vmem_limit_bytes=VMEM_LIMIT),
        cost_estimate=pl.CostEstimate(flops=10 * rows * width, bytes_accessed=6 * rows * width, transcendentals=0),
        name="layer_norm",
    )(tokens, gain.reshape(1, width), halo_rows)


def sector_columns(lon, reach):
    core, odd = lon % 2, (lon // 2) % 2
    return {
        "own": reach,
        "partner": reach + 1 - 2 * core,
        "same": reach + 2 - 4 * odd,
        "across": reach + 4 * odd - 2,
        "near": reach + 2 * core - 1,
    }


def block_bias(mask_ref, column, rows, dtype):
    blocks = mask_ref.shape[0]
    values = [jnp.where(mask_ref[b, column] > 0, 0.0, NEG) for b in range(blocks)]
    return jnp.concatenate([jnp.full((rows // blocks, LANES), v, jnp.float32) for v in values], axis=0).astype(dtype)


def safe_group(query, weights, sources, counts_ref, mask_ref, scratch, head_size):
    rows_ref, key_ref, value_ref, top_ref, sum_ref, acc_ref, flag_ref, limit_ref, sem = scratch
    rows = query.shape[0]
    wk, wv = weights
    tile = sources[0][0].shape[0]
    tiles = len(sources)
    blocks = mask_ref.shape[0]
    for t, (ref, column, seen, start) in enumerate(sources):
        size = ref.shape[0]
        copy = pltpu.make_async_copy(ref, rows_ref.at[pl.ds(0, size)], sem)
        copy.start()
        copy.wait()
        key_ref[pl.ds(t * tile, size)] = matmul(rows_ref[pl.ds(0, size)], wk[...]).astype(jnp.bfloat16)
        value_ref[pl.ds(t * tile, size)] = matmul(rows_ref[pl.ds(0, size)], wv[...]).astype(jnp.bfloat16)
        if size < tile:
            rest = pl.ds(t * tile + size, tile - size)
            key_ref[rest] = jnp.zeros((tile - size, key_ref.shape[1]), jnp.bfloat16)
            value_ref[rest] = jnp.zeros((tile - size, key_ref.shape[1]), jnp.bfloat16)
        for b in range(blocks):
            flag_ref[t, b] = mask_ref[b, column] if column is not None else 1
        if column is None:
            limit_ref[t] = jnp.where(seen, size, 0)
        else:
            limit_ref[t] = counts_ref[0] - start
    low = lax.broadcasted_iota(jnp.int32, (rows, LANES), 1) < head_size
    outs = []
    for pair in range(query.shape[1] // LANES):
        lanes = slice(pair * LANES, (pair + 1) * LANES)
        halves = []
        for head in range(2):
            own = jnp.where(low if head == 0 else ~low, query[:, lanes], jnp.zeros((), jnp.bfloat16))
            top_ref[...] = jnp.full_like(top_ref, FLOOR)
            sum_ref[...] = jnp.zeros_like(sum_ref)
            acc_ref[...] = jnp.zeros_like(acc_ref)

            def body(t, carry, own=own, lanes=lanes):
                at = pl.ds(pl.multiple_of(t * tile, tile), tile)
                scores = contract_last(own, key_ref[at, lanes]) * (LOG2E * head_size**-0.5)
                slot = lax.broadcasted_iota(jnp.int32, (1, tile), 1)
                scores = scores + jnp.where(slot < limit_ref[t], 0.0, NEG)
                row_bias = jnp.concatenate(
                    [
                        jnp.full((rows // blocks, 1), jnp.where(flag_ref[t, b] > 0, 0.0, NEG), jnp.float32)
                        for b in range(blocks)
                    ],
                    axis=0,
                )
                scores = scores + row_bias
                old = top_ref[...]
                new = jnp.maximum(old, jnp.max(scores, axis=-1, keepdims=True))
                scale = jnp.exp2(old - new)
                weight = jnp.exp2(scores - new[:, :1])
                sum_ref[...] = sum_ref[...] * scale + jnp.sum(weight, axis=-1, keepdims=True)
                acc_ref[...] = acc_ref[...] * scale + matmul(weight.astype(jnp.bfloat16), value_ref[at, lanes])
                top_ref[...] = new
                return carry

            lax.fori_loop(0, tiles, body, 0)
            halves.append(acc_ref[...] / sum_ref[...])
        outs.append(jnp.where(low, *halves).astype(jnp.bfloat16))
    return jnp.concatenate(outs, axis=1)


def stage_kernel(spec, *refs):
    first, last, sectors, halos, head_size = spec
    refs = list(refs)

    def take(count):
        taken = refs[:count]
        del refs[:count]
        return taken

    counts_ref, mask_ref = take(2)
    sector_refs = [take(PARTS) for _ in sectors]
    halo_refs = take(2) if halos else []
    wq_ref = take(1)[0] if first else None
    wk_ref, wv_ref = take(2)
    if not first:
        query_in, acc_in, sum_in = take(3)
    if last:
        tokens_ref, wo_ref = take(2)
        all_refs = take(5 * PARTS + 2)
        out_ref, res_ref, att_ref = take(3)
    else:
        if first:
            query_out = take(1)[0]
        acc_out, sum_out = take(2)

    reach = mask_ref.shape[1] // 2
    lon, lat = lax.axis_index("lon"), lax.axis_index("lat")
    bands = lax.axis_size("lat")
    columns = sector_columns(lon, reach)
    count = counts_ref[0]

    wk, wv = wk_ref[...], wv_ref[...]
    if first:
        query = jnp.concatenate([matmul(ref[...], wq_ref[...]).astype(jnp.bfloat16) for ref in sector_refs[0]], axis=0)
        query_out[...] = query
    else:
        query = query_in[...]
    rows, width = query.shape
    scaled = query.astype(jnp.float32) * (LOG2E * head_size**-0.5)
    query_hi = scaled.astype(jnp.bfloat16)
    query_lo = (scaled - query_hi.astype(jnp.float32)).astype(jnp.bfloat16)

    tiles = []
    zero = jnp.zeros((), jnp.bfloat16)
    one = jnp.ones((), jnp.bfloat16)
    for name, parts in zip(sectors, sector_refs):
        row_bias = block_bias(mask_ref, columns[name], rows, jnp.bfloat16)
        for i, ref in enumerate(parts):
            key = matmul(ref[...], wk).astype(jnp.bfloat16)
            value = matmul(ref[...], wv)
            start = i * ref.shape[0]
            live = start + lax.broadcasted_iota(jnp.int32, value.shape, 0) < count
            value = jnp.where(live, value, 0.0).astype(jnp.bfloat16)
            ones = jnp.where(live[:, :LANES], 1.0, 0.0)
            tiles.append((key, value, ones, row_bias))
    for ref, seen in zip(halo_refs, (lat > 0, lat < bands - 1)):
        key = matmul(ref[...], wk).astype(jnp.bfloat16)
        there = jnp.where(seen, 1.0, 0.0)
        value = (matmul(ref[...], wv) * there).astype(jnp.bfloat16)
        ones = jnp.full((ref.shape[0], LANES), there, jnp.float32)
        tiles.append((key, value, ones, None))

    low = lax.broadcasted_iota(jnp.int32, (rows, LANES), 1) < head_size
    total = None
    accs = []
    for pair in range(width // LANES):
        lanes = slice(pair * LANES, (pair + 1) * LANES)
        halves = []
        for head in range(2):
            half = low if head == 0 else ~low
            hi = query_hi[:, lanes]
            lo = jnp.where(half, query_lo[:, lanes], zero)
            weights, values = [], []
            for key, value, ones, row_bias in tiles:
                size = key.shape[0]
                key_half = (lax.broadcasted_iota(jnp.int32, (size, LANES), 1) < head_size) == (head == 0)
                left = jnp.where(half, hi, zero if row_bias is None else row_bias)
                left = jnp.concatenate([left, lo], axis=1)
                right = jnp.concatenate([jnp.where(key_half, key[:, lanes], one), key[:, lanes]], axis=1)
                weights.append(jnp.exp2(contract_last(left, right)).astype(jnp.bfloat16))
                here = lax.broadcasted_iota(jnp.int32, (size, LANES), 1) == 2 * pair + head
                summing = jnp.where(here, ones, 0.0).astype(jnp.bfloat16)
                values.append(jnp.concatenate([value[:, lanes], summing], axis=1))
            result = matmul(jnp.concatenate(weights, axis=1), jnp.concatenate(values, axis=0))
            halves.append(result[:, :LANES])
            total = result[:, LANES:] if total is None else total + result[:, LANES:]
        accs.append(jnp.where(low, *halves))
    acc = jnp.concatenate(accs, axis=1)
    if not first:
        acc = acc + acc_in[...]
        total = total + sum_in[...]
    if not last:
        acc_out[...] = acc
        sum_out[...] = total
        return

    inverse = 1.0 / total
    used = lax.broadcasted_iota(jnp.int32, total.shape, 1) < width // head_size
    fine = ((total > SUM_MIN) & (total < SUM_MAX)) | ~used
    attended = []
    for pair in range(width // LANES):
        lanes = slice(pair * LANES, (pair + 1) * LANES)
        scale = jnp.where(low, inverse[:, 2 * pair : 2 * pair + 1], inverse[:, 2 * pair + 1 : 2 * pair + 2])
        attended.append((acc[:, lanes] * scale).astype(jnp.bfloat16))
    att_ref[...] = jnp.concatenate(attended, axis=1)

    @pl.when(jnp.min(fine.astype(jnp.float32)) < 0.5)
    def _():
        sources = []
        for s, name in enumerate(("own", "partner", "same", "across", "near")):
            for i, ref in enumerate(all_refs[s * PARTS : (s + 1) * PARTS]):
                sources.append((ref, columns[name], None, i * ref.shape[0]))
        for ref, seen in zip(all_refs[5 * PARTS :], (lat > 0, lat < bands - 1)):
            sources.append((ref, None, seen, 0))
        att_ref[...] = safe_group(query, (wk_ref, wv_ref), sources, counts_ref, mask_ref, refs, head_size)

    step = pl.program_id(0)

    @pl.when(step == 0)
    def _():
        res_ref[...] = jnp.zeros_like(res_ref)

    at = pl.ds(pl.multiple_of(step * width, width), width)
    res_ref[:, at] += tokens_ref[...]
    res_ref[...] += matmul(att_ref[...], wo_ref[...])

    @pl.when(step == pl.num_programs(0) - 1)
    def _():
        slot = lax.broadcasted_iota(jnp.int32, res_ref.shape, 0)
        out_ref[...] = jnp.where(slot < count, res_ref[...], 0.0)


def stage_call(counts, mask, sectors, sector_parts, halos, qkv_weight, query=None, state=None, final=None):
    first, last = query is None, final is not None
    model, width = qkv_weight.shape[0], qkv_weight.shape[1] // 3
    head_size = width // HEADS
    rows = sum(p.shape[0] for p in sector_parts[0])
    steps = width // GROUP
    smem = pl.BlockSpec(memory_space=pltpu.SMEM)

    def fixed(shape):
        return pl.BlockSpec(shape, lambda g: (0, 0), pipeline_mode=pl.Buffered(1))

    def weight(third):
        return pl.BlockSpec((model, GROUP), lambda g: (0, third * steps + g))

    columns = pl.BlockSpec((rows, GROUP), lambda g: (0, g))
    sums = pl.BlockSpec((rows, LANES), lambda g: (0, g))
    args, specs = [counts, mask], [smem, smem]
    for parts in sector_parts:
        args += parts
        specs += [fixed(p.shape) for p in parts]
    for halo in halos:
        args.append(halo)
        specs.append(fixed(halo.shape))
    for third in range(0 if first else 1, 3):
        args.append(qkv_weight)
        specs.append(weight(third))
    if not first:
        args += [query, *state]
        specs += [columns, columns, sums]
    scratch = []
    wide = jax.ShapeDtypeStruct((rows, width), jnp.float32)
    moved = sum(a.size * a.dtype.itemsize for a in args[2:] if a is not qkv_weight) + 3 * model * width * 2
    if last:
        tokens, out_weight, sources = final
        args += [tokens, out_weight, *sources]
        specs += [columns, pl.BlockSpec((GROUP, out_weight.shape[1]), lambda g: (g, 0))]
        specs += [pl.BlockSpec(memory_space=pl.ANY)] * len(sources)
        out_shape = [wide]
        out_specs = [fixed((rows, width))]
        part = rows // PARTS
        scratch = [
            pltpu.VMEM((rows, width), jnp.float32),
            pltpu.VMEM((rows, GROUP), jnp.bfloat16),
            pltpu.VMEM((part, model), jnp.bfloat16),
            pltpu.VMEM((part * len(sources), GROUP), jnp.bfloat16),
            pltpu.VMEM((part * len(sources), GROUP), jnp.bfloat16),
            pltpu.VMEM((rows, LANES), jnp.float32),
            pltpu.VMEM((rows, LANES), jnp.float32),
            pltpu.VMEM((rows, LANES), jnp.float32),
            pltpu.SMEM((len(sources), mask.shape[0]), jnp.int32),
            pltpu.SMEM((len(sources),), jnp.int32),
            pltpu.SemaphoreType.DMA,
        ]
    else:
        out_shape = [wide, jax.ShapeDtypeStruct((rows, LANES * steps), jnp.float32)]
        out_specs = [columns, sums]
        if first:
            out_shape = [jax.ShapeDtypeStruct((rows, width), jnp.bfloat16)] + out_shape
            out_specs = [columns] + out_specs
    keys = sum(p.shape[0] for parts in sector_parts for p in parts) + sum(h.shape[0] for h in halos)
    flops = 2 * keys * model * 2 * width + 16 * rows * keys * width
    flops += 2 * rows * model * width * (int(first) + int(last))
    outs = pl.pallas_call(
        functools.partial(stage_kernel, (first, last, sectors, bool(halos), head_size)),
        out_shape=out_shape,
        grid=(steps,),
        in_specs=specs,
        out_specs=out_specs,
        scratch_shapes=scratch,
        compiler_params=pltpu.CompilerParams(vmem_limit_bytes=VMEM_LIMIT),
        cost_estimate=pl.CostEstimate(flops=flops, bytes_accessed=moved, transcendentals=rows * keys * HEADS),
        name="attend_" + "_".join(sectors),
    )(*args)
    if last:
        return outs[0]
    if first:
        return outs[0], outs[1:]
    return outs


def permuted(values, axis, target):
    size = lax.axis_size(axis)
    pairs = [(i, target(i)) for i in range(size) if 0 <= target(i) < size]
    return [lax.ppermute(v, axis, pairs) for v in values]


def on_device(tokens, norm_gain, qkv_weight, out_weight, band_counts, halo_rows, window_mask):
    mask = window_mask[0, 0]
    ring = lax.axis_size("lon")
    assert mask.shape[1] == 5 and ring % 4 == 0 and ring >= 8
    local = tokens[0, 0]
    outs = norm_call(local, norm_gain, halo_rows)
    own, north_rows, south_rows = outs[:PARTS], outs[PARTS], outs[PARTS + 1]

    partner = permuted(own, "lon", lambda i: i ^ 1)
    same = permuted(own, "lon", lambda i: i ^ 2)
    from_south = permuted([north_rows], "lat", lambda b: b - 1)[0]
    from_north = permuted([south_rows], "lat", lambda b: b + 1)[0]

    across = permuted(same, "lon", lambda i: (i + (4 if (i // 2) % 2 == 0 else -4)) % ring)
    lon = lax.axis_index("lon")
    gives_same = lon % 2 == (lon // 2) % 2
    near = permuted([jnp.where(gives_same, s, a) for s, a in zip(same, across)], "lon", lambda i: i ^ 1)

    halos = [from_north, from_south]
    query, state = stage_call(band_counts, mask, ["own"], [own], [], qkv_weight)
    state = stage_call(band_counts, mask, ["partner"], [partner], halos, qkv_weight, query, state)
    state = stage_call(band_counts, mask, ["same"], [same], [], qkv_weight, query, state)
    final = (local, out_weight, [*own, *partner, *same, *across, *near, *halos])
    result = stage_call(band_counts, mask, ["across", "near"], [across, near], [], qkv_weight, query, state, final)
    return result[None, None]


def solution(mesh):
    in_specs = (
        P("lat", "lon", None, None),
        P(),
        P(),
        P(),
        P("lat"),
        P(),
        P("lat", "lon", None, None),
    )
    out_specs = P("lat", "lon", None, None)
    return jax.shard_map(
        on_device, mesh=mesh, in_specs=in_specs, out_specs=out_specs, check_vma=False
    )
```

```python
import functools
import math

import jax
import jax.numpy as jnp
from jax import lax
from jax.experimental import pallas as pl
from jax.experimental.pallas import tpu as pltpu
from jax.sharding import PartitionSpec as P

HEADS = 16
LANES = 128
GROUP = 256
PARTS = 2
NEG = -1e30
FLOOR = -1e25
LOG2E = math.log2(math.e)
SUM_MIN, SUM_MAX = 2.0**-60, 2.0**100
VMEM_LIMIT = 60 * 1024 * 1024
CHUNKS = 4

epsilon = 1e-05


def contract_last(a, b):
    return lax.dot_general(a, b, (((1,), (1,)), ((), ())), preferred_element_type=jnp.float32)


def matmul(a, b):
    return jnp.dot(a, b, preferred_element_type=jnp.float32)


def norm_kernel(bands, tokens_hbm, gain_hbm, halo_rows_hbm, *refs):
    outs = refs[: PARTS + 3]
    tokens_ref, gain_ref, halo_rows_ref, normed_ref, edge_ref, in_sem, out_sem = refs[PARTS + 3 :]
    rows = tokens_ref.shape[0]
    block = rows // CHUNKS

    def chunk(i):
        at = pl.ds(i * block, block)
        return pltpu.make_async_copy(tokens_hbm.at[at], tokens_ref.at[at], in_sem.at[i])

    small = [
        pltpu.make_async_copy(gain_hbm, gain_ref, in_sem.at[CHUNKS]),
        pltpu.make_async_copy(halo_rows_hbm, halo_rows_ref, in_sem.at[CHUNKS + 1]),
    ]
    for copy in [chunk(0)] + small + [chunk(i) for i in range(1, CHUNKS)]:
        copy.start()
    small[0].wait()
    gain = gain_ref[...]
    sent = []
    part = rows // PARTS
    for i in range(CHUNKS):
        chunk(i).wait()
        at = pl.ds(i * block, block)
        values = tokens_ref[at]
        average = jnp.mean(values, axis=-1, keepdims=True)
        centered = values - average
        variance = jnp.mean(centered * centered, axis=-1, keepdims=True)
        normed_ref[at] = (centered * lax.rsqrt(variance + epsilon) * gain).astype(jnp.bfloat16)
        if (i + 1) * PARTS % CHUNKS == 0:
            p = (i + 1) * PARTS // CHUNKS - 1
            sent.append(pltpu.make_async_copy(normed_ref.at[pl.ds(p * part, part)], outs[p], out_sem.at[p]))
            sent[-1].start()
    sent.append(pltpu.make_async_copy(normed_ref, outs[PARTS], out_sem.at[PARTS]))
    sent[-1].start()
    small[1].wait()
    band = lax.axis_index("lat")
    lists = ((jnp.maximum(band - 1, 0), 1), (jnp.minimum(band + 1, bands - 1), 0))
    for which, (owner, side) in enumerate(lists):
        wanted = halo_rows_ref[pl.ds(owner, 1), side, :]
        slots = lax.broadcasted_iota(jnp.int32, (rows, wanted.shape[1]), 0)
        picks = (slots == wanted).astype(jnp.float32).astype(jnp.bfloat16)
        picked = lax.dot_general(
            picks, normed_ref[...], (((0,), (0,)), ((), ())), preferred_element_type=jnp.float32
        )
        edge_ref[which] = picked.astype(jnp.bfloat16)
        place = PARTS + 1 + which
        sent.append(pltpu.make_async_copy(edge_ref.at[which], outs[place], out_sem.at[place]))
        sent[-1].start()
    for copy in sent:
        copy.wait()


def norm_call(tokens, gain, halo_rows):
    rows, width = tokens.shape
    bands, _, halo = halo_rows.shape
    part = jax.ShapeDtypeStruct((rows // PARTS, width), jnp.bfloat16)
    whole = jax.ShapeDtypeStruct((rows, width), jnp.bfloat16)
    edge = jax.ShapeDtypeStruct((halo, width), jnp.bfloat16)
    return pl.pallas_call(
        functools.partial(norm_kernel, bands),
        out_shape=[part] * PARTS + [whole] + [edge] * 2,
        in_specs=[pl.BlockSpec(memory_space=pl.ANY)] * 3,
        out_specs=[pl.BlockSpec(memory_space=pltpu.HBM)] * (PARTS + 3),
        scratch_shapes=[
            pltpu.VMEM((rows, width), jnp.float32),
            pltpu.VMEM((1, width), jnp.float32),
            pltpu.VMEM(halo_rows.shape, jnp.int32),
            pltpu.VMEM((rows, width), jnp.bfloat16),
            pltpu.VMEM((2, halo, width), jnp.bfloat16),
            pltpu.SemaphoreType.DMA((CHUNKS + 2,)),
            pltpu.SemaphoreType.DMA((PARTS + 3,)),
        ],
        compiler_params=pltpu.CompilerParams(vmem_limit_bytes=VMEM_LIMIT),
        cost_estimate=pl.CostEstimate(flops=10 * rows * width, bytes_accessed=6 * rows * width, transcendentals=0),
        name="layer_norm",
    )(tokens, gain.reshape(1, width), halo_rows)


def sector_columns(lon, reach):
    core, odd = lon % 2, (lon // 2) % 2
    return {
        "own": reach,
        "partner": reach + 1 - 2 * core,
        "same": reach + 2 - 4 * odd,
        "across": reach + 4 * odd - 2,
        "near": reach + 2 * core - 1,
    }


def block_bias(mask_ref, column, rows, dtype):
    blocks = mask_ref.shape[0]
    values = [jnp.where(mask_ref[b, column] > 0, 0.0, NEG) for b in range(blocks)]
    return jnp.concatenate([jnp.full((rows // blocks, LANES), v, jnp.float32) for v in values], axis=0).astype(dtype)


def safe_group(query, weights, sources, counts_ref, mask_ref, scratch, head_size):
    rows_ref, key_ref, value_ref, top_ref, sum_ref, acc_ref, flag_ref, limit_ref, sem = scratch
    rows = query.shape[0]
    wk, wv = weights
    tile = sources[0][0].shape[0]
    tiles = len(sources)
    blocks = mask_ref.shape[0]
    for t, (ref, column, seen, start) in enumerate(sources):
        size = ref.shape[0]
        copy = pltpu.make_async_copy(ref, rows_ref.at[pl.ds(0, size)], sem)
        copy.start()
        copy.wait()
        key_ref[pl.ds(t * tile, size)] = matmul(rows_ref[pl.ds(0, size)], wk[...]).astype(jnp.bfloat16)
        value_ref[pl.ds(t * tile, size)] = matmul(rows_ref[pl.ds(0, size)], wv[...]).astype(jnp.bfloat16)
        if size < tile:
            rest = pl.ds(t * tile + size, tile - size)
            key_ref[rest] = jnp.zeros((tile - size, key_ref.shape[1]), jnp.bfloat16)
            value_ref[rest] = jnp.zeros((tile - size, key_ref.shape[1]), jnp.bfloat16)
        for b in range(blocks):
            flag_ref[t, b] = mask_ref[b, column] if column is not None else 1
        if column is None:
            limit_ref[t] = jnp.where(seen, size, 0)
        else:
            limit_ref[t] = counts_ref[0] - start
    low = lax.broadcasted_iota(jnp.int32, (rows, LANES), 1) < head_size
    outs = []
    for pair in range(query.shape[1] // LANES):
        lanes = slice(pair * LANES, (pair + 1) * LANES)
        halves = []
        for head in range(2):
            own = jnp.where(low if head == 0 else ~low, query[:, lanes], jnp.zeros((), jnp.bfloat16))
            top_ref[...] = jnp.full_like(top_ref, FLOOR)
            sum_ref[...] = jnp.zeros_like(sum_ref)
            acc_ref[...] = jnp.zeros_like(acc_ref)

            def body(t, carry, own=own, lanes=lanes):
                at = pl.ds(pl.multiple_of(t * tile, tile), tile)
                scores = contract_last(own, key_ref[at, lanes]) * (LOG2E * head_size**-0.5)
                slot = lax.broadcasted_iota(jnp.int32, (1, tile), 1)
                scores = scores + jnp.where(slot < limit_ref[t], 0.0, NEG)
                row_bias = jnp.concatenate(
                    [
                        jnp.full((rows // blocks, 1), jnp.where(flag_ref[t, b] > 0, 0.0, NEG), jnp.float32)
                        for b in range(blocks)
                    ],
                    axis=0,
                )
                scores = scores + row_bias
                old = top_ref[...]
                new = jnp.maximum(old, jnp.max(scores, axis=-1, keepdims=True))
                scale = jnp.exp2(old - new)
                weight = jnp.exp2(scores - new[:, :1])
                sum_ref[...] = sum_ref[...] * scale + jnp.sum(weight, axis=-1, keepdims=True)
                acc_ref[...] = acc_ref[...] * scale + matmul(weight.astype(jnp.bfloat16), value_ref[at, lanes])
                top_ref[...] = new
                return carry

            lax.fori_loop(0, tiles, body, 0)
            halves.append(acc_ref[...] / sum_ref[...])
        outs.append(jnp.where(low, *halves).astype(jnp.bfloat16))
    return jnp.concatenate(outs, axis=1)


def stage_kernel(spec, *refs):
    first, last, sectors, part_counts, halos, head_size, row_block = spec
    refs = list(refs)

    def take(count):
        taken = refs[:count]
        del refs[:count]
        return taken

    counts_ref, mask_ref = take(2)
    sector_refs = [take(n) for n in part_counts]
    halo_refs = take(2) if halos else []
    wq_ref = take(1)[0] if first else None
    wk_ref, wv_ref = take(2)
    if not first:
        query_in, acc_in, sum_in = take(3)
    if last:
        tokens_ref, wo_ref = take(2)
        all_refs = take(1 + 4 * PARTS + 2)
        out_ref, res_ref, att_ref, acc_ref, sum_ref = take(5)
    else:
        if first:
            query_out = take(1)[0]
        acc_out, sum_out = take(2)

    reach = mask_ref.shape[1] // 2
    lon, lat = lax.axis_index("lon"), lax.axis_index("lat")
    bands = lax.axis_size("lat")
    columns = sector_columns(lon, reach)
    count = counts_ref[0]

    wk, wv = wk_ref[...], wv_ref[...]
    if first:
        query = jnp.concatenate([matmul(ref[...], wq_ref[...]).astype(jnp.bfloat16) for ref in sector_refs[0]], axis=0)
        query_out[...] = query
    else:
        query = query_in[...]
    rows, width = query.shape
    scaled = query.astype(jnp.float32) * (LOG2E * head_size**-0.5)
    query_hi = scaled.astype(jnp.bfloat16)
    query_lo = (scaled - query_hi.astype(jnp.float32)).astype(jnp.bfloat16)

    tiles = []
    zero = jnp.zeros((), jnp.bfloat16)
    one = jnp.ones((), jnp.bfloat16)
    for name, parts in zip(sectors, sector_refs):
        row_bias = block_bias(mask_ref, columns[name], rows, jnp.bfloat16)
        for i, ref in enumerate(parts):
            key = matmul(ref[...], wk).astype(jnp.bfloat16)
            value = matmul(ref[...], wv)
            start = i * ref.shape[0]
            live = start + lax.broadcasted_iota(jnp.int32, value.shape, 0) < count
            value = jnp.where(live, value, 0.0).astype(jnp.bfloat16)
            ones = jnp.where(live[:, :LANES], 1.0, 0.0).astype(jnp.bfloat16)
            tiles.append((key, value, ones, row_bias))
    for ref, seen in zip(halo_refs, (lat > 0, lat < bands - 1)):
        key = matmul(ref[...], wk).astype(jnp.bfloat16)
        there = jnp.where(seen, 1.0, 0.0)
        value = (matmul(ref[...], wv) * there).astype(jnp.bfloat16)
        ones = jnp.full((ref.shape[0], LANES), there, jnp.float32).astype(jnp.bfloat16)
        tiles.append((key, value, ones, None))

    low = lax.broadcasted_iota(jnp.int32, (rows, LANES), 1) < head_size
    for pair in range(width // LANES):
        lanes = slice(pair * LANES, (pair + 1) * LANES)
        halves = []
        for head in range(2):
            half = low if head == 0 else ~low
            hi = query_hi[:, lanes]
            lo = jnp.where(half, query_lo[:, lanes], zero)
            lefts, rights, values = [], [], []
            for key, value, ones, row_bias in tiles:
                key_half = (lax.broadcasted_iota(jnp.int32, (key.shape[0], LANES), 1) < head_size) == (head == 0)
                left = jnp.where(half, hi, zero if row_bias is None else row_bias)
                lefts.append(jnp.concatenate([left, lo], axis=1))
                rights.append(jnp.concatenate([jnp.where(key_half, key[:, lanes], one), key[:, lanes]], axis=1))
                values.append(jnp.where(key_half, value[:, lanes], ones))
            values = jnp.concatenate(values, axis=0)
            results = []
            for r in range(0, rows, row_block):
                weights = [
                    jnp.exp2(contract_last(left[r : r + row_block], right)).astype(jnp.bfloat16)
                    for left, right in zip(lefts, rights)
                ]
                results.append(matmul(jnp.concatenate(weights, axis=1), values))
            halves.append(jnp.concatenate(results, axis=0))
        acc, total = jnp.where(low, *halves), jnp.where(low, halves[1], halves[0])
        if not first:
            acc = acc + acc_in[:, lanes]
            total = total + sum_in[:, lanes]
        if last:
            acc_ref[:, lanes] = acc
            sum_ref[:, lanes] = total
        else:
            acc_out[:, lanes] = acc
            sum_out[:, lanes] = total
    if not last:
        return

    total = sum_ref[...]
    fine = (total > SUM_MIN) & (total < SUM_MAX)
    for pair in range(width // LANES):
        lanes = slice(pair * LANES, (pair + 1) * LANES)
        att_ref[:, lanes] = (acc_ref[:, lanes] / pltpu.roll(total[:, lanes], head_size, 1)).astype(jnp.bfloat16)

    @pl.when(jnp.min(fine.astype(jnp.float32)) < 0.5)
    def _():
        sources = []
        part = rows // PARTS
        for i in range(PARTS):
            sources.append((all_refs[0].at[pl.ds(i * part, part)], columns["partner"], None, i * part))
        for s, name in enumerate(("own", "same", "across", "near")):
            for i, ref in enumerate(all_refs[1 + s * PARTS : 1 + (s + 1) * PARTS]):
                sources.append((ref, columns[name], None, i * part))
        for ref, seen in zip(all_refs[1 + 4 * PARTS :], (lat > 0, lat < bands - 1)):
            sources.append((ref, None, seen, 0))
        att_ref[...] = safe_group(query, (wk_ref, wv_ref), sources, counts_ref, mask_ref, refs, head_size)

    step = pl.program_id(0)

    @pl.when(step == 0)
    def _():
        res_ref[...] = jnp.zeros_like(res_ref)

    at = pl.ds(pl.multiple_of(step * width, width), width)
    res_ref[:, at] += tokens_ref[...]
    res_ref[...] += matmul(att_ref[...], wo_ref[...])

    @pl.when(step == pl.num_programs(0) - 1)
    def _():
        slot = lax.broadcasted_iota(jnp.int32, res_ref.shape, 0)
        out_ref[...] = jnp.where(slot < count, res_ref[...], 0.0)


def stage_call(counts, mask, sectors, sector_parts, halos, qkv_weight, query=None, state=None, final=None, row_block=512):
    first, last = query is None, final is not None
    model, width = qkv_weight.shape[0], qkv_weight.shape[1] // 3
    head_size = width // HEADS
    rows = sum(p.shape[0] for p in sector_parts[0])
    steps = width // GROUP
    smem = pl.BlockSpec(memory_space=pltpu.SMEM)

    def fixed(shape):
        return pl.BlockSpec(shape, lambda g: (0, 0), pipeline_mode=pl.Buffered(1))

    def weight(third):
        return pl.BlockSpec((model, GROUP), lambda g: (0, third * steps + g))

    columns = pl.BlockSpec((rows, GROUP), lambda g: (0, g))
    args, specs = [counts, mask], [smem, smem]
    for parts in sector_parts:
        args += parts
        specs += [fixed(p.shape) for p in parts]
    for halo in halos:
        args.append(halo)
        specs.append(fixed(halo.shape))
    for third in range(0 if first else 1, 3):
        args.append(qkv_weight)
        specs.append(weight(third))
    if not first:
        args += [query, *state]
        specs += [columns] * 3
    scratch = []
    wide = jax.ShapeDtypeStruct((rows, width), jnp.float32)
    moved = sum(a.size * a.dtype.itemsize for a in args[2:] if a is not qkv_weight) + 3 * model * width * 2
    if last:
        tokens, out_weight, sources = final
        args += [tokens, out_weight, *sources]
        specs += [columns, pl.BlockSpec((GROUP, out_weight.shape[1]), lambda g: (g, 0))]
        specs += [pl.BlockSpec(memory_space=pl.ANY)] * len(sources)
        out_shape = [wide]
        out_specs = [fixed((rows, width))]
        part = rows // PARTS
        tiles = len(sources) + PARTS - 1
        scratch = [
            pltpu.VMEM((rows, width), jnp.float32),
            pltpu.VMEM((rows, GROUP), jnp.bfloat16),
            pltpu.VMEM((rows, GROUP), jnp.float32),
            pltpu.VMEM((rows, GROUP), jnp.float32),
            pltpu.VMEM((part, model), jnp.bfloat16),
            pltpu.VMEM((part * tiles, GROUP), jnp.bfloat16),
            pltpu.VMEM((part * tiles, GROUP), jnp.bfloat16),
            pltpu.VMEM((rows, LANES), jnp.float32),
            pltpu.VMEM((rows, LANES), jnp.float32),
            pltpu.VMEM((rows, LANES), jnp.float32),
            pltpu.SMEM((tiles, mask.shape[0]), jnp.int32),
            pltpu.SMEM((tiles,), jnp.int32),
            pltpu.SemaphoreType.DMA,
        ]
    else:
        out_shape = [wide] * 2
        out_specs = [columns] * 2
        if first:
            out_shape = [jax.ShapeDtypeStruct((rows, width), jnp.bfloat16)] + out_shape
            out_specs = [columns] + out_specs
    part_counts = [len(parts) for parts in sector_parts]
    keys = sum(p.shape[0] for parts in sector_parts for p in parts) + sum(h.shape[0] for h in halos)
    flops = 2 * keys * model * 2 * width + 16 * rows * keys * width
    flops += 2 * rows * model * width * (int(first) + int(last))
    outs = pl.pallas_call(
        functools.partial(stage_kernel, (first, last, sectors, part_counts, bool(halos), head_size, row_block)),
        out_shape=out_shape,
        grid=(steps,),
        in_specs=specs,
        out_specs=out_specs,
        scratch_shapes=scratch,
        compiler_params=pltpu.CompilerParams(vmem_limit_bytes=VMEM_LIMIT),
        cost_estimate=pl.CostEstimate(flops=flops, bytes_accessed=moved, transcendentals=rows * keys * HEADS),
        name="attend_" + "_".join(sectors),
    )(*args)
    if last:
        return outs[0]
    if first:
        return outs[0], outs[1:]
    return outs


def permuted(values, axis, target):
    size = lax.axis_size(axis)
    pairs = [(i, target(i)) for i in range(size) if 0 <= target(i) < size]
    return [lax.ppermute(v, axis, pairs) for v in values]


def on_device(tokens, norm_gain, qkv_weight, out_weight, band_counts, halo_rows, window_mask):
    mask = window_mask[0, 0]
    ring = lax.axis_size("lon")
    assert mask.shape[1] == 5 and ring % 4 == 0 and ring >= 8
    local = tokens[0, 0]
    outs = norm_call(local, norm_gain, halo_rows)
    own, (whole, north_rows, south_rows) = outs[:PARTS], outs[PARTS:]

    same = permuted(own, "lon", lambda i: i ^ 2)
    partner = permuted([whole], "lon", lambda i: i ^ 1)
    from_south = permuted([north_rows], "lat", lambda b: b - 1)[0]
    from_north = permuted([south_rows], "lat", lambda b: b + 1)[0]

    across = permuted(same[:1], "lon", lambda i: (i + (4 if (i // 2) % 2 == 0 else -4)) % ring)
    across += permuted(own[1:], "lon", lambda i: (i + (-2 if (i // 2) % 2 == 0 else 2)) % ring)
    lon = lax.axis_index("lon")
    gives_same = lon % 2 == (lon // 2) % 2
    near = permuted([jnp.where(gives_same, s, a) for s, a in zip(same, across)], "lon", lambda i: i ^ 1)

    halos = [from_north, from_south]
    query, state = stage_call(band_counts, mask, ["own"], [own], [], qkv_weight)
    state = stage_call(band_counts, mask, ["partner"], [partner], halos, qkv_weight, query, state, row_block=256)
    state = stage_call(band_counts, mask, ["same"], [same], [], qkv_weight, query, state)
    final = (local, out_weight, [*partner, *own, *same, *across, *near, *halos])
    result = stage_call(band_counts, mask, ["across", "near"], [across, near], [], qkv_weight, query, state, final)
    return result[None, None]


def solution(mesh):
    in_specs = (
        P("lat", "lon", None, None),
        P(),
        P(),
        P(),
        P("lat"),
        P(),
        P("lat", "lon", None, None),
    )
    out_specs = P("lat", "lon", None, None)
    return jax.shard_map(
        on_device, mesh=mesh, in_specs=in_specs, out_specs=out_specs, check_vma=False
    )
```

```python
import functools
import math

import jax
import jax.numpy as jnp
from jax import lax
from jax.experimental import pallas as pl
from jax.experimental.pallas import tpu as pltpu
from jax.sharding import PartitionSpec as P

HEADS = 16
LANES = 128
GROUP = 256
PARTS = 2
NEG = -1e30
FLOOR = -1e25
LOG2E = math.log2(math.e)
SUM_MIN, SUM_MAX = 2.0**-60, 2.0**100
VMEM_LIMIT = 60 * 1024 * 1024
CHUNKS = 4

epsilon = 1e-05


def contract_last(a, b):
    return lax.dot_general(a, b, (((1,), (1,)), ((), ())), preferred_element_type=jnp.float32)


def matmul(a, b):
    return jnp.dot(a, b, preferred_element_type=jnp.float32)


def norm_kernel(bands, tokens_hbm, gain_hbm, halo_rows_hbm, *refs):
    outs = refs[: PARTS + 3]
    tokens_ref, gain_ref, halo_rows_ref, normed_ref, edge_ref, in_sem, out_sem = refs[PARTS + 3 :]
    rows = tokens_ref.shape[0]
    block = rows // CHUNKS

    def chunk(i):
        at = pl.ds(i * block, block)
        return pltpu.make_async_copy(tokens_hbm.at[at], tokens_ref.at[at], in_sem.at[i])

    small = [
        pltpu.make_async_copy(gain_hbm, gain_ref, in_sem.at[CHUNKS]),
        pltpu.make_async_copy(halo_rows_hbm, halo_rows_ref, in_sem.at[CHUNKS + 1]),
    ]
    for copy in [chunk(0)] + small + [chunk(i) for i in range(1, CHUNKS)]:
        copy.start()
    small[0].wait()
    gain = gain_ref[...]
    sent = []
    part = rows // PARTS
    for i in range(CHUNKS):
        chunk(i).wait()
        at = pl.ds(i * block, block)
        values = tokens_ref[at]
        average = jnp.mean(values, axis=-1, keepdims=True)
        centered = values - average
        variance = jnp.mean(centered * centered, axis=-1, keepdims=True)
        normed_ref[at] = (centered * lax.rsqrt(variance + epsilon) * gain).astype(jnp.bfloat16)
        if (i + 1) * PARTS % CHUNKS == 0:
            p = (i + 1) * PARTS // CHUNKS - 1
            sent.append(pltpu.make_async_copy(normed_ref.at[pl.ds(p * part, part)], outs[p], out_sem.at[p]))
            sent[-1].start()
    sent.append(pltpu.make_async_copy(normed_ref, outs[PARTS], out_sem.at[PARTS]))
    sent[-1].start()
    small[1].wait()
    band = lax.axis_index("lat")
    lists = ((jnp.maximum(band - 1, 0), 1), (jnp.minimum(band + 1, bands - 1), 0))
    for which, (owner, side) in enumerate(lists):
        wanted = halo_rows_ref[pl.ds(owner, 1), side, :]
        slots = lax.broadcasted_iota(jnp.int32, (rows, wanted.shape[1]), 0)
        picks = (slots == wanted).astype(jnp.float32).astype(jnp.bfloat16)
        picked = lax.dot_general(
            picks, normed_ref[...], (((0,), (0,)), ((), ())), preferred_element_type=jnp.float32
        )
        edge_ref[which] = picked.astype(jnp.bfloat16)
        place = PARTS + 1 + which
        sent.append(pltpu.make_async_copy(edge_ref.at[which], outs[place], out_sem.at[place]))
        sent[-1].start()
    for copy in sent:
        copy.wait()


def norm_call(tokens, gain, halo_rows):
    rows, width = tokens.shape
    bands, _, halo = halo_rows.shape
    part = jax.ShapeDtypeStruct((rows // PARTS, width), jnp.bfloat16)
    whole = jax.ShapeDtypeStruct((rows, width), jnp.bfloat16)
    edge = jax.ShapeDtypeStruct((halo, width), jnp.bfloat16)
    return pl.pallas_call(
        functools.partial(norm_kernel, bands),
        out_shape=[part] * PARTS + [whole] + [edge] * 2,
        in_specs=[pl.BlockSpec(memory_space=pl.ANY)] * 3,
        out_specs=[pl.BlockSpec(memory_space=pltpu.HBM)] * (PARTS + 3),
        scratch_shapes=[
            pltpu.VMEM((rows, width), jnp.float32),
            pltpu.VMEM((1, width), jnp.float32),
            pltpu.VMEM(halo_rows.shape, jnp.int32),
            pltpu.VMEM((rows, width), jnp.bfloat16),
            pltpu.VMEM((2, halo, width), jnp.bfloat16),
            pltpu.SemaphoreType.DMA((CHUNKS + 2,)),
            pltpu.SemaphoreType.DMA((PARTS + 3,)),
        ],
        compiler_params=pltpu.CompilerParams(vmem_limit_bytes=VMEM_LIMIT),
        cost_estimate=pl.CostEstimate(flops=10 * rows * width, bytes_accessed=6 * rows * width, transcendentals=0),
        name="layer_norm",
    )(tokens, gain.reshape(1, width), halo_rows)


def sector_columns(lon, reach):
    core, odd = lon % 2, (lon // 2) % 2
    return {
        "own": reach,
        "partner": reach + 1 - 2 * core,
        "same": reach + 2 - 4 * odd,
        "across": reach + 4 * odd - 2,
        "near": reach + 2 * core - 1,
    }


def block_bias(mask_ref, column, rows, dtype):
    blocks = mask_ref.shape[0]
    values = [jnp.where(mask_ref[b, column] > 0, 0.0, NEG) for b in range(blocks)]
    return jnp.concatenate([jnp.full((rows // blocks, LANES), v, jnp.float32) for v in values], axis=0).astype(dtype)


def safe_group(query, weights, sources, counts_ref, mask_ref, scratch, head_size):
    rows_ref, key_ref, value_ref, top_ref, sum_ref, acc_ref, flag_ref, limit_ref, sem = scratch
    rows = query.shape[0]
    wk, wv = weights
    tile = sources[0][0].shape[0]
    tiles = len(sources)
    blocks = mask_ref.shape[0]
    for t, (ref, column, seen, start) in enumerate(sources):
        size = ref.shape[0]
        copy = pltpu.make_async_copy(ref, rows_ref.at[pl.ds(0, size)], sem)
        copy.start()
        copy.wait()
        key_ref[pl.ds(t * tile, size)] = matmul(rows_ref[pl.ds(0, size)], wk[...]).astype(jnp.bfloat16)
        value_ref[pl.ds(t * tile, size)] = matmul(rows_ref[pl.ds(0, size)], wv[...]).astype(jnp.bfloat16)
        if size < tile:
            rest = pl.ds(t * tile + size, tile - size)
            key_ref[rest] = jnp.zeros((tile - size, key_ref.shape[1]), jnp.bfloat16)
            value_ref[rest] = jnp.zeros((tile - size, key_ref.shape[1]), jnp.bfloat16)
        for b in range(blocks):
            flag_ref[t, b] = mask_ref[b, column] if column is not None else 1
        if column is None:
            limit_ref[t] = jnp.where(seen, size, 0)
        else:
            limit_ref[t] = counts_ref[0] - start
    low = lax.broadcasted_iota(jnp.int32, (rows, LANES), 1) < head_size
    outs = []
    for pair in range(query.shape[1] // LANES):
        lanes = slice(pair * LANES, (pair + 1) * LANES)
        halves = []
        for head in range(2):
            own = jnp.where(low if head == 0 else ~low, query[:, lanes], jnp.zeros((), jnp.bfloat16))
            top_ref[...] = jnp.full_like(top_ref, FLOOR)
            sum_ref[...] = jnp.zeros_like(sum_ref)
            acc_ref[...] = jnp.zeros_like(acc_ref)

            def body(t, carry, own=own, lanes=lanes):
                at = pl.ds(pl.multiple_of(t * tile, tile), tile)
                scores = contract_last(own, key_ref[at, lanes]) * (LOG2E * head_size**-0.5)
                slot = lax.broadcasted_iota(jnp.int32, (1, tile), 1)
                scores = scores + jnp.where(slot < limit_ref[t], 0.0, NEG)
                row_bias = jnp.concatenate(
                    [
                        jnp.full((rows // blocks, 1), jnp.where(flag_ref[t, b] > 0, 0.0, NEG), jnp.float32)
                        for b in range(blocks)
                    ],
                    axis=0,
                )
                scores = scores + row_bias
                old = top_ref[...]
                new = jnp.maximum(old, jnp.max(scores, axis=-1, keepdims=True))
                scale = jnp.exp2(old - new)
                weight = jnp.exp2(scores - new[:, :1])
                sum_ref[...] = sum_ref[...] * scale + jnp.sum(weight, axis=-1, keepdims=True)
                acc_ref[...] = acc_ref[...] * scale + matmul(weight.astype(jnp.bfloat16), value_ref[at, lanes])
                top_ref[...] = new
                return carry

            lax.fori_loop(0, tiles, body, 0)
            halves.append(acc_ref[...] / sum_ref[...])
        outs.append(jnp.where(low, *halves).astype(jnp.bfloat16))
    return jnp.concatenate(outs, axis=1)


def stage_kernel(spec, *refs):
    first, last, sectors, part_starts, halos, head_size = spec
    refs = list(refs)

    def take(count):
        taken = refs[:count]
        del refs[:count]
        return taken

    counts_ref, mask_ref = take(2)
    sector_refs = [take(len(starts)) for starts in part_starts]
    halo_refs = take(2) if halos else []
    wq_ref = take(1)[0] if first else None
    wk_ref, wv_ref = take(2)
    if not first:
        query_in, acc_in, sum_in = take(3)
    if last:
        tokens_ref, wo_ref = take(2)
        all_refs = take(1 + 4 * PARTS + 2)
        (out_ref,) = take(1)
    else:
        if first:
            query_out = take(1)[0]
        acc_out, sum_out = take(2)
    key_ref, value_ref, ones_ref, score_ref, weight_ref = take(5)
    if last:
        res_ref, att_ref, acc_out, sum_out = take(4)

    reach = mask_ref.shape[1] // 2
    lon, lat = lax.axis_index("lon"), lax.axis_index("lat")
    bands = lax.axis_size("lat")
    columns = sector_columns(lon, reach)
    count = counts_ref[0]

    wk, wv = wk_ref[...], wv_ref[...]
    if first:
        query = jnp.concatenate([matmul(ref[...], wq_ref[...]).astype(jnp.bfloat16) for ref in sector_refs[0]], axis=0)
        query_out[...] = query
    else:
        query = query_in[...]
    rows, width = query.shape
    scaled = query.astype(jnp.float32) * (LOG2E * head_size**-0.5)
    query_hi = scaled.astype(jnp.bfloat16)
    query_lo = (scaled - query_hi.astype(jnp.float32)).astype(jnp.bfloat16)

    zero = jnp.zeros((), jnp.bfloat16)
    one = jnp.ones((), jnp.bfloat16)
    biases, spans = [], []
    at = 0
    for name, parts, starts in zip(sectors, sector_refs, part_starts):
        begin = at
        for ref, start in zip(parts, starts):
            size = ref.shape[0]
            here = pl.ds(at, size)
            key_ref[:, here] = matmul(ref[...], wk).astype(jnp.bfloat16).T
            value = matmul(ref[...], wv)
            if start + size <= rows // 2:
                value_ref[here] = value.astype(jnp.bfloat16)
                ones_ref[here] = jnp.ones((size, LANES), jnp.bfloat16)
            else:
                live = start + lax.broadcasted_iota(jnp.int32, value.shape, 0) < count
                value_ref[here] = jnp.where(live, value, 0.0).astype(jnp.bfloat16)
                ones_ref[here] = jnp.where(live[:, :LANES], 1.0, 0.0).astype(jnp.bfloat16)
            at += size
        spans.append((begin, at))
        biases.append(block_bias(mask_ref, columns[name], rows, jnp.bfloat16))
    if halo_refs:
        begin = at
        for ref, seen in zip(halo_refs, (lat > 0, lat < bands - 1)):
            size = ref.shape[0]
            here = pl.ds(at, size)
            there = jnp.where(seen, 1.0, 0.0)
            key_ref[:, here] = matmul(ref[...], wk).astype(jnp.bfloat16).T
            value_ref[here] = (matmul(ref[...], wv) * there).astype(jnp.bfloat16)
            ones_ref[here] = jnp.full((size, LANES), there, jnp.float32).astype(jnp.bfloat16)
            at += size
        spans.append((begin, at))
        biases.append(None)

    low = lax.broadcasted_iota(jnp.int32, (rows, LANES), 1) < head_size
    low_key = lax.broadcasted_iota(jnp.int32, (LANES, at), 0) < head_size
    low_value = lax.broadcasted_iota(jnp.int32, (at, LANES), 1) < head_size

    def lanes_of(unit):
        return slice(unit // 2 * LANES, (unit // 2 + 1) * LANES)

    def score(unit):
        lanes, odd = lanes_of(unit), unit % 2
        half = ~low if odd else low
        lo = jnp.where(half, query_lo[:, lanes], zero)
        key = key_ref[lanes, :]
        right = jnp.concatenate([jnp.where(~low_key if odd else low_key, key, one), key], axis=0)
        for (begin, end), bias in zip(spans, biases):
            left = jnp.where(half, query_hi[:, lanes], zero if bias is None else bias)
            score_ref[odd, :, begin:end] = matmul(jnp.concatenate([left, lo], axis=1), right[:, begin:end])

    def weigh(unit):
        weight_ref[unit % 2] = jnp.exp2(score_ref[unit % 2]).astype(jnp.bfloat16)

    halves = {}

    def gather(unit):
        lanes, odd = lanes_of(unit), unit % 2
        values = jnp.where(~low_value if odd else low_value, value_ref[:, lanes], ones_ref[...])
        halves[odd] = matmul(weight_ref[odd], values)
        if not odd:
            return
        acc, total = jnp.where(low, halves[0], halves[1]), jnp.where(low, halves[1], halves[0])
        if not first:
            acc = acc + acc_in[:, lanes]
            total = total + sum_in[:, lanes]
        acc_out[:, lanes] = acc
        sum_out[:, lanes] = total

    units = width // head_size
    for u in range(units + 2):
        if u < units:
            score(u)
        if 0 <= u - 1 < units:
            weigh(u - 1)
        if 0 <= u - 2 < units:
            gather(u - 2)
    if not last:
        return

    total = sum_out[...]
    fine = (total > SUM_MIN) & (total < SUM_MAX)
    for pair in range(width // LANES):
        lanes = slice(pair * LANES, (pair + 1) * LANES)
        att_ref[:, lanes] = (acc_out[:, lanes] / pltpu.roll(total[:, lanes], head_size, 1)).astype(jnp.bfloat16)

    @pl.when(jnp.min(fine.astype(jnp.float32)) < 0.5)
    def _():
        sources = []
        part = rows // PARTS
        for i in range(PARTS):
            sources.append((all_refs[0].at[pl.ds(i * part, part)], columns["partner"], None, i * part))
        for s, name in enumerate(("own", "same", "across", "near")):
            for i, ref in enumerate(all_refs[1 + s * PARTS : 1 + (s + 1) * PARTS]):
                sources.append((ref, columns[name], None, i * part))
        for ref, seen in zip(all_refs[1 + 4 * PARTS :], (lat > 0, lat < bands - 1)):
            sources.append((ref, None, seen, 0))
        att_ref[...] = safe_group(query, (wk_ref, wv_ref), sources, counts_ref, mask_ref, refs, head_size)

    step = pl.program_id(0)

    @pl.when(step == 0)
    def _():
        res_ref[...] = jnp.zeros_like(res_ref)

    at = pl.ds(pl.multiple_of(step * width, width), width)
    res_ref[:, at] += tokens_ref[...]
    res_ref[...] += matmul(att_ref[...], wo_ref[...])

    @pl.when(step == pl.num_programs(0) - 1)
    def _():
        slot = lax.broadcasted_iota(jnp.int32, res_ref.shape, 0)
        out_ref[...] = jnp.where(slot < count, res_ref[...], 0.0)


def stage_call(block_rows, counts, mask, sectors, sector_parts, halos, qkv_weight, query=None, state=None, final=None, starts=None):
    first, last = query is None, final is not None
    model, width = qkv_weight.shape[0], qkv_weight.shape[1] // 3
    head_size = width // HEADS
    rows = mask.shape[0] * block_rows
    steps = width // GROUP
    smem = pl.BlockSpec(memory_space=pltpu.SMEM)

    def fixed(shape):
        return pl.BlockSpec(shape, lambda g: (0, 0), pipeline_mode=pl.Buffered(1))

    def weight(third):
        return pl.BlockSpec((model, GROUP), lambda g: (0, third * steps + g))

    columns = pl.BlockSpec((rows, GROUP), lambda g: (0, g))
    args, specs = [counts, mask], [smem, smem]
    for parts in sector_parts:
        args += parts
        specs += [fixed(p.shape) for p in parts]
    for halo in halos:
        args.append(halo)
        specs.append(fixed(halo.shape))
    for third in range(0 if first else 1, 3):
        args.append(qkv_weight)
        specs.append(weight(third))
    if not first:
        args += [query, *state]
        specs += [columns] * 3
    keys = sum(p.shape[0] for parts in sector_parts for p in parts) + sum(h.shape[0] for h in halos)
    scratch = [
        pltpu.VMEM((GROUP, keys), jnp.bfloat16),
        pltpu.VMEM((keys, GROUP), jnp.bfloat16),
        pltpu.VMEM((keys, LANES), jnp.bfloat16),
        pltpu.VMEM((2, rows, keys), jnp.float32),
        pltpu.VMEM((2, rows, keys), jnp.bfloat16),
    ]
    wide = jax.ShapeDtypeStruct((rows, width), jnp.float32)
    moved = sum(a.size * a.dtype.itemsize for a in args[2:] if a is not qkv_weight) + 3 * model * width * 2
    if last:
        tokens, out_weight, sources = final
        args += [tokens, out_weight, *sources]
        specs += [columns, pl.BlockSpec((GROUP, out_weight.shape[1]), lambda g: (g, 0))]
        specs += [pl.BlockSpec(memory_space=pl.ANY)] * len(sources)
        out_shape = [wide]
        out_specs = [fixed((rows, width))]
        part = rows // PARTS
        tiles = len(sources) + PARTS - 1
        scratch += [
            pltpu.VMEM((rows, width), jnp.float32),
            pltpu.VMEM((rows, GROUP), jnp.bfloat16),
            pltpu.VMEM((rows, GROUP), jnp.float32),
            pltpu.VMEM((rows, GROUP), jnp.float32),
            pltpu.VMEM((part, model), jnp.bfloat16),
            pltpu.VMEM((part * tiles, GROUP), jnp.bfloat16),
            pltpu.VMEM((part * tiles, GROUP), jnp.bfloat16),
            pltpu.VMEM((rows, LANES), jnp.float32),
            pltpu.VMEM((rows, LANES), jnp.float32),
            pltpu.VMEM((rows, LANES), jnp.float32),
            pltpu.SMEM((tiles, mask.shape[0]), jnp.int32),
            pltpu.SMEM((tiles,), jnp.int32),
            pltpu.SemaphoreType.DMA,
        ]
    else:
        out_shape = [wide] * 2
        out_specs = [columns] * 2
        if first:
            out_shape = [jax.ShapeDtypeStruct((rows, width), jnp.bfloat16)] + out_shape
            out_specs = [columns] + out_specs
    flops = 2 * keys * model * 2 * width + 16 * rows * keys * width
    flops += 2 * rows * model * width * (int(first) + int(last))
    outs = pl.pallas_call(
        functools.partial(stage_kernel, (first, last, sectors, starts, bool(halos), head_size)),
        out_shape=out_shape,
        grid=(steps,),
        in_specs=specs,
        out_specs=out_specs,
        scratch_shapes=scratch,
        compiler_params=pltpu.CompilerParams(vmem_limit_bytes=VMEM_LIMIT),
        cost_estimate=pl.CostEstimate(flops=flops, bytes_accessed=moved, transcendentals=rows * keys * HEADS),
        name="attend_" + "_".join(sectors),
    )(*args)
    if last:
        return outs[0]
    if first:
        return outs[0], outs[1:]
    return outs


def permuted(values, axis, target):
    size = lax.axis_size(axis)
    pairs = [(i, target(i)) for i in range(size) if 0 <= target(i) < size]
    return [lax.ppermute(v, axis, pairs) for v in values]


def on_device(tokens, norm_gain, qkv_weight, out_weight, band_counts, halo_rows, window_mask):
    mask = window_mask[0, 0]
    ring = lax.axis_size("lon")
    assert mask.shape[1] == 5 and ring % 4 == 0 and ring >= 8
    local = tokens[0, 0]
    rows = local.shape[0]
    outs = norm_call(local, norm_gain, halo_rows)
    own, (whole, north_rows, south_rows) = outs[:PARTS], outs[PARTS:]

    same = permuted(own, "lon", lambda i: i ^ 2)
    across = permuted(own[1:], "lon", lambda i: (i + (-2 if (i // 2) % 2 == 0 else 2)) % ring)
    partner = permuted([whole], "lon", lambda i: i ^ 1)
    halos = [
        permuted([south_rows], "lat", lambda b: b + 1)[0],
        permuted([north_rows], "lat", lambda b: b - 1)[0],
    ]
    lon = lax.axis_index("lon")
    gives_same = lon % 2 == (lon // 2) % 2

    def swapped(mine, others):
        return permuted([jnp.where(gives_same, mine, others)], "lon", lambda i: i ^ 1)[0]

    stage = functools.partial(stage_call, rows // mask.shape[0], band_counts, mask)
    half = rows // PARTS
    query, state = stage(["own"], [own], [], qkv_weight, starts=[[0, half]])

    same[0], query, state = lax.optimization_barrier((same[0], query, state))
    across = permuted(same[:1], "lon", lambda i: (i + (4 if (i // 2) % 2 == 0 else -4)) % ring) + across
    state = stage(["partner"], [partner], halos, qkv_weight, query, state, starts=[[0]])

    across[0], state = lax.optimization_barrier((across[0], state))
    near = [swapped(same[0], across[0])]
    state = stage(["same", "across"], [same[:1], across[:1]], [], qkv_weight, query, state, starts=[[0], [0]])

    across[1], state = lax.optimization_barrier((across[1], state))
    near.append(swapped(same[1], across[1]))
    final = (local, out_weight, [*partner, *own, *same, *across, *near, *halos])
    result = stage(
        ["same", "across", "near"],
        [same[1:], across[1:], near],
        [],
        qkv_weight,
        query,
        state,
        final,
        starts=[[half], [half], [0, half]],
    )
    return result[None, None]


def solution(mesh):
    in_specs = (
        P("lat", "lon", None, None),
        P(),
        P(),
        P(),
        P("lat"),
        P(),
        P("lat", "lon", None, None),
    )
    out_specs = P("lat", "lon", None, None)
    return jax.shard_map(
        on_device, mesh=mesh, in_specs=in_specs, out_specs=out_specs, check_vma=False
    )
```

```python
import functools
import math

import jax
import jax.numpy as jnp
from jax import lax
from jax.experimental import pallas as pl
from jax.experimental.pallas import tpu as pltpu
from jax.sharding import PartitionSpec as P

HEADS = 16
LANES = 128
GROUP = 256
PARTS = 2
NEG = -1e30
FLOOR = -1e25
LOG2E = math.log2(math.e)
SUM_MIN, SUM_MAX = 2.0**-60, 2.0**100
VMEM_LIMIT = 60 * 1024 * 1024
CHUNKS = 4

epsilon = 1e-05


def contract_last(a, b):
    return lax.dot_general(a, b, (((1,), (1,)), ((), ())), preferred_element_type=jnp.float32)


def matmul(a, b):
    return jnp.dot(a, b, preferred_element_type=jnp.float32)


def norm_kernel(bands, tokens_hbm, gain_hbm, halo_rows_hbm, *refs):
    outs = refs[: PARTS + 3]
    tokens_ref, gain_ref, halo_rows_ref, normed_ref, edge_ref, in_sem, out_sem = refs[PARTS + 3 :]
    rows = tokens_ref.shape[0]
    block = rows // CHUNKS

    def chunk(i):
        at = pl.ds(i * block, block)
        return pltpu.make_async_copy(tokens_hbm.at[at], tokens_ref.at[at], in_sem.at[i])

    small = [
        pltpu.make_async_copy(gain_hbm, gain_ref, in_sem.at[CHUNKS]),
        pltpu.make_async_copy(halo_rows_hbm, halo_rows_ref, in_sem.at[CHUNKS + 1]),
    ]
    for copy in [chunk(0)] + small + [chunk(i) for i in range(1, CHUNKS)]:
        copy.start()
    small[0].wait()
    gain = gain_ref[...]
    sent = []
    part = rows // PARTS
    for i in range(CHUNKS):
        chunk(i).wait()
        at = pl.ds(i * block, block)
        values = tokens_ref[at]
        average = jnp.mean(values, axis=-1, keepdims=True)
        centered = values - average
        variance = jnp.mean(centered * centered, axis=-1, keepdims=True)
        normed_ref[at] = (centered * lax.rsqrt(variance + epsilon) * gain).astype(jnp.bfloat16)
        if (i + 1) * PARTS % CHUNKS == 0:
            p = (i + 1) * PARTS // CHUNKS - 1
            sent.append(pltpu.make_async_copy(normed_ref.at[pl.ds(p * part, part)], outs[p], out_sem.at[p]))
            sent[-1].start()
    sent.append(pltpu.make_async_copy(normed_ref, outs[PARTS], out_sem.at[PARTS]))
    sent[-1].start()
    small[1].wait()
    band = lax.axis_index("lat")
    lists = ((jnp.maximum(band - 1, 0), 1), (jnp.minimum(band + 1, bands - 1), 0))
    for which, (owner, side) in enumerate(lists):
        wanted = halo_rows_ref[pl.ds(owner, 1), side, :]
        slots = lax.broadcasted_iota(jnp.int32, (rows, wanted.shape[1]), 0)
        picks = (slots == wanted).astype(jnp.float32).astype(jnp.bfloat16)
        picked = lax.dot_general(
            picks, normed_ref[...], (((0,), (0,)), ((), ())), preferred_element_type=jnp.float32
        )
        edge_ref[which] = picked.astype(jnp.bfloat16)
        place = PARTS + 1 + which
        sent.append(pltpu.make_async_copy(edge_ref.at[which], outs[place], out_sem.at[place]))
        sent[-1].start()
    for copy in sent:
        copy.wait()


def norm_call(tokens, gain, halo_rows):
    rows, width = tokens.shape
    bands, _, halo = halo_rows.shape
    part = jax.ShapeDtypeStruct((rows // PARTS, width), jnp.bfloat16)
    whole = jax.ShapeDtypeStruct((rows, width), jnp.bfloat16)
    edge = jax.ShapeDtypeStruct((halo, width), jnp.bfloat16)
    return pl.pallas_call(
        functools.partial(norm_kernel, bands),
        out_shape=[part] * PARTS + [whole] + [edge] * 2,
        in_specs=[pl.BlockSpec(memory_space=pl.ANY)] * 3,
        out_specs=[pl.BlockSpec(memory_space=pltpu.HBM)] * (PARTS + 3),
        scratch_shapes=[
            pltpu.VMEM((rows, width), jnp.float32),
            pltpu.VMEM((1, width), jnp.float32),
            pltpu.VMEM(halo_rows.shape, jnp.int32),
            pltpu.VMEM((rows, width), jnp.bfloat16),
            pltpu.VMEM((2, halo, width), jnp.bfloat16),
            pltpu.SemaphoreType.DMA((CHUNKS + 2,)),
            pltpu.SemaphoreType.DMA((PARTS + 3,)),
        ],
        compiler_params=pltpu.CompilerParams(vmem_limit_bytes=VMEM_LIMIT),
        cost_estimate=pl.CostEstimate(flops=10 * rows * width, bytes_accessed=6 * rows * width, transcendentals=0),
        name="layer_norm",
    )(tokens, gain.reshape(1, width), halo_rows)


def sector_columns(lon, reach):
    core, odd = lon % 2, (lon // 2) % 2
    return {
        "own": reach,
        "partner": reach + 1 - 2 * core,
        "same": reach + 2 - 4 * odd,
        "across": reach + 4 * odd - 2,
        "near": reach + 2 * core - 1,
    }


def block_bias(mask_ref, column, rows, dtype):
    blocks = mask_ref.shape[0]
    values = [jnp.where(mask_ref[b, column] > 0, 0.0, NEG) for b in range(blocks)]
    return jnp.concatenate([jnp.full((rows // blocks, LANES), v, jnp.float32) for v in values], axis=0).astype(dtype)


def safe_attention(query_ref, weights, sources, counts_ref, mask_ref, att_ref, scratch, head_size):
    rows_ref, key_ref, value_ref, top_ref, sum_ref, acc_ref, flag_ref, limit_ref, sem = scratch
    pairs, rows, _ = query_ref.shape
    wk_ref, wv_ref = weights
    groups = wk_ref.shape[0]
    tile = sources[0][0].shape[0]
    blocks = mask_ref.shape[0]
    low = lax.broadcasted_iota(jnp.int32, (rows, LANES), 1) < head_size

    def group_body(g, carry):
        for t, (ref, column, seen, start) in enumerate(sources):
            size = ref.shape[0]
            copy = pltpu.make_async_copy(ref, rows_ref.at[pl.ds(0, size)], sem)
            copy.start()
            copy.wait()
            key_ref[pl.ds(t * tile, size)] = matmul(rows_ref[pl.ds(0, size)], wk_ref[g]).astype(jnp.bfloat16)
            value_ref[pl.ds(t * tile, size)] = matmul(rows_ref[pl.ds(0, size)], wv_ref[g]).astype(jnp.bfloat16)
            if size < tile:
                rest = pl.ds(t * tile + size, tile - size)
                key_ref[rest] = jnp.zeros((tile - size, key_ref.shape[1]), jnp.bfloat16)
                value_ref[rest] = jnp.zeros((tile - size, key_ref.shape[1]), jnp.bfloat16)
            for b in range(blocks):
                flag_ref[t, b] = mask_ref[b, column] if column is not None else 1
            if column is None:
                limit_ref[t] = jnp.where(seen, size, 0)
            else:
                limit_ref[t] = counts_ref[0] - start
        for pair in range(pairs // groups):
            lanes = slice(pair * LANES, (pair + 1) * LANES)
            place = g * (pairs // groups) + pair
            halves = []
            for head in range(2):
                own = jnp.where(low if head == 0 else ~low, query_ref[place], jnp.zeros((), jnp.bfloat16))
                top_ref[...] = jnp.full_like(top_ref, FLOOR)
                sum_ref[...] = jnp.zeros_like(sum_ref)
                acc_ref[...] = jnp.zeros_like(acc_ref)

                def body(t, carry, own=own, lanes=lanes):
                    at = pl.ds(pl.multiple_of(t * tile, tile), tile)
                    scores = contract_last(own, key_ref[at, lanes]) * (LOG2E * head_size**-0.5)
                    slot = lax.broadcasted_iota(jnp.int32, (1, tile), 1)
                    scores = scores + jnp.where(slot < limit_ref[t], 0.0, NEG)
                    row_bias = jnp.concatenate(
                        [
                            jnp.full((rows // blocks, 1), jnp.where(flag_ref[t, b] > 0, 0.0, NEG), jnp.float32)
                            for b in range(blocks)
                        ],
                        axis=0,
                    )
                    scores = scores + row_bias
                    old = top_ref[...]
                    new = jnp.maximum(old, jnp.max(scores, axis=-1, keepdims=True))
                    scale = jnp.exp2(old - new)
                    weight = jnp.exp2(scores - new[:, :1])
                    sum_ref[...] = sum_ref[...] * scale + jnp.sum(weight, axis=-1, keepdims=True)
                    acc_ref[...] = acc_ref[...] * scale + matmul(weight.astype(jnp.bfloat16), value_ref[at, lanes])
                    top_ref[...] = new
                    return carry

                lax.fori_loop(0, len(sources), body, 0)
                halves.append(acc_ref[...] / sum_ref[...])
            att_ref[place] = jnp.where(low, *halves).astype(jnp.bfloat16)
        return carry

    lax.fori_loop(0, groups, group_body, 0)


def stage_kernel(spec, *refs):
    first, last, sectors, part_starts, halos, head_size = spec
    refs = list(refs)

    def take(count):
        taken = refs[:count]
        del refs[:count]
        return taken

    counts_ref, mask_ref = take(2)
    sector_refs = [take(len(starts)) for starts in part_starts]
    halo_refs = take(2) if halos else []
    (qkv_hbm,) = take(1)
    if not first:
        query_hbm, sums_hbm = take(2)
    if last:
        tokens_hbm, wo_hbm = take(2)
        all_refs = take(1 + 4 * PARTS + 2)
        (out_hbm,) = take(1)
    else:
        if first:
            (query_out,) = take(1)
        (sums_out,) = take(1)
    rows_ref, weight_ref, key_ref, value_ref, ones_ref, query_ref, sums_ref = take(7)
    score_refs, exp_refs = take(2), take(2)
    rows_sem, weight_sem, in_sem, out_sem = take(4)
    if last:
        att_ref, tokens_ref, wo_ref, fine_ref = take(4)

    pairs, rows, _ = query_ref.shape
    groups, model, group = weight_ref.shape[1:]
    each = pairs // groups
    reach = mask_ref.shape[1] // 2
    lon, lat = lax.axis_index("lon"), lax.axis_index("lat")
    bands = lax.axis_size("lat")
    columns = sector_columns(lon, reach)
    count = counts_ref[0]
    thirds = range(0 if first else 1, 3)

    row_copies = []
    at = 0
    for ref in [r for parts in sector_refs for r in parts] + halo_refs:
        here = rows_ref.at[pl.ds(at, ref.shape[0])]
        row_copies.append(pltpu.make_async_copy(ref, here, rows_sem.at[len(row_copies)]))
        at += ref.shape[0]
    keys = at

    def weight_copy(third, g):
        start = third * groups * group + g * group
        if not isinstance(start, int):
            start = pl.multiple_of(start, group)
        t = third - thirds[0]
        return pltpu.make_async_copy(qkv_hbm.at[:, pl.ds(start, group)], weight_ref.at[t, g], weight_sem.at[t, g])

    later = []
    if not first:
        later.append(pltpu.make_async_copy(query_hbm, query_ref, in_sem.at[0]))
        later.append(pltpu.make_async_copy(sums_hbm, sums_ref, in_sem.at[1]))
    if last:
        later.append(pltpu.make_async_copy(tokens_hbm, tokens_ref, in_sem.at[2]))
        later.append(pltpu.make_async_copy(wo_hbm, wo_ref, in_sem.at[3]))
    for copy in row_copies + [weight_copy(t, g) for g in range(groups) for t in thirds] + later:
        copy.start()

    biases, spans, pieces = [], [], []
    at = 0
    for name, parts, starts in zip(sectors, sector_refs, part_starts):
        begin = at
        for ref, start in zip(parts, starts):
            for r in range(0, ref.shape[0], group):
                size = min(group, ref.shape[0] - r)
                if start + r + size <= rows // 2:
                    live = None
                else:
                    slot = start + r + lax.broadcasted_iota(jnp.int32, (size, group), 0)
                    live = jnp.where(slot < count, 1.0, 0.0)
                pieces.append((at, size, live))
                at += size
        spans.append((begin, at))
        biases.append(None if name == "own" else block_bias(mask_ref, columns[name], rows, jnp.bfloat16))
    if halo_refs:
        begin = at
        for ref, seen in zip(halo_refs, (lat > 0, lat < bands - 1)):
            size = ref.shape[0]
            pieces.append((at, size, jnp.full((size, group), jnp.where(seen, 1.0, 0.0), jnp.float32)))
            at += size
        spans.append((begin, at))
        biases.append(None)
    for begin, size, live in pieces:
        ones = jnp.ones((size, LANES), jnp.float32) if live is None else live[:, :LANES]
        ones_ref[pl.ds(begin, size)] = ones.astype(jnp.bfloat16)
    for copy in row_copies:
        copy.wait()

    def project(g, carry):
        for t in thirds:
            weight_copy(t, g).wait()
        for begin, size, live in pieces:
            here = pl.ds(begin, size)
            normed = rows_ref[here]
            if first:
                query = matmul(normed, weight_ref[0, g]).astype(jnp.bfloat16)
                for p in range(each):
                    query_ref[g * each + p, here] = query[:, p * LANES : (p + 1) * LANES]
            key = matmul(normed, weight_ref[1 - thirds[0], g]).astype(jnp.bfloat16).T
            value = matmul(normed, weight_ref[2 - thirds[0], g])
            if live is not None:
                value = jnp.where(live > 0, value, 0.0)
            value = value.astype(jnp.bfloat16)
            for p in range(each):
                lanes = slice(p * LANES, (p + 1) * LANES)
                key_ref[g * each + p, :, here] = key[lanes]
                value_ref[g * each + p, here] = value[:, lanes]
        return carry

    lax.fori_loop(0, groups, project, 0)
    if first:
        sent = pltpu.make_async_copy(query_ref, query_out, in_sem.at[0])
        sent.start()
    else:
        for copy in later[:2]:
            copy.wait()

    zero = jnp.zeros((), jnp.bfloat16)
    one = jnp.ones((), jnp.bfloat16)
    low = lax.broadcasted_iota(jnp.int32, (rows, LANES), 1) < head_size
    low_key = lax.broadcasted_iota(jnp.int32, (LANES, keys), 0) < head_size
    low_value = lax.broadcasted_iota(jnp.int32, (keys, LANES), 1) < head_size

    def score(pair, odd):
        half = ~low if odd else low
        query = query_ref[pair]
        right = jnp.where(~low_key if odd else low_key, key_ref[pair], one)
        for (begin, end), bias in zip(spans, biases):
            left = jnp.where(half, query, zero if bias is None else bias)
            score_refs[odd][:, begin:end] = matmul(left, right[:, begin:end])

    def weigh(odd):
        exp_refs[odd][...] = jnp.exp2(score_refs[odd][...] * (LOG2E * head_size**-0.5)).astype(jnp.bfloat16)

    def gather(pair, odd):
        values = jnp.where(~low_value if odd else low_value, value_ref[pair], ones_ref[...])
        result = matmul(exp_refs[odd][...], values)
        if not first:
            result = result + sums_ref[2 * pair + odd]
        sums_ref[2 * pair + odd] = result

    def finish(pair):
        if not last:
            at = pl.ds(2 * pair, 2)
            pltpu.make_async_copy(sums_ref.at[at], sums_out.at[at], out_sem.at[pair]).start()
            return
        even, odd = sums_ref[2 * pair], sums_ref[2 * pair + 1]
        total = jnp.where(low, odd, even)
        fine = jnp.where((total > SUM_MIN) & (total < SUM_MAX), 1.0, 0.0)
        fine_ref[...] = jnp.minimum(fine_ref[...], fine)
        att_ref[pair] = (jnp.where(low, even, odd) / pltpu.roll(total, head_size, 1)).astype(jnp.bfloat16)

    if last:
        fine_ref[...] = jnp.ones_like(fine_ref)
    score(0, 0)
    score(0, 1)
    weigh(0)

    def attend(pair, carry):
        score(pair, 0)
        weigh(1)
        gather(pair - 1, 0)
        score(pair, 1)
        weigh(0)
        gather(pair - 1, 1)
        finish(pair - 1)
        return carry

    lax.fori_loop(1, pairs, attend, 0)
    weigh(1)
    gather(pairs - 1, 0)
    gather(pairs - 1, 1)
    finish(pairs - 1)

    if not last:
        if first:
            sent.wait()

        def arrived(pair, carry):
            at = pl.ds(2 * pair, 2)
            pltpu.make_async_copy(sums_ref.at[at], sums_out.at[at], out_sem.at[pair]).wait()
            return carry

        lax.fori_loop(0, pairs, arrived, 0)
        return

    @pl.when(jnp.min(fine_ref[...]) < 0.5)
    def _():
        sources = []
        part = rows // PARTS
        for i in range(PARTS):
            sources.append((all_refs[0].at[pl.ds(i * part, part)], columns["partner"], None, i * part))
        for s, name in enumerate(("own", "same", "across", "near")):
            for i, ref in enumerate(all_refs[1 + s * PARTS : 1 + (s + 1) * PARTS]):
                sources.append((ref, columns[name], None, i * part))
        for ref, seen in zip(all_refs[1 + 4 * PARTS :], (lat > 0, lat < bands - 1)):
            sources.append((ref, None, seen, 0))
        weights = (weight_ref.at[0], weight_ref.at[1])
        safe_attention(query_ref, weights, sources, counts_ref, mask_ref, att_ref, refs, head_size)

    for copy in later[2:]:
        copy.wait()
    attended = jnp.concatenate([att_ref[p] for p in range(pairs)], axis=1)
    live = lax.broadcasted_iota(jnp.int32, (rows, group), 0) < count
    sent = []
    for n in range(out_hbm.shape[1] // group):
        lanes = pl.ds(n * group, group)
        result = tokens_ref[:, lanes] + matmul(attended, wo_ref[:, lanes])
        tokens_ref[:, lanes] = jnp.where(live, result, 0.0)
        sent.append(pltpu.make_async_copy(tokens_ref.at[:, lanes], out_hbm.at[:, lanes], out_sem.at[n]))
        sent[-1].start()
    for copy in sent:
        copy.wait()


def stage_call(block_rows, counts, mask, sectors, sector_parts, halos, qkv_weight, query=None, sums=None, final=None, starts=None):
    first, last = query is None, final is not None
    model, width = qkv_weight.shape[0], qkv_weight.shape[1] // 3
    head_size = width // HEADS
    rows = mask.shape[0] * block_rows
    pairs, groups = width // LANES, width // GROUP
    thirds = 3 if first else 2
    smem = pl.BlockSpec(memory_space=pltpu.SMEM)
    hbm = pl.BlockSpec(memory_space=pl.ANY)
    sources = [p for parts in sector_parts for p in parts] + halos
    keys = sum(p.shape[0] for p in sources)
    args = [counts, mask, *sources, qkv_weight]
    if not first:
        args += [query, sums]
    query_shape = jax.ShapeDtypeStruct((pairs, rows, LANES), jnp.bfloat16)
    sums_shape = jax.ShapeDtypeStruct((2 * pairs, rows, LANES), jnp.float32)
    scratch = [
        pltpu.VMEM((keys, model), jnp.bfloat16),
        pltpu.VMEM((thirds, groups, model, GROUP), jnp.bfloat16),
        pltpu.VMEM((pairs, LANES, keys), jnp.bfloat16),
        pltpu.VMEM((pairs, keys, LANES), jnp.bfloat16),
        pltpu.VMEM((keys, LANES), jnp.bfloat16),
        pltpu.VMEM(query_shape.shape, jnp.bfloat16),
        pltpu.VMEM(sums_shape.shape, jnp.float32),
        pltpu.VMEM((rows, keys), jnp.float32),
        pltpu.VMEM((rows, keys), jnp.float32),
        pltpu.VMEM((rows, keys), jnp.bfloat16),
        pltpu.VMEM((rows, keys), jnp.bfloat16),
        pltpu.SemaphoreType.DMA((len(sources),)),
        pltpu.SemaphoreType.DMA((thirds, groups)),
        pltpu.SemaphoreType.DMA((4,)),
        pltpu.SemaphoreType.DMA((pairs,)),
    ]
    if last:
        tokens, out_weight, everything = final
        args += [tokens, out_weight, *everything]
        out_shape = [jax.ShapeDtypeStruct((rows, width), jnp.float32)]
        part = rows // PARTS
        tiles = len(everything) + PARTS - 1
        scratch += [
            pltpu.VMEM((pairs, rows, LANES), jnp.bfloat16),
            pltpu.VMEM(tokens.shape, jnp.float32),
            pltpu.VMEM(out_weight.shape, jnp.bfloat16),
            pltpu.VMEM((rows, LANES), jnp.float32),
            pltpu.VMEM((part, model), jnp.bfloat16),
            pltpu.VMEM((part * tiles, GROUP), jnp.bfloat16),
            pltpu.VMEM((part * tiles, GROUP), jnp.bfloat16),
            pltpu.VMEM((rows, LANES), jnp.float32),
            pltpu.VMEM((rows, LANES), jnp.float32),
            pltpu.VMEM((rows, LANES), jnp.float32),
            pltpu.SMEM((tiles, mask.shape[0]), jnp.int32),
            pltpu.SMEM((tiles,), jnp.int32),
            pltpu.SemaphoreType.DMA,
        ]
    else:
        out_shape = [query_shape, sums_shape] if first else [sums_shape]
    flops = 2 * keys * model * 2 * width + 16 * rows * keys * width
    flops += 2 * rows * model * width * (int(first) + int(last))
    moved = 2 * (thirds * model * width + keys * model) + 4 * rows * width * (2 if first else 5)
    outs = pl.pallas_call(
        functools.partial(stage_kernel, (first, last, sectors, starts, bool(halos), head_size)),
        out_shape=out_shape,
        in_specs=[smem, smem] + [hbm] * (len(args) - 2),
        out_specs=[hbm] * len(out_shape),
        scratch_shapes=scratch,
        compiler_params=pltpu.CompilerParams(vmem_limit_bytes=VMEM_LIMIT),
        cost_estimate=pl.CostEstimate(flops=flops, bytes_accessed=moved, transcendentals=rows * keys * HEADS),
        name="attend_" + "_".join(sectors),
    )(*args)
    return outs if first else outs[0]


def permuted(values, axis, target):
    size = lax.axis_size(axis)
    pairs = [(i, target(i)) for i in range(size) if 0 <= target(i) < size]
    return [lax.ppermute(v, axis, pairs) for v in values]


def on_device(tokens, norm_gain, qkv_weight, out_weight, band_counts, halo_rows, window_mask):
    mask = window_mask[0, 0]
    ring = lax.axis_size("lon")
    assert mask.shape[1] == 5 and ring % 4 == 0 and ring >= 8
    local = tokens[0, 0]
    rows = local.shape[0]
    outs = norm_call(local, norm_gain, halo_rows)
    own, (whole, north_rows, south_rows) = outs[:PARTS], outs[PARTS:]

    same = permuted(own, "lon", lambda i: i ^ 2)
    across = permuted(own[1:], "lon", lambda i: (i + (-2 if (i // 2) % 2 == 0 else 2)) % ring)
    partner = permuted([whole], "lon", lambda i: i ^ 1)
    halos = [
        permuted([south_rows], "lat", lambda b: b + 1)[0],
        permuted([north_rows], "lat", lambda b: b - 1)[0],
    ]
    lon = lax.axis_index("lon")
    gives_same = lon % 2 == (lon // 2) % 2

    def swapped(mine, others):
        return permuted([jnp.where(gives_same, mine, others)], "lon", lambda i: i ^ 1)[0]

    stage = functools.partial(stage_call, rows // mask.shape[0], band_counts, mask)
    half = rows // PARTS
    query, state = stage(["own"], [own], [], qkv_weight, starts=[[0, half]])

    same[0], query, state = lax.optimization_barrier((same[0], query, state))
    across = permuted(same[:1], "lon", lambda i: (i + (4 if (i // 2) % 2 == 0 else -4)) % ring) + across
    state = stage(["partner"], [partner], halos, qkv_weight, query, state, starts=[[0]])

    across[0], state = lax.optimization_barrier((across[0], state))
    near = [swapped(same[0], across[0])]
    state = stage(["same", "across"], [same[:1], across[:1]], [], qkv_weight, query, state, starts=[[0], [0]])

    across[1], state = lax.optimization_barrier((across[1], state))
    near.append(swapped(same[1], across[1]))
    final = (local, out_weight, [*partner, *own, *same, *across, *near, *halos])
    result = stage(
        ["same", "across", "near"],
        [same[1:], across[1:], near],
        [],
        qkv_weight,
        query,
        state,
        final,
        starts=[[half], [half], [0, half]],
    )
    return result[None, None]


def solution(mesh):
    in_specs = (
        P("lat", "lon", None, None),
        P(),
        P(),
        P(),
        P("lat"),
        P(),
        P("lat", "lon", None, None),
    )
    out_specs = P("lat", "lon", None, None)
    return jax.shard_map(
        on_device, mesh=mesh, in_specs=in_specs, out_specs=out_specs, check_vma=False
    )
```

```python
import functools
import math

import jax
import jax.numpy as jnp
from jax import lax
from jax.experimental import pallas as pl
from jax.experimental.pallas import tpu as pltpu
from jax.sharding import PartitionSpec as P

HEADS = 16
LANES = 128
GROUP = 256
PARTS = 2
NEG = -1e30
FLOOR = -1e25
LOG2E = math.log2(math.e)
SUM_MIN, SUM_MAX = 2.0**-60, 2.0**100
VMEM_LIMIT = 60 * 1024 * 1024
CHUNKS = 4

epsilon = 1e-05


def contract_last(a, b):
    return lax.dot_general(a, b, (((1,), (1,)), ((), ())), preferred_element_type=jnp.float32)


def matmul(a, b):
    return jnp.dot(a, b, preferred_element_type=jnp.float32)


def norm_kernel(bands, tokens_hbm, gain_hbm, halo_rows_hbm, *refs):
    outs = refs[: PARTS + 3]
    tokens_ref, gain_ref, halo_rows_ref, normed_ref, edge_ref, in_sem, out_sem = refs[PARTS + 3 :]
    rows = tokens_ref.shape[0]
    block = rows // CHUNKS

    def chunk(i):
        at = pl.ds(i * block, block)
        return pltpu.make_async_copy(tokens_hbm.at[at], tokens_ref.at[at], in_sem.at[i])

    small = [
        pltpu.make_async_copy(gain_hbm, gain_ref, in_sem.at[CHUNKS]),
        pltpu.make_async_copy(halo_rows_hbm, halo_rows_ref, in_sem.at[CHUNKS + 1]),
    ]
    for copy in [chunk(0)] + small + [chunk(i) for i in range(1, CHUNKS)]:
        copy.start()
    small[0].wait()
    gain = gain_ref[...]
    sent = []
    part = rows // PARTS
    for i in range(CHUNKS):
        chunk(i).wait()
        at = pl.ds(i * block, block)
        values = tokens_ref[at]
        average = jnp.mean(values, axis=-1, keepdims=True)
        centered = values - average
        variance = jnp.mean(centered * centered, axis=-1, keepdims=True)
        normed_ref[at] = (centered * lax.rsqrt(variance + epsilon) * gain).astype(jnp.bfloat16)
        if (i + 1) * PARTS % CHUNKS == 0:
            p = (i + 1) * PARTS // CHUNKS - 1
            sent.append(pltpu.make_async_copy(normed_ref.at[pl.ds(p * part, part)], outs[p], out_sem.at[p]))
            sent[-1].start()
    sent.append(pltpu.make_async_copy(normed_ref, outs[PARTS], out_sem.at[PARTS]))
    sent[-1].start()
    small[1].wait()
    band = lax.axis_index("lat")
    lists = ((jnp.maximum(band - 1, 0), 1), (jnp.minimum(band + 1, bands - 1), 0))
    for which, (owner, side) in enumerate(lists):
        wanted = halo_rows_ref[pl.ds(owner, 1), side, :]
        slots = lax.broadcasted_iota(jnp.int32, (rows, wanted.shape[1]), 0)
        picks = (slots == wanted).astype(jnp.float32).astype(jnp.bfloat16)
        picked = lax.dot_general(
            picks, normed_ref[...], (((0,), (0,)), ((), ())), preferred_element_type=jnp.float32
        )
        edge_ref[which] = picked.astype(jnp.bfloat16)
        place = PARTS + 1 + which
        sent.append(pltpu.make_async_copy(edge_ref.at[which], outs[place], out_sem.at[place]))
        sent[-1].start()
    for copy in sent:
        copy.wait()


def norm_call(tokens, gain, halo_rows):
    rows, width = tokens.shape
    bands, _, halo = halo_rows.shape
    part = jax.ShapeDtypeStruct((rows // PARTS, width), jnp.bfloat16)
    whole = jax.ShapeDtypeStruct((rows, width), jnp.bfloat16)
    edge = jax.ShapeDtypeStruct((halo, width), jnp.bfloat16)
    return pl.pallas_call(
        functools.partial(norm_kernel, bands),
        out_shape=[part] * PARTS + [whole] + [edge] * 2,
        in_specs=[pl.BlockSpec(memory_space=pl.ANY)] * 3,
        out_specs=[pl.BlockSpec(memory_space=pltpu.HBM)] * (PARTS + 3),
        scratch_shapes=[
            pltpu.VMEM((rows, width), jnp.float32),
            pltpu.VMEM((1, width), jnp.float32),
            pltpu.VMEM(halo_rows.shape, jnp.int32),
            pltpu.VMEM((rows, width), jnp.bfloat16),
            pltpu.VMEM((2, halo, width), jnp.bfloat16),
            pltpu.SemaphoreType.DMA((CHUNKS + 2,)),
            pltpu.SemaphoreType.DMA((PARTS + 3,)),
        ],
        compiler_params=pltpu.CompilerParams(vmem_limit_bytes=VMEM_LIMIT),
        cost_estimate=pl.CostEstimate(flops=10 * rows * width, bytes_accessed=6 * rows * width, transcendentals=0),
        name="layer_norm",
    )(tokens, gain.reshape(1, width), halo_rows)


def sector_columns(lon, reach):
    core, odd = lon % 2, (lon // 2) % 2
    return {
        "own": reach,
        "partner": reach + 1 - 2 * core,
        "same": reach + 2 - 4 * odd,
        "across": reach + 4 * odd - 2,
        "near": reach + 2 * core - 1,
    }


def block_bias(mask_ref, column, rows, dtype):
    blocks = mask_ref.shape[0]
    values = [jnp.where(mask_ref[b, column] > 0, 0.0, NEG) for b in range(blocks)]
    return jnp.concatenate([jnp.full((rows // blocks, LANES), v, jnp.float32) for v in values], axis=0).astype(dtype)


def safe_group(query, weights, sources, counts_ref, mask_ref, scratch, head_size):
    rows_ref, key_ref, value_ref, top_ref, sum_ref, acc_ref, flag_ref, limit_ref, sem = scratch
    rows = query.shape[0]
    wk, wv = weights
    tile = sources[0][0].shape[0]
    tiles = len(sources)
    blocks = mask_ref.shape[0]
    for t, (ref, column, seen, start) in enumerate(sources):
        size = ref.shape[0]
        copy = pltpu.make_async_copy(ref, rows_ref.at[pl.ds(0, size)], sem)
        copy.start()
        copy.wait()
        key_ref[pl.ds(t * tile, size)] = matmul(rows_ref[pl.ds(0, size)], wk[...]).astype(jnp.bfloat16)
        value_ref[pl.ds(t * tile, size)] = matmul(rows_ref[pl.ds(0, size)], wv[...]).astype(jnp.bfloat16)
        if size < tile:
            rest = pl.ds(t * tile + size, tile - size)
            key_ref[rest] = jnp.zeros((tile - size, key_ref.shape[1]), jnp.bfloat16)
            value_ref[rest] = jnp.zeros((tile - size, key_ref.shape[1]), jnp.bfloat16)
        for b in range(blocks):
            flag_ref[t, b] = mask_ref[b, column] if column is not None else 1
        if column is None:
            limit_ref[t] = jnp.where(seen, size, 0)
        else:
            limit_ref[t] = counts_ref[0] - start
    low = lax.broadcasted_iota(jnp.int32, (rows, LANES), 1) < head_size
    outs = []
    for pair in range(query.shape[1] // LANES):
        lanes = slice(pair * LANES, (pair + 1) * LANES)
        halves = []
        for head in range(2):
            own = jnp.where(low if head == 0 else ~low, query[:, lanes], jnp.zeros((), jnp.bfloat16))
            top_ref[...] = jnp.full_like(top_ref, FLOOR)
            sum_ref[...] = jnp.zeros_like(sum_ref)
            acc_ref[...] = jnp.zeros_like(acc_ref)

            def body(t, carry, own=own, lanes=lanes):
                at = pl.ds(pl.multiple_of(t * tile, tile), tile)
                scores = contract_last(own, key_ref[at, lanes]) * (LOG2E * head_size**-0.5)
                slot = lax.broadcasted_iota(jnp.int32, (1, tile), 1)
                scores = scores + jnp.where(slot < limit_ref[t], 0.0, NEG)
                row_bias = jnp.concatenate(
                    [
                        jnp.full((rows // blocks, 1), jnp.where(flag_ref[t, b] > 0, 0.0, NEG), jnp.float32)
                        for b in range(blocks)
                    ],
                    axis=0,
                )
                scores = scores + row_bias
                old = top_ref[...]
                new = jnp.maximum(old, jnp.max(scores, axis=-1, keepdims=True))
                scale = jnp.exp2(old - new)
                weight = jnp.exp2(scores - new[:, :1])
                sum_ref[...] = sum_ref[...] * scale + jnp.sum(weight, axis=-1, keepdims=True)
                acc_ref[...] = acc_ref[...] * scale + matmul(weight.astype(jnp.bfloat16), value_ref[at, lanes])
                top_ref[...] = new
                return carry

            lax.fori_loop(0, tiles, body, 0)
            halves.append(acc_ref[...] / sum_ref[...])
        outs.append(jnp.where(low, *halves).astype(jnp.bfloat16))
    return jnp.concatenate(outs, axis=1)


def stage_kernel(spec, *refs):
    first, last, sectors, part_starts, halos, head_size = spec
    refs = list(refs)

    def take(count):
        taken = refs[:count]
        del refs[:count]
        return taken

    counts_ref, mask_ref = take(2)
    sector_refs = [take(len(starts)) for starts in part_starts]
    halo_refs = take(2) if halos else []
    wq_ref = take(1)[0] if first else None
    wk_ref, wv_ref = take(2)
    if not first:
        query_in, acc_in, sum_in = take(3)
    if last:
        tokens_ref, wo_ref = take(2)
        all_refs = take(1 + 4 * PARTS + 2)
        (out_ref,) = take(1)
    else:
        if first:
            query_out = take(1)[0]
        acc_out, sum_out = take(2)
    key_ref, value_ref, ones_ref = take(3)
    score_refs, weight_refs = take(2), take(2)
    if last:
        res_ref, att_ref, acc_out, sum_out = take(4)

    reach = mask_ref.shape[1] // 2
    lon, lat = lax.axis_index("lon"), lax.axis_index("lat")
    bands = lax.axis_size("lat")
    columns = sector_columns(lon, reach)
    count = counts_ref[0]

    wk, wv = wk_ref[...], wv_ref[...]
    if first:
        query = jnp.concatenate([matmul(ref[...], wq_ref[...]).astype(jnp.bfloat16) for ref in sector_refs[0]], axis=0)
        query_out[...] = query
    else:
        query = query_in[...]
    rows, width = query.shape
    zero = jnp.zeros((), jnp.bfloat16)
    one = jnp.ones((), jnp.bfloat16)
    biases, spans = [], []
    at = 0
    for name, parts, starts in zip(sectors, sector_refs, part_starts):
        begin = at
        for ref, start in zip(parts, starts):
            size = ref.shape[0]
            here = pl.ds(at, size)
            key_ref[:, here] = matmul(ref[...], wk).astype(jnp.bfloat16).T
            value = matmul(ref[...], wv)
            if start + size <= rows // 2:
                value_ref[here] = value.astype(jnp.bfloat16)
                ones_ref[here] = jnp.ones((size, LANES), jnp.bfloat16)
            else:
                live = start + lax.broadcasted_iota(jnp.int32, value.shape, 0) < count
                value_ref[here] = jnp.where(live, value, 0.0).astype(jnp.bfloat16)
                ones_ref[here] = jnp.where(live[:, :LANES], 1.0, 0.0).astype(jnp.bfloat16)
            at += size
        spans.append((begin, at))
        biases.append(None if name == "own" else block_bias(mask_ref, columns[name], rows, jnp.bfloat16))
    if halo_refs:
        begin = at
        for ref, seen in zip(halo_refs, (lat > 0, lat < bands - 1)):
            size = ref.shape[0]
            here = pl.ds(at, size)
            there = jnp.where(seen, 1.0, 0.0)
            key_ref[:, here] = matmul(ref[...], wk).astype(jnp.bfloat16).T
            value_ref[here] = (matmul(ref[...], wv) * there).astype(jnp.bfloat16)
            ones_ref[here] = jnp.full((size, LANES), there, jnp.float32).astype(jnp.bfloat16)
            at += size
        spans.append((begin, at))
        biases.append(None)

    low = lax.broadcasted_iota(jnp.int32, (rows, LANES), 1) < head_size
    low_key = lax.broadcasted_iota(jnp.int32, (LANES, at), 0) < head_size
    low_value = lax.broadcasted_iota(jnp.int32, (at, LANES), 1) < head_size

    def lanes_of(unit):
        return slice(unit // 2 * LANES, (unit // 2 + 1) * LANES)

    def score(unit):
        lanes, odd = lanes_of(unit), unit % 2
        half = ~low if odd else low
        right = jnp.where(~low_key if odd else low_key, key_ref[lanes, :], one)
        for (begin, end), bias in zip(spans, biases):
            left = jnp.where(half, query[:, lanes], zero if bias is None else bias)
            score_refs[odd][:, begin:end] = matmul(left, right[:, begin:end])

    def weigh(unit):
        scores = score_refs[unit % 2][...] * (LOG2E * head_size**-0.5)
        weight_refs[unit % 2][...] = jnp.exp2(scores).astype(jnp.bfloat16)

    halves = {}

    def gather(unit):
        lanes, odd = lanes_of(unit), unit % 2
        values = jnp.where(~low_value if odd else low_value, value_ref[:, lanes], ones_ref[...])
        halves[odd] = matmul(weight_refs[odd][...], values)
        if not odd:
            return
        acc, total = jnp.where(low, halves[0], halves[1]), jnp.where(low, halves[1], halves[0])
        if not first:
            acc = acc + acc_in[:, lanes]
            total = total + sum_in[:, lanes]
        acc_out[:, lanes] = acc
        sum_out[:, lanes] = total

    units = width // head_size
    for u in range(units + 2):
        if u < units:
            score(u)
        if 0 <= u - 1 < units:
            weigh(u - 1)
        if 0 <= u - 2 < units:
            gather(u - 2)
    if not last:
        return

    total = sum_out[...]
    fine = (total > SUM_MIN) & (total < SUM_MAX)
    for pair in range(width // LANES):
        lanes = slice(pair * LANES, (pair + 1) * LANES)
        att_ref[:, lanes] = (acc_out[:, lanes] / pltpu.roll(total[:, lanes], head_size, 1)).astype(jnp.bfloat16)

    @pl.when(jnp.min(fine.astype(jnp.float32)) < 0.5)
    def _():
        sources = []
        part = rows // PARTS
        for i in range(PARTS):
            sources.append((all_refs[0].at[pl.ds(i * part, part)], columns["partner"], None, i * part))
        for s, name in enumerate(("own", "same", "across", "near")):
            for i, ref in enumerate(all_refs[1 + s * PARTS : 1 + (s + 1) * PARTS]):
                sources.append((ref, columns[name], None, i * part))
        for ref, seen in zip(all_refs[1 + 4 * PARTS :], (lat > 0, lat < bands - 1)):
            sources.append((ref, None, seen, 0))
        att_ref[...] = safe_group(query, (wk_ref, wv_ref), sources, counts_ref, mask_ref, refs, head_size)

    step = pl.program_id(0)

    @pl.when(step == 0)
    def _():
        res_ref[...] = jnp.zeros_like(res_ref)

    at = pl.ds(pl.multiple_of(step * width, width), width)
    res_ref[:, at] += tokens_ref[...]
    res_ref[...] += matmul(att_ref[...], wo_ref[...])

    @pl.when(step == pl.num_programs(0) - 1)
    def _():
        slot = lax.broadcasted_iota(jnp.int32, res_ref.shape, 0)
        out_ref[...] = jnp.where(slot < count, res_ref[...], 0.0)


def stage_call(block_rows, counts, mask, sectors, sector_parts, halos, qkv_weight, query=None, state=None, final=None, starts=None):
    first, last = query is None, final is not None
    model, width = qkv_weight.shape[0], qkv_weight.shape[1] // 3
    head_size = width // HEADS
    rows = mask.shape[0] * block_rows
    steps = width // GROUP
    smem = pl.BlockSpec(memory_space=pltpu.SMEM)

    def fixed(shape):
        return pl.BlockSpec(shape, lambda g: (0, 0), pipeline_mode=pl.Buffered(1))

    def weight(third):
        return pl.BlockSpec((model, GROUP), lambda g: (0, third * steps + g))

    columns = pl.BlockSpec((rows, GROUP), lambda g: (0, g))
    args, specs = [counts, mask], [smem, smem]
    for parts in sector_parts:
        args += parts
        specs += [fixed(p.shape) for p in parts]
    for halo in halos:
        args.append(halo)
        specs.append(fixed(halo.shape))
    for third in range(0 if first else 1, 3):
        args.append(qkv_weight)
        specs.append(weight(third))
    if not first:
        args += [query, *state]
        specs += [columns] * 3
    keys = sum(p.shape[0] for parts in sector_parts for p in parts) + sum(h.shape[0] for h in halos)
    scratch = [
        pltpu.VMEM((GROUP, keys), jnp.bfloat16),
        pltpu.VMEM((keys, GROUP), jnp.bfloat16),
        pltpu.VMEM((keys, LANES), jnp.bfloat16),
        pltpu.VMEM((rows, keys), jnp.float32),
        pltpu.VMEM((rows, keys), jnp.float32),
        pltpu.VMEM((rows, keys), jnp.bfloat16),
        pltpu.VMEM((rows, keys), jnp.bfloat16),
    ]
    wide = jax.ShapeDtypeStruct((rows, width), jnp.float32)
    moved = sum(a.size * a.dtype.itemsize for a in args[2:] if a is not qkv_weight) + 3 * model * width * 2
    if last:
        tokens, out_weight, sources = final
        args += [tokens, out_weight, *sources]
        specs += [columns, pl.BlockSpec((GROUP, out_weight.shape[1]), lambda g: (g, 0))]
        specs += [pl.BlockSpec(memory_space=pl.ANY)] * len(sources)
        out_shape = [wide]
        out_specs = [fixed((rows, width))]
        part = rows // PARTS
        tiles = len(sources) + PARTS - 1
        scratch += [
            pltpu.VMEM((rows, width), jnp.float32),
            pltpu.VMEM((rows, GROUP), jnp.bfloat16),
            pltpu.VMEM((rows, GROUP), jnp.float32),
            pltpu.VMEM((rows, GROUP), jnp.float32),
            pltpu.VMEM((part, model), jnp.bfloat16),
            pltpu.VMEM((part * tiles, GROUP), jnp.bfloat16),
            pltpu.VMEM((part * tiles, GROUP), jnp.bfloat16),
            pltpu.VMEM((rows, LANES), jnp.float32),
            pltpu.VMEM((rows, LANES), jnp.float32),
            pltpu.VMEM((rows, LANES), jnp.float32),
            pltpu.SMEM((tiles, mask.shape[0]), jnp.int32),
            pltpu.SMEM((tiles,), jnp.int32),
            pltpu.SemaphoreType.DMA,
        ]
    else:
        out_shape = [wide] * 2
        out_specs = [columns] * 2
        if first:
            out_shape = [jax.ShapeDtypeStruct((rows, width), jnp.bfloat16)] + out_shape
            out_specs = [columns] + out_specs
    flops = 2 * keys * model * 2 * width + 16 * rows * keys * width
    flops += 2 * rows * model * width * (int(first) + int(last))
    outs = pl.pallas_call(
        functools.partial(stage_kernel, (first, last, sectors, starts, bool(halos), head_size)),
        out_shape=out_shape,
        grid=(steps,),
        in_specs=specs,
        out_specs=out_specs,
        scratch_shapes=scratch,
        compiler_params=pltpu.CompilerParams(vmem_limit_bytes=VMEM_LIMIT),
        cost_estimate=pl.CostEstimate(flops=flops, bytes_accessed=moved, transcendentals=rows * keys * HEADS),
        name="attend_" + "_".join(sectors),
    )(*args)
    if last:
        return outs[0]
    if first:
        return outs[0], outs[1:]
    return outs


def permuted(values, axis, target):
    size = lax.axis_size(axis)
    pairs = [(i, target(i)) for i in range(size) if 0 <= target(i) < size]
    return [lax.ppermute(v, axis, pairs) for v in values]


def on_device(tokens, norm_gain, qkv_weight, out_weight, band_counts, halo_rows, window_mask):
    mask = window_mask[0, 0]
    ring = lax.axis_size("lon")
    assert mask.shape[1] == 5 and ring % 4 == 0 and ring >= 8
    local = tokens[0, 0]
    rows = local.shape[0]
    outs = norm_call(local, norm_gain, halo_rows)
    own, (whole, north_rows, south_rows) = outs[:PARTS], outs[PARTS:]

    same = permuted(own, "lon", lambda i: i ^ 2)
    across = permuted(own[1:], "lon", lambda i: (i + (-2 if (i // 2) % 2 == 0 else 2)) % ring)
    partner = permuted([whole], "lon", lambda i: i ^ 1)
    halos = [
        permuted([south_rows], "lat", lambda b: b + 1)[0],
        permuted([north_rows], "lat", lambda b: b - 1)[0],
    ]
    lon = lax.axis_index("lon")
    gives_same = lon % 2 == (lon // 2) % 2

    def swapped(mine, others):
        return permuted([jnp.where(gives_same, mine, others)], "lon", lambda i: i ^ 1)[0]

    stage = functools.partial(stage_call, rows // mask.shape[0], band_counts, mask)
    half = rows // PARTS
    query, state = stage(["own"], [own], [], qkv_weight, starts=[[0, half]])

    same[0], query, state = lax.optimization_barrier((same[0], query, state))
    across = permuted(same[:1], "lon", lambda i: (i + (4 if (i // 2) % 2 == 0 else -4)) % ring) + across
    state = stage(["partner"], [partner], halos, qkv_weight, query, state, starts=[[0]])

    across[0], state = lax.optimization_barrier((across[0], state))
    near = [swapped(same[0], across[0])]
    state = stage(["same", "across"], [same[:1], across[:1]], [], qkv_weight, query, state, starts=[[0], [0]])

    across[1], state = lax.optimization_barrier((across[1], state))
    near.append(swapped(same[1], across[1]))
    final = (local, out_weight, [*partner, *own, *same, *across, *near, *halos])
    result = stage(
        ["same", "across", "near"],
        [same[1:], across[1:], near],
        [],
        qkv_weight,
        query,
        state,
        final,
        starts=[[half], [half], [0, half]],
    )
    return result[None, None]


def solution(mesh):
    in_specs = (
        P("lat", "lon", None, None),
        P(),
        P(),
        P(),
        P("lat"),
        P(),
        P("lat", "lon", None, None),
    )
    out_specs = P("lat", "lon", None, None)
    return jax.shard_map(
        on_device, mesh=mesh, in_specs=in_specs, out_specs=out_specs, check_vma=False
    )
```

```python
import functools
import math

import jax
import jax.numpy as jnp
from jax import lax
from jax.experimental import pallas as pl
from jax.experimental.pallas import tpu as pltpu
from jax.sharding import PartitionSpec as P

HEADS = 16
LANES = 128
GROUP = 256
PARTS = 2
NEG = -1e30
FLOOR = -1e25
LOG2E = math.log2(math.e)
SUM_MIN, SUM_MAX = 2.0**-60, 2.0**100
NORM_VMEM = 60 * 1024 * 1024
STAGE_VMEM = 32 * 1024 * 1024
CHUNKS = 4

epsilon = 1e-05


def contract_last(a, b):
    return lax.dot_general(a, b, (((1,), (1,)), ((), ())), preferred_element_type=jnp.float32)


def matmul(a, b):
    return jnp.dot(a, b, preferred_element_type=jnp.float32)


def norm_kernel(bands, tokens_hbm, gain_hbm, halo_rows_hbm, *refs):
    outs = refs[: PARTS + 3]
    tokens_ref, gain_ref, halo_rows_ref, normed_ref, edge_ref, in_sem, out_sem = refs[PARTS + 3 :]
    rows = tokens_ref.shape[0]
    block = rows // CHUNKS

    def chunk(i):
        at = pl.ds(i * block, block)
        return pltpu.make_async_copy(tokens_hbm.at[at], tokens_ref.at[at], in_sem.at[i])

    small = [
        pltpu.make_async_copy(gain_hbm, gain_ref, in_sem.at[CHUNKS]),
        pltpu.make_async_copy(halo_rows_hbm, halo_rows_ref, in_sem.at[CHUNKS + 1]),
    ]
    for copy in [chunk(0)] + small + [chunk(i) for i in range(1, CHUNKS)]:
        copy.start()
    small[0].wait()
    gain = gain_ref[...]
    sent = []
    part = rows // PARTS
    for i in range(CHUNKS):
        chunk(i).wait()
        at = pl.ds(i * block, block)
        values = tokens_ref[at]
        average = jnp.mean(values, axis=-1, keepdims=True)
        centered = values - average
        variance = jnp.mean(centered * centered, axis=-1, keepdims=True)
        normed_ref[at] = (centered * lax.rsqrt(variance + epsilon) * gain).astype(jnp.bfloat16)
        if (i + 1) * PARTS % CHUNKS == 0:
            p = (i + 1) * PARTS // CHUNKS - 1
            sent.append(pltpu.make_async_copy(normed_ref.at[pl.ds(p * part, part)], outs[p], out_sem.at[p]))
            sent[-1].start()
    sent.append(pltpu.make_async_copy(normed_ref, outs[PARTS], out_sem.at[PARTS]))
    sent[-1].start()
    small[1].wait()
    band = lax.axis_index("lat")
    lists = ((jnp.maximum(band - 1, 0), 1), (jnp.minimum(band + 1, bands - 1), 0))
    for which, (owner, side) in enumerate(lists):
        wanted = halo_rows_ref[pl.ds(owner, 1), side, :]
        slots = lax.broadcasted_iota(jnp.int32, (rows, wanted.shape[1]), 0)
        picks = (slots == wanted).astype(jnp.float32).astype(jnp.bfloat16)
        picked = lax.dot_general(
            picks, normed_ref[...], (((0,), (0,)), ((), ())), preferred_element_type=jnp.float32
        )
        edge_ref[which] = picked.astype(jnp.bfloat16)
        place = PARTS + 1 + which
        sent.append(pltpu.make_async_copy(edge_ref.at[which], outs[place], out_sem.at[place]))
        sent[-1].start()
    for copy in sent:
        copy.wait()


def norm_call(tokens, gain, halo_rows):
    rows, width = tokens.shape
    bands, _, halo = halo_rows.shape
    part = jax.ShapeDtypeStruct((rows // PARTS, width), jnp.bfloat16)
    whole = jax.ShapeDtypeStruct((rows, width), jnp.bfloat16)
    edge = jax.ShapeDtypeStruct((halo, width), jnp.bfloat16)
    return pl.pallas_call(
        functools.partial(norm_kernel, bands),
        out_shape=[part] * PARTS + [whole] + [edge] * 2,
        in_specs=[pl.BlockSpec(memory_space=pl.ANY)] * 3,
        out_specs=[pl.BlockSpec(memory_space=pltpu.HBM)] * (PARTS + 3),
        scratch_shapes=[
            pltpu.VMEM((rows, width), jnp.float32),
            pltpu.VMEM((1, width), jnp.float32),
            pltpu.VMEM(halo_rows.shape, jnp.int32),
            pltpu.VMEM((rows, width), jnp.bfloat16),
            pltpu.VMEM((2, halo, width), jnp.bfloat16),
            pltpu.SemaphoreType.DMA((CHUNKS + 2,)),
            pltpu.SemaphoreType.DMA((PARTS + 3,)),
        ],
        compiler_params=pltpu.CompilerParams(vmem_limit_bytes=NORM_VMEM),
        cost_estimate=pl.CostEstimate(flops=10 * rows * width, bytes_accessed=6 * rows * width, transcendentals=0),
        name="layer_norm",
    )(tokens, gain.reshape(1, width), halo_rows)


def sector_columns(lon, reach):
    core, odd = lon % 2, (lon // 2) % 2
    return {
        "own": reach,
        "partner": reach + 1 - 2 * core,
        "same": reach + 2 - 4 * odd,
        "across": reach + 4 * odd - 2,
        "near": reach + 2 * core - 1,
    }


def block_bias(mask_ref, column, rows, dtype):
    blocks = mask_ref.shape[0]
    values = [jnp.where(mask_ref[b, column] > 0, 0.0, NEG) for b in range(blocks)]
    return jnp.concatenate([jnp.full((rows // blocks, LANES), v, jnp.float32) for v in values], axis=0).astype(dtype)


def safe_attention(query_ref, weight, groups, sources, counts_ref, mask_ref, att_ref, scratch, head_size):
    key_ref, value_ref, top_ref, sum_ref, acc_ref, flag_ref, limit_ref = scratch
    pairs, rows, _ = query_ref.shape
    tile = sources[0][0].shape[0]
    blocks = mask_ref.shape[0]
    low = lax.broadcasted_iota(jnp.int32, (rows, LANES), 1) < head_size

    def group_body(g, carry):
        for t, (ref, column, seen, start) in enumerate(sources):
            size = ref.shape[0]
            key_ref[pl.ds(t * tile, size)] = matmul(ref[...], weight(1, g)).astype(jnp.bfloat16)
            value_ref[pl.ds(t * tile, size)] = matmul(ref[...], weight(2, g)).astype(jnp.bfloat16)
            if size < tile:
                rest = pl.ds(t * tile + size, tile - size)
                key_ref[rest] = jnp.zeros((tile - size, key_ref.shape[1]), jnp.bfloat16)
                value_ref[rest] = jnp.zeros((tile - size, key_ref.shape[1]), jnp.bfloat16)
            for b in range(blocks):
                flag_ref[t, b] = mask_ref[b, column] if column is not None else 1
            if column is None:
                limit_ref[t] = jnp.where(seen, size, 0)
            else:
                limit_ref[t] = counts_ref[0] - start
        for pair in range(pairs // groups):
            lanes = slice(pair * LANES, (pair + 1) * LANES)
            place = g * (pairs // groups) + pair
            halves = []
            for head in range(2):
                own = jnp.where(low if head == 0 else ~low, query_ref[place], jnp.zeros((), jnp.bfloat16))
                top_ref[...] = jnp.full_like(top_ref, FLOOR)
                sum_ref[...] = jnp.zeros_like(sum_ref)
                acc_ref[...] = jnp.zeros_like(acc_ref)

                def body(t, carry, own=own, lanes=lanes):
                    at = pl.ds(pl.multiple_of(t * tile, tile), tile)
                    scores = contract_last(own, key_ref[at, lanes]) * (LOG2E * head_size**-0.5)
                    slot = lax.broadcasted_iota(jnp.int32, (1, tile), 1)
                    scores = scores + jnp.where(slot < limit_ref[t], 0.0, NEG)
                    row_bias = jnp.concatenate(
                        [
                            jnp.full((rows // blocks, 1), jnp.where(flag_ref[t, b] > 0, 0.0, NEG), jnp.float32)
                            for b in range(blocks)
                        ],
                        axis=0,
                    )
                    scores = scores + row_bias
                    old = top_ref[...]
                    new = jnp.maximum(old, jnp.max(scores, axis=-1, keepdims=True))
                    scale = jnp.exp2(old - new)
                    weight = jnp.exp2(scores - new[:, :1])
                    sum_ref[...] = sum_ref[...] * scale + jnp.sum(weight, axis=-1, keepdims=True)
                    acc_ref[...] = acc_ref[...] * scale + matmul(weight.astype(jnp.bfloat16), value_ref[at, lanes])
                    top_ref[...] = new
                    return carry

                lax.fori_loop(0, len(sources), body, 0)
                halves.append(acc_ref[...] / sum_ref[...])
            att_ref[place] = jnp.where(low, *halves).astype(jnp.bfloat16)
        return carry

    lax.fori_loop(0, groups, group_body, 0)


def stage_kernel(spec, *refs):
    first, last, sectors, part_starts, halos, head_size = spec
    refs = list(refs)

    def take(count):
        taken = refs[:count]
        del refs[:count]
        return taken

    counts_ref, mask_ref = take(2)
    sector_refs = [take(len(starts)) for starts in part_starts]
    halo_refs = take(2) if halos else []
    (qkv_ref,) = take(1)
    if not first:
        query_ref, sums_in = take(2)
    if last:
        tokens_hbm, wo_hbm = take(2)
        all_refs = take(1 + 4 * PARTS + 2)
        (out_hbm,) = take(1)
    else:
        if first:
            (query_ref,) = take(1)
        (sums_ref,) = take(1)
    key_ref, value_ref, ones_ref = take(3)
    score_refs, exp_refs = take(2), take(2)
    if last:
        sums_ref, att_ref, tokens_ref, wo_ref, fine_ref, in_sem, out_sem = take(7)

    pairs, rows, _ = query_ref.shape
    group = GROUP
    each = group // LANES
    groups = pairs // each
    reach = mask_ref.shape[1] // 2
    lon, lat = lax.axis_index("lon"), lax.axis_index("lat")
    bands = lax.axis_size("lat")
    columns = sector_columns(lon, reach)
    count = counts_ref[0]
    keys = ones_ref.shape[0]

    def weight(third, g):
        return qkv_ref[:, pl.ds(pl.multiple_of(third * groups * group + g * group, group), group)]

    later = []
    if last:
        later.append(pltpu.make_async_copy(tokens_hbm, tokens_ref, in_sem.at[0]))
        later.append(pltpu.make_async_copy(wo_hbm, wo_ref, in_sem.at[1]))
    for copy in later:
        copy.start()

    biases, spans, pieces = [], [], []
    at = 0
    for name, parts, starts in zip(sectors, sector_refs, part_starts):
        begin = at
        for ref, start in zip(parts, starts):
            for r in range(0, ref.shape[0], group):
                size = min(group, ref.shape[0] - r)
                if start + r + size <= rows // 2:
                    live = None
                else:
                    slot = start + r + lax.broadcasted_iota(jnp.int32, (size, group), 0)
                    live = jnp.where(slot < count, 1.0, 0.0)
                pieces.append((ref, r, at, size, live))
                at += size
        spans.append((begin, at))
        biases.append(None if name == "own" else block_bias(mask_ref, columns[name], rows, jnp.bfloat16))
    if halo_refs:
        begin = at
        for ref, seen in zip(halo_refs, (lat > 0, lat < bands - 1)):
            size = ref.shape[0]
            pieces.append((ref, 0, at, size, jnp.full((size, group), jnp.where(seen, 1.0, 0.0), jnp.float32)))
            at += size
        spans.append((begin, at))
        biases.append(None)
    for _, _, begin, size, live in pieces:
        ones = jnp.ones((size, LANES), jnp.float32) if live is None else live[:, :LANES]
        ones_ref[pl.ds(begin, size)] = ones.astype(jnp.bfloat16)

    def project(g, carry):
        for ref, r, begin, size, live in pieces:
            here = pl.ds(begin, size)
            normed = ref[pl.ds(r, size)]
            if first:
                query = matmul(normed, weight(0, g)).astype(jnp.bfloat16)
                for p in range(each):
                    query_ref[g * each + p, here] = query[:, p * LANES : (p + 1) * LANES]
            key = matmul(normed, weight(1, g)).astype(jnp.bfloat16).T
            value = matmul(normed, weight(2, g))
            if live is not None:
                value = jnp.where(live > 0, value, 0.0)
            value = value.astype(jnp.bfloat16)
            for p in range(each):
                lanes = slice(p * LANES, (p + 1) * LANES)
                key_ref[g * each + p, :, here] = key[lanes]
                value_ref[g * each + p, here] = value[:, lanes]
        return carry

    lax.fori_loop(0, groups, project, 0)

    zero = jnp.zeros((), jnp.bfloat16)
    one = jnp.ones((), jnp.bfloat16)
    low = lax.broadcasted_iota(jnp.int32, (rows, LANES), 1) < head_size
    low_key = lax.broadcasted_iota(jnp.int32, (LANES, keys), 0) < head_size
    low_value = lax.broadcasted_iota(jnp.int32, (keys, LANES), 1) < head_size

    def score(pair, odd):
        half = ~low if odd else low
        query = query_ref[pair]
        right = jnp.where(~low_key if odd else low_key, key_ref[pair], one)
        for (begin, end), bias in zip(spans, biases):
            left = jnp.where(half, query, zero if bias is None else bias)
            score_refs[odd][:, begin:end] = matmul(left, right[:, begin:end])

    def weigh(odd):
        exp_refs[odd][...] = jnp.exp2(score_refs[odd][...] * (LOG2E * head_size**-0.5)).astype(jnp.bfloat16)

    def gather(pair, odd):
        values = jnp.where(~low_value if odd else low_value, value_ref[pair], ones_ref[...])
        result = matmul(exp_refs[odd][...], values)
        if not first:
            result = result + sums_in[2 * pair + odd]
        sums_ref[2 * pair + odd] = result

    def finish(pair):
        if not last:
            return
        even, odd = sums_ref[2 * pair], sums_ref[2 * pair + 1]
        total = jnp.where(low, odd, even)
        fine = jnp.where((total > SUM_MIN) & (total < SUM_MAX), 1.0, 0.0)
        fine_ref[...] = jnp.minimum(fine_ref[...], fine)
        att_ref[pair] = (jnp.where(low, even, odd) / pltpu.roll(total, head_size, 1)).astype(jnp.bfloat16)

    if last:
        fine_ref[...] = jnp.ones_like(fine_ref)
    score(0, 0)
    score(0, 1)
    weigh(0)

    def attend(pair, carry):
        score(pair, 0)
        weigh(1)
        gather(pair - 1, 0)
        score(pair, 1)
        weigh(0)
        gather(pair - 1, 1)
        finish(pair - 1)
        return carry

    lax.fori_loop(1, pairs, attend, 0)
    weigh(1)
    gather(pairs - 1, 0)
    gather(pairs - 1, 1)
    finish(pairs - 1)

    if not last:
        return

    @pl.when(jnp.min(fine_ref[...]) < 0.5)
    def _():
        sources = []
        part = rows // PARTS
        for i in range(PARTS):
            sources.append((all_refs[0].at[pl.ds(i * part, part)], columns["partner"], None, i * part))
        for s, name in enumerate(("own", "same", "across", "near")):
            for i, ref in enumerate(all_refs[1 + s * PARTS : 1 + (s + 1) * PARTS]):
                sources.append((ref, columns[name], None, i * part))
        for ref, seen in zip(all_refs[1 + 4 * PARTS :], (lat > 0, lat < bands - 1)):
            sources.append((ref, None, seen, 0))
        safe_attention(query_ref, weight, groups, sources, counts_ref, mask_ref, att_ref, refs, head_size)

    for copy in later:
        copy.wait()
    attended = jnp.concatenate([att_ref[p] for p in range(pairs)], axis=1)
    live = lax.broadcasted_iota(jnp.int32, (rows, group), 0) < count
    sent = []
    for n in range(out_hbm.shape[1] // group):
        lanes = pl.ds(n * group, group)
        result = tokens_ref[:, lanes] + matmul(attended, wo_ref[:, lanes])
        tokens_ref[:, lanes] = jnp.where(live, result, 0.0)
        sent.append(pltpu.make_async_copy(tokens_ref.at[:, lanes], out_hbm.at[:, lanes], out_sem.at[n]))
        sent[-1].start()
    for copy in sent:
        copy.wait()


def stage_call(block_rows, counts, mask, sectors, sector_parts, halos, qkv_weight, query=None, sums=None, final=None, starts=None):
    first, last = query is None, final is not None
    model, width = qkv_weight.shape[0], qkv_weight.shape[1] // 3
    head_size = width // HEADS
    rows = mask.shape[0] * block_rows
    pairs, groups = width // LANES, width // GROUP
    smem = pl.BlockSpec(memory_space=pltpu.SMEM)
    hbm = pl.BlockSpec(memory_space=pltpu.HBM)
    vmem = pl.BlockSpec(memory_space=pltpu.VMEM)
    sources = [p for parts in sector_parts for p in parts] + halos
    keys = sum(p.shape[0] for p in sources)
    args = [counts, mask, *sources, qkv_weight]
    if not first:
        args += [query, sums]
    specs = [smem, smem] + [vmem] * (len(args) - 2)
    query_shape = jax.ShapeDtypeStruct((pairs, rows, LANES), jnp.bfloat16)
    sums_shape = jax.ShapeDtypeStruct((2 * pairs, rows, LANES), jnp.float32)
    scratch = [
        pltpu.VMEM((pairs, LANES, keys), jnp.bfloat16),
        pltpu.VMEM((pairs, keys, LANES), jnp.bfloat16),
        pltpu.VMEM((keys, LANES), jnp.bfloat16),
        pltpu.VMEM((rows, keys), jnp.float32),
        pltpu.VMEM((rows, keys), jnp.float32),
        pltpu.VMEM((rows, keys), jnp.bfloat16),
        pltpu.VMEM((rows, keys), jnp.bfloat16),
    ]
    out_specs = [vmem]
    if last:
        tokens, out_weight, everything = final
        args += [tokens, out_weight, *everything]
        specs += [hbm, hbm] + [vmem] * len(everything)
        out_shape = [jax.ShapeDtypeStruct((rows, width), jnp.float32)]
        out_specs = [hbm]
        part = rows // PARTS
        tiles = len(everything) + PARTS - 1
        scratch += [
            pltpu.VMEM(sums_shape.shape, jnp.float32),
            pltpu.VMEM((pairs, rows, LANES), jnp.bfloat16),
            pltpu.VMEM(tokens.shape, jnp.float32),
            pltpu.VMEM(out_weight.shape, jnp.bfloat16),
            pltpu.VMEM((rows, LANES), jnp.float32),
            pltpu.SemaphoreType.DMA((2,)),
            pltpu.SemaphoreType.DMA((groups,)),
            pltpu.VMEM((part * tiles, GROUP), jnp.bfloat16),
            pltpu.VMEM((part * tiles, GROUP), jnp.bfloat16),
            pltpu.VMEM((rows, LANES), jnp.float32),
            pltpu.VMEM((rows, LANES), jnp.float32),
            pltpu.VMEM((rows, LANES), jnp.float32),
            pltpu.SMEM((tiles, mask.shape[0]), jnp.int32),
            pltpu.SMEM((tiles,), jnp.int32),
        ]
    elif first:
        out_shape = [query_shape, sums_shape]
        out_specs = [vmem, vmem]
    else:
        out_shape = [sums_shape]
    flops = 2 * keys * model * 2 * width + 16 * rows * keys * width
    flops += 2 * rows * model * width * (int(first) + int(last))
    moved = 2 * (3 * model * width + keys * model) + 4 * rows * width
    outs = pl.pallas_call(
        functools.partial(stage_kernel, (first, last, sectors, starts, bool(halos), head_size)),
        out_shape=out_shape,
        in_specs=specs,
        out_specs=out_specs,
        scratch_shapes=scratch,
        compiler_params=pltpu.CompilerParams(vmem_limit_bytes=STAGE_VMEM),
        cost_estimate=pl.CostEstimate(flops=flops, bytes_accessed=moved, transcendentals=rows * keys * HEADS),
        name="attend_" + "_".join(sectors),
    )(*args)
    return outs if first else outs[0]


def permuted(values, axis, target):
    size = lax.axis_size(axis)
    pairs = [(i, target(i)) for i in range(size) if 0 <= target(i) < size]
    return [lax.ppermute(v, axis, pairs) for v in values]


def on_device(tokens, norm_gain, qkv_weight, out_weight, band_counts, halo_rows, window_mask):
    mask = window_mask[0, 0]
    ring = lax.axis_size("lon")
    assert mask.shape[1] == 5 and ring % 4 == 0 and ring >= 8
    local = tokens[0, 0]
    rows = local.shape[0]
    outs = norm_call(local, norm_gain, halo_rows)
    own, (whole, north_rows, south_rows) = outs[:PARTS], outs[PARTS:]

    same = permuted(own, "lon", lambda i: i ^ 2)
    across = permuted(own[1:], "lon", lambda i: (i + (-2 if (i // 2) % 2 == 0 else 2)) % ring)
    partner = permuted([whole], "lon", lambda i: i ^ 1)
    halos = [
        permuted([south_rows], "lat", lambda b: b + 1)[0],
        permuted([north_rows], "lat", lambda b: b - 1)[0],
    ]
    lon = lax.axis_index("lon")
    gives_same = lon % 2 == (lon // 2) % 2

    def swapped(mine, others):
        return permuted([jnp.where(gives_same, mine, others)], "lon", lambda i: i ^ 1)[0]

    stage = functools.partial(stage_call, rows // mask.shape[0], band_counts, mask)
    half = rows // PARTS
    query, state = stage(["own"], [own], [], qkv_weight, starts=[[0, half]])

    same[0], query, state = lax.optimization_barrier((same[0], query, state))
    across = permuted(same[:1], "lon", lambda i: (i + (4 if (i // 2) % 2 == 0 else -4)) % ring) + across
    state = stage(["partner"], [partner], halos, qkv_weight, query, state, starts=[[0]])

    across[0], state = lax.optimization_barrier((across[0], state))
    near = [swapped(same[0], across[0])]
    state = stage(["same", "across"], [same[:1], across[:1]], [], qkv_weight, query, state, starts=[[0], [0]])

    across[1], state = lax.optimization_barrier((across[1], state))
    near.append(swapped(same[1], across[1]))
    final = (local, out_weight, [*partner, *own, *same, *across, *near, *halos])
    result = stage(
        ["same", "across", "near"],
        [same[1:], across[1:], near],
        [],
        qkv_weight,
        query,
        state,
        final,
        starts=[[half], [half], [0, half]],
    )
    return result[None, None]


def solution(mesh):
    in_specs = (
        P("lat", "lon", None, None),
        P(),
        P(),
        P(),
        P("lat"),
        P(),
        P("lat", "lon", None, None),
    )
    out_specs = P("lat", "lon", None, None)
    return jax.shard_map(
        on_device, mesh=mesh, in_specs=in_specs, out_specs=out_specs, check_vma=False
    )
```

```python
import functools
import math

import jax
import jax.numpy as jnp
from jax import lax
from jax.experimental import pallas as pl
from jax.experimental.pallas import tpu as pltpu
from jax.sharding import PartitionSpec as P

HEADS = 16
LANES = 128
GROUP = 256
PARTS = 2
NEG = -1e30
FLOOR = -1e25
LOG2E = math.log2(math.e)
SUM_MIN, SUM_MAX = 2.0**-60, 2.0**100
VMEM_LIMIT = 60 * 1024 * 1024
CHUNKS = 4

epsilon = 1e-05


def contract_last(a, b):
    return lax.dot_general(a, b, (((1,), (1,)), ((), ())), preferred_element_type=jnp.float32)


def matmul(a, b):
    return jnp.dot(a, b, preferred_element_type=jnp.float32)


def norm_kernel(bands, tokens_hbm, gain_hbm, halo_rows_hbm, *refs):
    outs = refs[: PARTS + 3]
    tokens_ref, gain_ref, halo_rows_ref, normed_ref, edge_ref, in_sem, out_sem = refs[PARTS + 3 :]
    rows = tokens_ref.shape[0]
    block = rows // CHUNKS

    def chunk(i):
        at = pl.ds(i * block, block)
        return pltpu.make_async_copy(tokens_hbm.at[at], tokens_ref.at[at], in_sem.at[i])

    small = [
        pltpu.make_async_copy(gain_hbm, gain_ref, in_sem.at[CHUNKS]),
        pltpu.make_async_copy(halo_rows_hbm, halo_rows_ref, in_sem.at[CHUNKS + 1]),
    ]
    for copy in [chunk(0)] + small + [chunk(i) for i in range(1, CHUNKS)]:
        copy.start()
    small[0].wait()
    gain = gain_ref[...]
    sent = []
    part = rows // PARTS
    for i in range(CHUNKS):
        chunk(i).wait()
        at = pl.ds(i * block, block)
        values = tokens_ref[at]
        average = jnp.mean(values, axis=-1, keepdims=True)
        centered = values - average
        variance = jnp.mean(centered * centered, axis=-1, keepdims=True)
        normed_ref[at] = (centered * lax.rsqrt(variance + epsilon) * gain).astype(jnp.bfloat16)
        if (i + 1) * PARTS % CHUNKS == 0:
            p = (i + 1) * PARTS // CHUNKS - 1
            sent.append(pltpu.make_async_copy(normed_ref.at[pl.ds(p * part, part)], outs[p], out_sem.at[p]))
            sent[-1].start()
    sent.append(pltpu.make_async_copy(normed_ref, outs[PARTS], out_sem.at[PARTS]))
    sent[-1].start()
    small[1].wait()
    band = lax.axis_index("lat")
    lists = ((jnp.maximum(band - 1, 0), 1), (jnp.minimum(band + 1, bands - 1), 0))
    for which, (owner, side) in enumerate(lists):
        wanted = halo_rows_ref[pl.ds(owner, 1), side, :]
        slots = lax.broadcasted_iota(jnp.int32, (rows, wanted.shape[1]), 0)
        picks = (slots == wanted).astype(jnp.float32).astype(jnp.bfloat16)
        picked = lax.dot_general(
            picks, normed_ref[...], (((0,), (0,)), ((), ())), preferred_element_type=jnp.float32
        )
        edge_ref[which] = picked.astype(jnp.bfloat16)
        place = PARTS + 1 + which
        sent.append(pltpu.make_async_copy(edge_ref.at[which], outs[place], out_sem.at[place]))
        sent[-1].start()
    for copy in sent:
        copy.wait()


def norm_call(tokens, gain, halo_rows):
    rows, width = tokens.shape
    bands, _, halo = halo_rows.shape
    part = jax.ShapeDtypeStruct((rows // PARTS, width), jnp.bfloat16)
    whole = jax.ShapeDtypeStruct((rows, width), jnp.bfloat16)
    edge = jax.ShapeDtypeStruct((halo, width), jnp.bfloat16)
    return pl.pallas_call(
        functools.partial(norm_kernel, bands),
        out_shape=[part] * PARTS + [whole] + [edge] * 2,
        in_specs=[pl.BlockSpec(memory_space=pl.ANY)] * 3,
        out_specs=[pl.BlockSpec(memory_space=pltpu.HBM)] * (PARTS + 3),
        scratch_shapes=[
            pltpu.VMEM((rows, width), jnp.float32),
            pltpu.VMEM((1, width), jnp.float32),
            pltpu.VMEM(halo_rows.shape, jnp.int32),
            pltpu.VMEM((rows, width), jnp.bfloat16),
            pltpu.VMEM((2, halo, width), jnp.bfloat16),
            pltpu.SemaphoreType.DMA((CHUNKS + 2,)),
            pltpu.SemaphoreType.DMA((PARTS + 3,)),
        ],
        compiler_params=pltpu.CompilerParams(vmem_limit_bytes=VMEM_LIMIT),
        cost_estimate=pl.CostEstimate(flops=10 * rows * width, bytes_accessed=6 * rows * width, transcendentals=0),
        name="layer_norm",
    )(tokens, gain.reshape(1, width), halo_rows)


def sector_columns(lon, reach):
    core, odd = lon % 2, (lon // 2) % 2
    return {
        "own": reach,
        "partner": reach + 1 - 2 * core,
        "same": reach + 2 - 4 * odd,
        "across": reach + 4 * odd - 2,
        "near": reach + 2 * core - 1,
    }


def block_bias(mask_ref, column, rows, dtype):
    blocks = mask_ref.shape[0]
    values = [jnp.where(mask_ref[b, column] > 0, 0.0, NEG) for b in range(blocks)]
    return jnp.concatenate([jnp.full((rows // blocks, LANES), v, jnp.float32) for v in values], axis=0).astype(dtype)


def safe_group(query, weights, sources, counts_ref, mask_ref, scratch, head_size):
    rows_ref, key_ref, value_ref, top_ref, sum_ref, acc_ref, flag_ref, limit_ref, sem = scratch
    rows = query.shape[0]
    wk, wv = weights
    tile = sources[0][0].shape[0]
    tiles = len(sources)
    blocks = mask_ref.shape[0]
    for t, (ref, column, seen, start) in enumerate(sources):
        size = ref.shape[0]
        copy = pltpu.make_async_copy(ref, rows_ref.at[pl.ds(0, size)], sem)
        copy.start()
        copy.wait()
        key_ref[pl.ds(t * tile, size)] = matmul(rows_ref[pl.ds(0, size)], wk[...]).astype(jnp.bfloat16)
        value_ref[pl.ds(t * tile, size)] = matmul(rows_ref[pl.ds(0, size)], wv[...]).astype(jnp.bfloat16)
        if size < tile:
            rest = pl.ds(t * tile + size, tile - size)
            key_ref[rest] = jnp.zeros((tile - size, key_ref.shape[1]), jnp.bfloat16)
            value_ref[rest] = jnp.zeros((tile - size, key_ref.shape[1]), jnp.bfloat16)
        for b in range(blocks):
            flag_ref[t, b] = mask_ref[b, column] if column is not None else 1
        if column is None:
            limit_ref[t] = jnp.where(seen, size, 0)
        else:
            limit_ref[t] = counts_ref[0] - start
    low = lax.broadcasted_iota(jnp.int32, (rows, LANES), 1) < head_size
    outs = []
    for pair in range(query.shape[1] // LANES):
        lanes = slice(pair * LANES, (pair + 1) * LANES)
        halves = []
        for head in range(2):
            own = jnp.where(low if head == 0 else ~low, query[:, lanes], jnp.zeros((), jnp.bfloat16))
            top_ref[...] = jnp.full_like(top_ref, FLOOR)
            sum_ref[...] = jnp.zeros_like(sum_ref)
            acc_ref[...] = jnp.zeros_like(acc_ref)

            def body(t, carry, own=own, lanes=lanes):
                at = pl.ds(pl.multiple_of(t * tile, tile), tile)
                scores = contract_last(own, key_ref[at, lanes]) * (LOG2E * head_size**-0.5)
                slot = lax.broadcasted_iota(jnp.int32, (1, tile), 1)
                scores = scores + jnp.where(slot < limit_ref[t], 0.0, NEG)
                row_bias = jnp.concatenate(
                    [
                        jnp.full((rows // blocks, 1), jnp.where(flag_ref[t, b] > 0, 0.0, NEG), jnp.float32)
                        for b in range(blocks)
                    ],
                    axis=0,
                )
                scores = scores + row_bias
                old = top_ref[...]
                new = jnp.maximum(old, jnp.max(scores, axis=-1, keepdims=True))
                scale = jnp.exp2(old - new)
                weight = jnp.exp2(scores - new[:, :1])
                sum_ref[...] = sum_ref[...] * scale + jnp.sum(weight, axis=-1, keepdims=True)
                acc_ref[...] = acc_ref[...] * scale + matmul(weight.astype(jnp.bfloat16), value_ref[at, lanes])
                top_ref[...] = new
                return carry

            lax.fori_loop(0, tiles, body, 0)
            halves.append(acc_ref[...] / sum_ref[...])
        outs.append(jnp.where(low, *halves).astype(jnp.bfloat16))
    return jnp.concatenate(outs, axis=1)


def stage_kernel(spec, *refs):
    first, last, sectors, part_starts, halos, head_size = spec
    refs = list(refs)

    def take(count):
        taken = refs[:count]
        del refs[:count]
        return taken

    counts_ref, mask_ref = take(2)
    sector_refs = [take(len(starts)) for starts in part_starts]
    halo_refs = take(2) if halos else []
    wq_ref = take(1)[0] if first else None
    wk_ref, wv_ref = take(2)
    if not first:
        query_in, acc_in, sum_in = take(3)
    if last:
        tokens_ref, wo_ref = take(2)
        all_refs = take(2 + 3 * PARTS + 2)
        (out_ref,) = take(1)
    else:
        if first:
            query_out = take(1)[0]
        acc_out, sum_out = take(2)
    key_ref, value_ref, ones_ref = take(3)
    score_refs, weight_refs = take(2), take(2)
    if last:
        res_ref, att_ref, acc_out, sum_out = take(4)

    reach = mask_ref.shape[1] // 2
    lon, lat = lax.axis_index("lon"), lax.axis_index("lat")
    bands = lax.axis_size("lat")
    columns = sector_columns(lon, reach)
    count = counts_ref[0]

    wk, wv = wk_ref[...], wv_ref[...]
    if first:
        query = jnp.concatenate([matmul(ref[...], wq_ref[...]).astype(jnp.bfloat16) for ref in sector_refs[0]], axis=0)
        query_out[...] = query
    else:
        query = query_in[...]
    rows, width = query.shape
    zero = jnp.zeros((), jnp.bfloat16)
    one = jnp.ones((), jnp.bfloat16)
    biases, spans = [], []
    at = 0
    for name, parts, starts in zip(sectors, sector_refs, part_starts):
        begin = at
        for ref, start in zip(parts, starts):
            size = ref.shape[0]
            here = pl.ds(at, size)
            key_ref[:, here] = matmul(ref[...], wk).astype(jnp.bfloat16).T
            value = matmul(ref[...], wv)
            if start + size <= rows // 2:
                value_ref[here] = value.astype(jnp.bfloat16)
                ones_ref[here] = jnp.ones((size, LANES), jnp.bfloat16)
            else:
                live = start + lax.broadcasted_iota(jnp.int32, value.shape, 0) < count
                value_ref[here] = jnp.where(live, value, 0.0).astype(jnp.bfloat16)
                ones_ref[here] = jnp.where(live[:, :LANES], 1.0, 0.0).astype(jnp.bfloat16)
            at += size
        spans.append((begin, at))
        biases.append(None if name == "own" else block_bias(mask_ref, columns[name], rows, jnp.bfloat16))
    if halo_refs:
        begin = at
        for ref, seen in zip(halo_refs, (lat > 0, lat < bands - 1)):
            size = ref.shape[0]
            here = pl.ds(at, size)
            there = jnp.where(seen, 1.0, 0.0)
            key_ref[:, here] = matmul(ref[...], wk).astype(jnp.bfloat16).T
            value_ref[here] = (matmul(ref[...], wv) * there).astype(jnp.bfloat16)
            ones_ref[here] = jnp.full((size, LANES), there, jnp.float32).astype(jnp.bfloat16)
            at += size
        spans.append((begin, at))
        biases.append(None)

    low = lax.broadcasted_iota(jnp.int32, (rows, LANES), 1) < head_size
    low_key = lax.broadcasted_iota(jnp.int32, (LANES, at), 0) < head_size
    low_value = lax.broadcasted_iota(jnp.int32, (at, LANES), 1) < head_size

    def lanes_of(unit):
        return slice(unit // 2 * LANES, (unit // 2 + 1) * LANES)

    def score(unit):
        lanes, odd = lanes_of(unit), unit % 2
        half = ~low if odd else low
        right = jnp.where(~low_key if odd else low_key, key_ref[lanes, :], one)
        for (begin, end), bias in zip(spans, biases):
            left = jnp.where(half, query[:, lanes], zero if bias is None else bias)
            score_refs[odd][:, begin:end] = matmul(left, right[:, begin:end])

    def weigh(unit):
        scores = score_refs[unit % 2][...] * (LOG2E * head_size**-0.5)
        weight_refs[unit % 2][...] = jnp.exp2(scores).astype(jnp.bfloat16)

    halves = {}

    def gather(unit):
        lanes, odd = lanes_of(unit), unit % 2
        values = jnp.where(~low_value if odd else low_value, value_ref[:, lanes], ones_ref[...])
        halves[odd] = matmul(weight_refs[odd][...], values)
        if not odd:
            return
        acc, total = jnp.where(low, halves[0], halves[1]), jnp.where(low, halves[1], halves[0])
        if not first:
            acc = acc + acc_in[:, lanes]
            total = total + sum_in[:, lanes]
        acc_out[:, lanes] = acc
        sum_out[:, lanes] = total

    units = width // head_size
    for u in range(units + 2):
        if u < units:
            score(u)
        if 0 <= u - 1 < units:
            weigh(u - 1)
        if 0 <= u - 2 < units:
            gather(u - 2)
    if not last:
        return

    total = sum_out[...]
    fine = (total > SUM_MIN) & (total < SUM_MAX)
    for pair in range(width // LANES):
        lanes = slice(pair * LANES, (pair + 1) * LANES)
        att_ref[:, lanes] = (acc_out[:, lanes] / pltpu.roll(total[:, lanes], head_size, 1)).astype(jnp.bfloat16)

    @pl.when(jnp.min(fine.astype(jnp.float32)) < 0.5)
    def _():
        sources = []
        part = rows // PARTS
        for ref, name in zip(all_refs, ("partner", "near")):
            for i in range(PARTS):
                sources.append((ref.at[pl.ds(i * part, part)], columns[name], None, i * part))
        for s, name in enumerate(("own", "same", "across")):
            for i, ref in enumerate(all_refs[2 + s * PARTS : 2 + (s + 1) * PARTS]):
                sources.append((ref, columns[name], None, i * part))
        for ref, seen in zip(all_refs[2 + 3 * PARTS :], (lat > 0, lat < bands - 1)):
            sources.append((ref, None, seen, 0))
        att_ref[...] = safe_group(query, (wk_ref, wv_ref), sources, counts_ref, mask_ref, refs, head_size)

    step = pl.program_id(0)

    @pl.when(step == 0)
    def _():
        res_ref[...] = jnp.zeros_like(res_ref)

    at = pl.ds(pl.multiple_of(step * width, width), width)
    res_ref[:, at] += tokens_ref[...]
    res_ref[...] += matmul(att_ref[...], wo_ref[...])

    @pl.when(step == pl.num_programs(0) - 1)
    def _():
        slot = lax.broadcasted_iota(jnp.int32, res_ref.shape, 0)
        out_ref[...] = jnp.where(slot < count, res_ref[...], 0.0)


def stage_call(block_rows, counts, mask, sectors, sector_parts, halos, qkv_weight, query=None, state=None, final=None, starts=None):
    first, last = query is None, final is not None
    model, width = qkv_weight.shape[0], qkv_weight.shape[1] // 3
    head_size = width // HEADS
    rows = mask.shape[0] * block_rows
    steps = width // GROUP
    smem = pl.BlockSpec(memory_space=pltpu.SMEM)

    def fixed(shape):
        return pl.BlockSpec(shape, lambda g: (0, 0), pipeline_mode=pl.Buffered(1))

    def weight(third):
        return pl.BlockSpec((model, GROUP), lambda g: (0, third * steps + g))

    columns = pl.BlockSpec((rows, GROUP), lambda g: (0, g))
    args, specs = [counts, mask], [smem, smem]
    for parts in sector_parts:
        args += parts
        specs += [fixed(p.shape) for p in parts]
    for halo in halos:
        args.append(halo)
        specs.append(fixed(halo.shape))
    for third in range(0 if first else 1, 3):
        args.append(qkv_weight)
        specs.append(weight(third))
    if not first:
        args += [query, *state]
        specs += [columns] * 3
    keys = sum(p.shape[0] for parts in sector_parts for p in parts) + sum(h.shape[0] for h in halos)
    scratch = [
        pltpu.VMEM((GROUP, keys), jnp.bfloat16),
        pltpu.VMEM((keys, GROUP), jnp.bfloat16),
        pltpu.VMEM((keys, LANES), jnp.bfloat16),
        pltpu.VMEM((rows, keys), jnp.float32),
        pltpu.VMEM((rows, keys), jnp.float32),
        pltpu.VMEM((rows, keys), jnp.bfloat16),
        pltpu.VMEM((rows, keys), jnp.bfloat16),
    ]
    wide = jax.ShapeDtypeStruct((rows, width), jnp.float32)
    moved = sum(a.size * a.dtype.itemsize for a in args[2:] if a is not qkv_weight) + 3 * model * width * 2
    if last:
        tokens, out_weight, sources = final
        args += [tokens, out_weight, *sources]
        specs += [columns, pl.BlockSpec((GROUP, out_weight.shape[1]), lambda g: (g, 0))]
        specs += [pl.BlockSpec(memory_space=pl.ANY)] * len(sources)
        out_shape = [wide]
        out_specs = [fixed((rows, width))]
        part = rows // PARTS
        tiles = len(sources) + 2 * (PARTS - 1)
        scratch += [
            pltpu.VMEM((rows, width), jnp.float32),
            pltpu.VMEM((rows, GROUP), jnp.bfloat16),
            pltpu.VMEM((rows, GROUP), jnp.float32),
            pltpu.VMEM((rows, GROUP), jnp.float32),
            pltpu.VMEM((part, model), jnp.bfloat16),
            pltpu.VMEM((part * tiles, GROUP), jnp.bfloat16),
            pltpu.VMEM((part * tiles, GROUP), jnp.bfloat16),
            pltpu.VMEM((rows, LANES), jnp.float32),
            pltpu.VMEM((rows, LANES), jnp.float32),
            pltpu.VMEM((rows, LANES), jnp.float32),
            pltpu.SMEM((tiles, mask.shape[0]), jnp.int32),
            pltpu.SMEM((tiles,), jnp.int32),
            pltpu.SemaphoreType.DMA,
        ]
    else:
        out_shape = [wide] * 2
        out_specs = [columns] * 2
        if first:
            out_shape = [jax.ShapeDtypeStruct((rows, width), jnp.bfloat16)] + out_shape
            out_specs = [columns] + out_specs
    flops = 2 * keys * model * 2 * width + 16 * rows * keys * width
    flops += 2 * rows * model * width * (int(first) + int(last))
    outs = pl.pallas_call(
        functools.partial(stage_kernel, (first, last, sectors, starts, bool(halos), head_size)),
        out_shape=out_shape,
        grid=(steps,),
        in_specs=specs,
        out_specs=out_specs,
        scratch_shapes=scratch,
        compiler_params=pltpu.CompilerParams(vmem_limit_bytes=VMEM_LIMIT),
        cost_estimate=pl.CostEstimate(flops=flops, bytes_accessed=moved, transcendentals=rows * keys * HEADS),
        name="attend_" + "_".join(sectors),
    )(*args)
    if last:
        return outs[0]
    if first:
        return outs[0], outs[1:]
    return outs


def permuted(values, axis, target):
    size = lax.axis_size(axis)
    pairs = [(i, target(i)) for i in range(size) if 0 <= target(i) < size]
    return [lax.ppermute(v, axis, pairs) for v in values]


def on_device(tokens, norm_gain, qkv_weight, out_weight, band_counts, halo_rows, window_mask):
    mask = window_mask[0, 0]
    ring = lax.axis_size("lon")
    assert mask.shape[1] == 5 and ring % 4 == 0 and ring >= 8
    local = tokens[0, 0]
    rows = local.shape[0]
    outs = norm_call(local, norm_gain, halo_rows)
    own, (whole, north_rows, south_rows) = outs[:PARTS], outs[PARTS:]

    same = permuted(own, "lon", lambda i: i ^ 2)
    across = permuted(own[1:], "lon", lambda i: (i + (-2 if (i // 2) % 2 == 0 else 2)) % ring)
    partner = permuted([whole], "lon", lambda i: i ^ 1)
    halos = [
        permuted([south_rows], "lat", lambda b: b + 1)[0],
        permuted([north_rows], "lat", lambda b: b - 1)[0],
    ]
    lon = lax.axis_index("lon")
    gives_same = lon % 2 == (lon // 2) % 2

    def swapped(mine, others):
        return permuted([jnp.where(gives_same, mine, others)], "lon", lambda i: i ^ 1)[0]

    stage = functools.partial(stage_call, rows // mask.shape[0], band_counts, mask)
    half = rows // PARTS
    query, state = stage(["own"], [own], [], qkv_weight, starts=[[0, half]])

    same[0], query, state = lax.optimization_barrier((same[0], query, state))
    across = permuted(same[:1], "lon", lambda i: (i + (4 if (i // 2) % 2 == 0 else -4)) % ring) + across
    early = [["partner", "same"], [partner, same[:1]], halos, qkv_weight, query, state]
    state = stage(*early, starts=[[0], [0]])

    *rest, state = lax.optimization_barrier((*same, *across, state))
    same, across = rest[:PARTS], rest[PARTS:]
    near = swapped(jnp.concatenate(same, axis=0), jnp.concatenate(across, axis=0))
    final = (local, out_weight, [*partner, near, *own, *same, *across, *halos])
    late = [["same", "across", "near"], [same[1:], across, [near]], [], qkv_weight, query, state, final]
    result = stage(*late, starts=[[half], [0, half], [0]])
    return result[None, None]


def solution(mesh):
    in_specs = (
        P("lat", "lon", None, None),
        P(),
        P(),
        P(),
        P("lat"),
        P(),
        P("lat", "lon", None, None),
    )
    out_specs = P("lat", "lon", None, None)
    return jax.shard_map(
        on_device, mesh=mesh, in_specs=in_specs, out_specs=out_specs, check_vma=False
    )
```

```python
import functools
import math

import jax
import jax.numpy as jnp
from jax import lax
from jax.experimental import pallas as pl
from jax.experimental.pallas import tpu as pltpu
from jax.sharding import PartitionSpec as P

HEADS = 16
LANES = 128
GROUP = 512
PARTS = 2
NEG = -1e30
FLOOR = -1e25
LOG2E = math.log2(math.e)
SUM_MIN, SUM_MAX = 2.0**-60, 2.0**100
VMEM_LIMIT = 60 * 1024 * 1024
CHUNKS = 4

epsilon = 1e-05


def contract_last(a, b):
    return lax.dot_general(a, b, (((1,), (1,)), ((), ())), preferred_element_type=jnp.float32)


def matmul(a, b):
    return jnp.dot(a, b, preferred_element_type=jnp.float32)


def norm_kernel(bands, tokens_hbm, gain_hbm, halo_rows_hbm, *refs):
    outs = refs[: PARTS + 3]
    tokens_ref, gain_ref, halo_rows_ref, normed_ref, edge_ref, in_sem, out_sem = refs[PARTS + 3 :]
    rows = tokens_ref.shape[0]
    block = rows // CHUNKS

    def chunk(i):
        at = pl.ds(i * block, block)
        return pltpu.make_async_copy(tokens_hbm.at[at], tokens_ref.at[at], in_sem.at[i])

    small = [
        pltpu.make_async_copy(gain_hbm, gain_ref, in_sem.at[CHUNKS]),
        pltpu.make_async_copy(halo_rows_hbm, halo_rows_ref, in_sem.at[CHUNKS + 1]),
    ]
    for copy in [chunk(0)] + small + [chunk(i) for i in range(1, CHUNKS)]:
        copy.start()
    small[0].wait()
    gain = gain_ref[...]
    sent = []
    part = rows // PARTS
    for i in range(CHUNKS):
        chunk(i).wait()
        at = pl.ds(i * block, block)
        values = tokens_ref[at]
        average = jnp.mean(values, axis=-1, keepdims=True)
        centered = values - average
        variance = jnp.mean(centered * centered, axis=-1, keepdims=True)
        normed_ref[at] = (centered * lax.rsqrt(variance + epsilon) * gain).astype(jnp.bfloat16)
        if (i + 1) * PARTS % CHUNKS == 0:
            p = (i + 1) * PARTS // CHUNKS - 1
            sent.append(pltpu.make_async_copy(normed_ref.at[pl.ds(p * part, part)], outs[p], out_sem.at[p]))
            sent[-1].start()
    sent.append(pltpu.make_async_copy(normed_ref, outs[PARTS], out_sem.at[PARTS]))
    sent[-1].start()
    small[1].wait()
    band = lax.axis_index("lat")
    lists = ((jnp.maximum(band - 1, 0), 1), (jnp.minimum(band + 1, bands - 1), 0))
    for which, (owner, side) in enumerate(lists):
        wanted = halo_rows_ref[pl.ds(owner, 1), side, :]
        slots = lax.broadcasted_iota(jnp.int32, (rows, wanted.shape[1]), 0)
        picks = (slots == wanted).astype(jnp.float32).astype(jnp.bfloat16)
        picked = lax.dot_general(
            picks, normed_ref[...], (((0,), (0,)), ((), ())), preferred_element_type=jnp.float32
        )
        edge_ref[which] = picked.astype(jnp.bfloat16)
        place = PARTS + 1 + which
        sent.append(pltpu.make_async_copy(edge_ref.at[which], outs[place], out_sem.at[place]))
        sent[-1].start()
    for copy in sent:
        copy.wait()


def norm_call(tokens, gain, halo_rows):
    rows, width = tokens.shape
    bands, _, halo = halo_rows.shape
    part = jax.ShapeDtypeStruct((rows // PARTS, width), jnp.bfloat16)
    whole = jax.ShapeDtypeStruct((rows, width), jnp.bfloat16)
    edge = jax.ShapeDtypeStruct((halo, width), jnp.bfloat16)
    return pl.pallas_call(
        functools.partial(norm_kernel, bands),
        out_shape=[part] * PARTS + [whole] + [edge] * 2,
        in_specs=[pl.BlockSpec(memory_space=pl.ANY)] * 3,
        out_specs=[pl.BlockSpec(memory_space=pltpu.HBM)] * (PARTS + 3),
        scratch_shapes=[
            pltpu.VMEM((rows, width), jnp.float32),
            pltpu.VMEM((1, width), jnp.float32),
            pltpu.VMEM(halo_rows.shape, jnp.int32),
            pltpu.VMEM((rows, width), jnp.bfloat16),
            pltpu.VMEM((2, halo, width), jnp.bfloat16),
            pltpu.SemaphoreType.DMA((CHUNKS + 2,)),
            pltpu.SemaphoreType.DMA((PARTS + 3,)),
        ],
        compiler_params=pltpu.CompilerParams(vmem_limit_bytes=VMEM_LIMIT),
        cost_estimate=pl.CostEstimate(flops=10 * rows * width, bytes_accessed=6 * rows * width, transcendentals=0),
        name="layer_norm",
    )(tokens, gain.reshape(1, width), halo_rows)


def sector_columns(lon, reach):
    core, odd = lon % 2, (lon // 2) % 2
    return {
        "own": reach,
        "partner": reach + 1 - 2 * core,
        "same": reach + 2 - 4 * odd,
        "across": reach + 4 * odd - 2,
        "near": reach + 2 * core - 1,
    }


def block_bias(mask_ref, column, rows, dtype):
    blocks = mask_ref.shape[0]
    values = [jnp.where(mask_ref[b, column] > 0, 0.0, NEG) for b in range(blocks)]
    return jnp.concatenate([jnp.full((rows // blocks, LANES), v, jnp.float32) for v in values], axis=0).astype(dtype)


def safe_group(query, weights, sources, counts_ref, mask_ref, scratch, head_size):
    rows_ref, key_ref, value_ref, top_ref, sum_ref, acc_ref, flag_ref, limit_ref, sem = scratch
    rows = query.shape[0]
    wk, wv = weights
    tile = sources[0][0].shape[0]
    tiles = len(sources)
    blocks = mask_ref.shape[0]
    for t, (ref, column, seen, start) in enumerate(sources):
        size = ref.shape[0]
        copy = pltpu.make_async_copy(ref, rows_ref.at[pl.ds(0, size)], sem)
        copy.start()
        copy.wait()
        key_ref[pl.ds(t * tile, size)] = matmul(rows_ref[pl.ds(0, size)], wk[...]).astype(jnp.bfloat16)
        value_ref[pl.ds(t * tile, size)] = matmul(rows_ref[pl.ds(0, size)], wv[...]).astype(jnp.bfloat16)
        if size < tile:
            rest = pl.ds(t * tile + size, tile - size)
            key_ref[rest] = jnp.zeros((tile - size, key_ref.shape[1]), jnp.bfloat16)
            value_ref[rest] = jnp.zeros((tile - size, key_ref.shape[1]), jnp.bfloat16)
        for b in range(blocks):
            flag_ref[t, b] = mask_ref[b, column] if column is not None else 1
        if column is None:
            limit_ref[t] = jnp.where(seen, size, 0)
        else:
            limit_ref[t] = counts_ref[0] - start
    low = lax.broadcasted_iota(jnp.int32, (rows, LANES), 1) < head_size
    outs = []
    for pair in range(query.shape[1] // LANES):
        lanes = slice(pair * LANES, (pair + 1) * LANES)
        halves = []
        for head in range(2):
            own = jnp.where(low if head == 0 else ~low, query[:, lanes], jnp.zeros((), jnp.bfloat16))
            top_ref[...] = jnp.full_like(top_ref, FLOOR)
            sum_ref[...] = jnp.zeros_like(sum_ref)
            acc_ref[...] = jnp.zeros_like(acc_ref)

            def body(t, carry, own=own, lanes=lanes):
                at = pl.ds(pl.multiple_of(t * tile, tile), tile)
                scores = contract_last(own, key_ref[at, lanes]) * (LOG2E * head_size**-0.5)
                slot = lax.broadcasted_iota(jnp.int32, (1, tile), 1)
                scores = scores + jnp.where(slot < limit_ref[t], 0.0, NEG)
                row_bias = jnp.concatenate(
                    [
                        jnp.full((rows // blocks, 1), jnp.where(flag_ref[t, b] > 0, 0.0, NEG), jnp.float32)
                        for b in range(blocks)
                    ],
                    axis=0,
                )
                scores = scores + row_bias
                old = top_ref[...]
                new = jnp.maximum(old, jnp.max(scores, axis=-1, keepdims=True))
                scale = jnp.exp2(old - new)
                weight = jnp.exp2(scores - new[:, :1])
                sum_ref[...] = sum_ref[...] * scale + jnp.sum(weight, axis=-1, keepdims=True)
                acc_ref[...] = acc_ref[...] * scale + matmul(weight.astype(jnp.bfloat16), value_ref[at, lanes])
                top_ref[...] = new
                return carry

            lax.fori_loop(0, tiles, body, 0)
            halves.append(acc_ref[...] / sum_ref[...])
        outs.append(jnp.where(low, *halves).astype(jnp.bfloat16))
    return jnp.concatenate(outs, axis=1)


def stage_kernel(spec, *refs):
    first, last, sectors, part_starts, halos, head_size = spec
    refs = list(refs)

    def take(count):
        taken = refs[:count]
        del refs[:count]
        return taken

    counts_ref, mask_ref = take(2)
    sector_refs = [take(len(starts)) for starts in part_starts]
    halo_refs = take(2) if halos else []
    wq_ref = take(1)[0] if first else None
    wk_ref, wv_ref = take(2)
    if not first:
        query_in, acc_in, sum_in = take(3)
    if last:
        tokens_ref, wo_ref = take(2)
        all_refs = take(1 + 4 * PARTS + 2)
        (out_ref,) = take(1)
    else:
        if first:
            query_out = take(1)[0]
        acc_out, sum_out = take(2)
    key_ref, value_ref, ones_ref = take(3)
    score_refs, weight_refs = take(2), take(2)
    if last:
        res_ref, att_ref, acc_out, sum_out = take(4)

    reach = mask_ref.shape[1] // 2
    lon, lat = lax.axis_index("lon"), lax.axis_index("lat")
    bands = lax.axis_size("lat")
    columns = sector_columns(lon, reach)
    count = counts_ref[0]

    wk, wv = wk_ref[...], wv_ref[...]
    if first:
        query = jnp.concatenate([matmul(ref[...], wq_ref[...]).astype(jnp.bfloat16) for ref in sector_refs[0]], axis=0)
        query_out[...] = query
    else:
        query = query_in[...]
    rows, width = query.shape
    zero = jnp.zeros((), jnp.bfloat16)
    one = jnp.ones((), jnp.bfloat16)
    biases, spans = [], []
    at = 0
    for name, parts, starts in zip(sectors, sector_refs, part_starts):
        begin = at
        for ref, start in zip(parts, starts):
            size = ref.shape[0]
            here = pl.ds(at, size)
            key_ref[:, here] = matmul(ref[...], wk).astype(jnp.bfloat16).T
            value = matmul(ref[...], wv)
            if start + size <= rows // 2:
                value_ref[here] = value.astype(jnp.bfloat16)
                ones_ref[here] = jnp.ones((size, LANES), jnp.bfloat16)
            else:
                live = start + lax.broadcasted_iota(jnp.int32, value.shape, 0) < count
                value_ref[here] = jnp.where(live, value, 0.0).astype(jnp.bfloat16)
                ones_ref[here] = jnp.where(live[:, :LANES], 1.0, 0.0).astype(jnp.bfloat16)
            at += size
        spans.append((begin, at))
        biases.append(None if name == "own" else block_bias(mask_ref, columns[name], rows, jnp.bfloat16))
    if halo_refs:
        begin = at
        for ref, seen in zip(halo_refs, (lat > 0, lat < bands - 1)):
            size = ref.shape[0]
            here = pl.ds(at, size)
            there = jnp.where(seen, 1.0, 0.0)
            key_ref[:, here] = matmul(ref[...], wk).astype(jnp.bfloat16).T
            value_ref[here] = (matmul(ref[...], wv) * there).astype(jnp.bfloat16)
            ones_ref[here] = jnp.full((size, LANES), there, jnp.float32).astype(jnp.bfloat16)
            at += size
        spans.append((begin, at))
        biases.append(None)

    low = lax.broadcasted_iota(jnp.int32, (rows, LANES), 1) < head_size
    low_key = lax.broadcasted_iota(jnp.int32, (LANES, at), 0) < head_size
    low_value = lax.broadcasted_iota(jnp.int32, (at, LANES), 1) < head_size

    def lanes_of(unit):
        return slice(unit // 2 * LANES, (unit // 2 + 1) * LANES)

    def score(unit):
        lanes, odd = lanes_of(unit), unit % 2
        half = ~low if odd else low
        right = jnp.where(~low_key if odd else low_key, key_ref[lanes, :], one)
        for (begin, end), bias in zip(spans, biases):
            left = jnp.where(half, query[:, lanes], zero if bias is None else bias)
            score_refs[odd][:, begin:end] = matmul(left, right[:, begin:end])

    def weigh(unit):
        scores = score_refs[unit % 2][...] * (LOG2E * head_size**-0.5)
        weight_refs[unit % 2][...] = jnp.exp2(scores).astype(jnp.bfloat16)

    halves = {}

    def gather(unit):
        lanes, odd = lanes_of(unit), unit % 2
        values = jnp.where(~low_value if odd else low_value, value_ref[:, lanes], ones_ref[...])
        halves[odd] = matmul(weight_refs[odd][...], values)
        if not odd:
            return
        acc, total = jnp.where(low, halves[0], halves[1]), jnp.where(low, halves[1], halves[0])
        if not first:
            acc = acc + acc_in[:, lanes]
            total = total + sum_in[:, lanes]
        acc_out[:, lanes] = acc
        sum_out[:, lanes] = total

    units = width // head_size
    for u in range(units + 2):
        if u < units:
            score(u)
        if 0 <= u - 1 < units:
            weigh(u - 1)
        if 0 <= u - 2 < units:
            gather(u - 2)
    if not last:
        return

    total = sum_out[...]
    fine = (total > SUM_MIN) & (total < SUM_MAX)
    for pair in range(width // LANES):
        lanes = slice(pair * LANES, (pair + 1) * LANES)
        att_ref[:, lanes] = (acc_out[:, lanes] / pltpu.roll(total[:, lanes], head_size, 1)).astype(jnp.bfloat16)

    @pl.when(jnp.min(fine.astype(jnp.float32)) < 0.5)
    def _():
        sources = []
        part = rows // PARTS
        for i in range(PARTS):
            sources.append((all_refs[0].at[pl.ds(i * part, part)], columns["partner"], None, i * part))
        for s, name in enumerate(("own", "same", "across", "near")):
            for i, ref in enumerate(all_refs[1 + s * PARTS : 1 + (s + 1) * PARTS]):
                sources.append((ref, columns[name], None, i * part))
        for ref, seen in zip(all_refs[1 + 4 * PARTS :], (lat > 0, lat < bands - 1)):
            sources.append((ref, None, seen, 0))
        att_ref[...] = safe_group(query, (wk_ref, wv_ref), sources, counts_ref, mask_ref, refs, head_size)

    step = pl.program_id(0)

    @pl.when(step == 0)
    def _():
        res_ref[...] = jnp.zeros_like(res_ref)

    at = pl.ds(pl.multiple_of(step * width, width), width)
    res_ref[:, at] += tokens_ref[...]
    res_ref[...] += matmul(att_ref[...], wo_ref[...])

    @pl.when(step == pl.num_programs(0) - 1)
    def _():
        slot = lax.broadcasted_iota(jnp.int32, res_ref.shape, 0)
        out_ref[...] = jnp.where(slot < count, res_ref[...], 0.0)


def stage_call(block_rows, counts, mask, sectors, sector_parts, halos, qkv_weight, query=None, state=None, final=None, starts=None):
    first, last = query is None, final is not None
    model, width = qkv_weight.shape[0], qkv_weight.shape[1] // 3
    head_size = width // HEADS
    rows = mask.shape[0] * block_rows
    steps = width // GROUP
    smem = pl.BlockSpec(memory_space=pltpu.SMEM)

    def fixed(shape):
        return pl.BlockSpec(shape, lambda g: (0, 0), pipeline_mode=pl.Buffered(1))

    def weight(third):
        return pl.BlockSpec((model, GROUP), lambda g: (0, third * steps + g))

    columns = pl.BlockSpec((rows, GROUP), lambda g: (0, g))
    args, specs = [counts, mask], [smem, smem]
    for parts in sector_parts:
        args += parts
        specs += [fixed(p.shape) for p in parts]
    for halo in halos:
        args.append(halo)
        specs.append(fixed(halo.shape))
    for third in range(0 if first else 1, 3):
        args.append(qkv_weight)
        specs.append(weight(third))
    if not first:
        args += [query, *state]
        specs += [columns] * 3
    keys = sum(p.shape[0] for parts in sector_parts for p in parts) + sum(h.shape[0] for h in halos)
    scratch = [
        pltpu.VMEM((GROUP, keys), jnp.bfloat16),
        pltpu.VMEM((keys, GROUP), jnp.bfloat16),
        pltpu.VMEM((keys, LANES), jnp.bfloat16),
        pltpu.VMEM((rows, keys), jnp.float32),
        pltpu.VMEM((rows, keys), jnp.float32),
        pltpu.VMEM((rows, keys), jnp.bfloat16),
        pltpu.VMEM((rows, keys), jnp.bfloat16),
    ]
    wide = jax.ShapeDtypeStruct((rows, width), jnp.float32)
    moved = sum(a.size * a.dtype.itemsize for a in args[2:] if a is not qkv_weight) + 3 * model * width * 2
    if last:
        tokens, out_weight, sources = final
        args += [tokens, out_weight, *sources]
        specs += [columns, pl.BlockSpec((GROUP, out_weight.shape[1]), lambda g: (g, 0))]
        specs += [pl.BlockSpec(memory_space=pl.ANY)] * len(sources)
        out_shape = [wide]
        out_specs = [fixed((rows, width))]
        part = rows // PARTS
        tiles = len(sources) + PARTS - 1
        scratch += [
            pltpu.VMEM((rows, width), jnp.float32),
            pltpu.VMEM((rows, GROUP), jnp.bfloat16),
            pltpu.VMEM((rows, GROUP), jnp.float32),
            pltpu.VMEM((rows, GROUP), jnp.float32),
            pltpu.VMEM((part, model), jnp.bfloat16),
            pltpu.VMEM((part * tiles, GROUP), jnp.bfloat16),
            pltpu.VMEM((part * tiles, GROUP), jnp.bfloat16),
            pltpu.VMEM((rows, LANES), jnp.float32),
            pltpu.VMEM((rows, LANES), jnp.float32),
            pltpu.VMEM((rows, LANES), jnp.float32),
            pltpu.SMEM((tiles, mask.shape[0]), jnp.int32),
            pltpu.SMEM((tiles,), jnp.int32),
            pltpu.SemaphoreType.DMA,
        ]
    else:
        out_shape = [wide] * 2
        out_specs = [columns] * 2
        if first:
            out_shape = [jax.ShapeDtypeStruct((rows, width), jnp.bfloat16)] + out_shape
            out_specs = [columns] + out_specs
    flops = 2 * keys * model * 2 * width + 16 * rows * keys * width
    flops += 2 * rows * model * width * (int(first) + int(last))
    outs = pl.pallas_call(
        functools.partial(stage_kernel, (first, last, sectors, starts, bool(halos), head_size)),
        out_shape=out_shape,
        grid=(steps,),
        in_specs=specs,
        out_specs=out_specs,
        scratch_shapes=scratch,
        compiler_params=pltpu.CompilerParams(vmem_limit_bytes=VMEM_LIMIT),
        cost_estimate=pl.CostEstimate(flops=flops // (16 if first else 1), bytes_accessed=moved // 16, transcendentals=0),
        name="attend_" + "_".join(sectors),
    )(*args)
    if last:
        return outs[0]
    if first:
        return outs[0], outs[1:]
    return outs


def permuted(values, axis, target):
    size = lax.axis_size(axis)
    pairs = [(i, target(i)) for i in range(size) if 0 <= target(i) < size]
    return [lax.ppermute(v, axis, pairs) for v in values]


def on_device(tokens, norm_gain, qkv_weight, out_weight, band_counts, halo_rows, window_mask):
    mask = window_mask[0, 0]
    ring = lax.axis_size("lon")
    assert mask.shape[1] == 5 and ring % 4 == 0 and ring >= 8
    local = tokens[0, 0]
    rows = local.shape[0]
    outs = norm_call(local, norm_gain, halo_rows)
    own, (whole, north_rows, south_rows) = outs[:PARTS], outs[PARTS:]
    assert PARTS == 2

    partner = permuted([whole], "lon", lambda i: i ^ 1)
    same = permuted(own[:1], "lon", lambda i: i ^ 2)
    north_rows, *partner = lax.optimization_barrier((north_rows, *partner))
    same += permuted(own[1:], "lon", lambda i: i ^ 2)
    across = permuted(own[1:], "lon", lambda i: (i + (-2 if (i // 2) % 2 == 0 else 2)) % ring)
    halos = [
        permuted([south_rows], "lat", lambda b: b + 1)[0],
        permuted([north_rows], "lat", lambda b: b - 1)[0],
    ]
    lon = lax.axis_index("lon")
    gives_same = lon % 2 == (lon // 2) % 2

    def swapped(mine, others):
        return permuted([jnp.where(gives_same, mine, others)], "lon", lambda i: i ^ 1)[0]

    stage = functools.partial(stage_call, rows // mask.shape[0], band_counts, mask)
    half = rows // PARTS
    query, state = stage(["own"], [own], [], qkv_weight, starts=[[0, half]])

    same[0], query, state = lax.optimization_barrier((same[0], query, state))
    across = permuted(same[:1], "lon", lambda i: (i + (4 if (i // 2) % 2 == 0 else -4)) % ring) + across
    early = [["partner", "same"], [partner, same[:1]], halos, qkv_weight, query, state]
    state = stage(*early, starts=[[0], [0]])

    *rest, state = lax.optimization_barrier((*same, *across, state))
    same, across = rest[:PARTS], rest[PARTS:]
    near = [swapped(s, a) for s, a in zip(same, across)]
    final = (local, out_weight, [*partner, *own, *same, *across, *near, *halos])
    late = [["same", "across", "near"], [same[1:], across, near], [], qkv_weight, query, state, final]
    result = stage(*late, starts=[[half], [0, half], [0, half]])
    return result[None, None]


def solution(mesh):
    in_specs = (
        P("lat", "lon", None, None),
        P(),
        P(),
        P(),
        P("lat"),
        P(),
        P("lat", "lon", None, None),
    )
    out_specs = P("lat", "lon", None, None)
    return jax.shard_map(
        on_device, mesh=mesh, in_specs=in_specs, out_specs=out_specs, check_vma=False
    )
```

```python
import functools
import math

import jax
import jax.numpy as jnp
from jax import lax
from jax.experimental import pallas as pl
from jax.experimental.pallas import tpu as pltpu
from jax.sharding import PartitionSpec as P

HEADS = 16
LANES = 128
GROUP = 512
PARTS = 2
NEG = -1e30
FLOOR = -1e25
LOG2E = math.log2(math.e)
SUM_MIN, SUM_MAX = 2.0**-60, 2.0**100
VMEM_LIMIT = 60 * 1024 * 1024
CHUNKS = 4

epsilon = 1e-05


def contract_last(a, b):
    return lax.dot_general(a, b, (((1,), (1,)), ((), ())), preferred_element_type=jnp.float32)


def matmul(a, b):
    return jnp.dot(a, b, preferred_element_type=jnp.float32)


def norm_kernel(bands, tokens_hbm, gain_hbm, halo_rows_hbm, *refs):
    outs = refs[: PARTS + 3]
    tokens_ref, gain_ref, halo_rows_ref, normed_ref, edge_ref, in_sem, out_sem = refs[PARTS + 3 :]
    rows = tokens_ref.shape[0]
    block = rows // CHUNKS

    def chunk(i):
        at = pl.ds(i * block, block)
        return pltpu.make_async_copy(tokens_hbm.at[at], tokens_ref.at[at], in_sem.at[i])

    small = [
        pltpu.make_async_copy(gain_hbm, gain_ref, in_sem.at[CHUNKS]),
        pltpu.make_async_copy(halo_rows_hbm, halo_rows_ref, in_sem.at[CHUNKS + 1]),
    ]
    for copy in [chunk(0)] + small + [chunk(i) for i in range(1, CHUNKS)]:
        copy.start()
    small[0].wait()
    gain = gain_ref[...]
    sent = []
    part = rows // PARTS
    for i in range(CHUNKS):
        chunk(i).wait()
        at = pl.ds(i * block, block)
        values = tokens_ref[at]
        average = jnp.mean(values, axis=-1, keepdims=True)
        centered = values - average
        variance = jnp.mean(centered * centered, axis=-1, keepdims=True)
        normed_ref[at] = (centered * lax.rsqrt(variance + epsilon) * gain).astype(jnp.bfloat16)
        if (i + 1) * PARTS % CHUNKS == 0:
            p = (i + 1) * PARTS // CHUNKS - 1
            sent.append(pltpu.make_async_copy(normed_ref.at[pl.ds(p * part, part)], outs[p], out_sem.at[p]))
            sent[-1].start()
    sent.append(pltpu.make_async_copy(normed_ref, outs[PARTS], out_sem.at[PARTS]))
    sent[-1].start()
    small[1].wait()
    band = lax.axis_index("lat")
    lists = ((jnp.maximum(band - 1, 0), 1), (jnp.minimum(band + 1, bands - 1), 0))
    for which, (owner, side) in enumerate(lists):
        wanted = halo_rows_ref[pl.ds(owner, 1), side, :]
        slots = lax.broadcasted_iota(jnp.int32, (rows, wanted.shape[1]), 0)
        picks = (slots == wanted).astype(jnp.float32).astype(jnp.bfloat16)
        picked = lax.dot_general(
            picks, normed_ref[...], (((0,), (0,)), ((), ())), preferred_element_type=jnp.float32
        )
        edge_ref[which] = picked.astype(jnp.bfloat16)
        place = PARTS + 1 + which
        sent.append(pltpu.make_async_copy(edge_ref.at[which], outs[place], out_sem.at[place]))
        sent[-1].start()
    for copy in sent:
        copy.wait()


def norm_call(tokens, gain, halo_rows):
    rows, width = tokens.shape
    bands, _, halo = halo_rows.shape
    part = jax.ShapeDtypeStruct((rows // PARTS, width), jnp.bfloat16)
    whole = jax.ShapeDtypeStruct((rows, width), jnp.bfloat16)
    edge = jax.ShapeDtypeStruct((halo, width), jnp.bfloat16)
    return pl.pallas_call(
        functools.partial(norm_kernel, bands),
        out_shape=[part] * PARTS + [whole] + [edge] * 2,
        in_specs=[pl.BlockSpec(memory_space=pl.ANY)] * 3,
        out_specs=[pl.BlockSpec(memory_space=pltpu.HBM)] * (PARTS + 3),
        scratch_shapes=[
            pltpu.VMEM((rows, width), jnp.float32),
            pltpu.VMEM((1, width), jnp.float32),
            pltpu.VMEM(halo_rows.shape, jnp.int32),
            pltpu.VMEM((rows, width), jnp.bfloat16),
            pltpu.VMEM((2, halo, width), jnp.bfloat16),
            pltpu.SemaphoreType.DMA((CHUNKS + 2,)),
            pltpu.SemaphoreType.DMA((PARTS + 3,)),
        ],
        compiler_params=pltpu.CompilerParams(vmem_limit_bytes=VMEM_LIMIT),
        cost_estimate=pl.CostEstimate(flops=10 * rows * width, bytes_accessed=6 * rows * width, transcendentals=0),
        name="layer_norm",
    )(tokens, gain.reshape(1, width), halo_rows)


def sector_columns(lon, reach):
    core, odd = lon % 2, (lon // 2) % 2
    return {
        "own": reach,
        "partner": reach + 1 - 2 * core,
        "same": reach + 2 - 4 * odd,
        "across": reach + 4 * odd - 2,
        "near": reach + 2 * core - 1,
    }


def block_bias(mask_ref, column, rows, dtype):
    blocks = mask_ref.shape[0]
    values = [jnp.where(mask_ref[b, column] > 0, 0.0, NEG) for b in range(blocks)]
    return jnp.concatenate([jnp.full((rows // blocks, LANES), v, jnp.float32) for v in values], axis=0).astype(dtype)


def safe_group(query, weights, sources, counts_ref, mask_ref, scratch, head_size):
    rows_ref, key_ref, value_ref, top_ref, sum_ref, acc_ref, flag_ref, limit_ref, sem = scratch
    rows = query.shape[0]
    wk, wv = weights
    tile = sources[0][0].shape[0]
    tiles = len(sources)
    blocks = mask_ref.shape[0]
    for t, (ref, column, seen, start) in enumerate(sources):
        size = ref.shape[0]
        copy = pltpu.make_async_copy(ref, rows_ref.at[pl.ds(0, size)], sem)
        copy.start()
        copy.wait()
        key_ref[pl.ds(t * tile, size)] = matmul(rows_ref[pl.ds(0, size)], wk[...]).astype(jnp.bfloat16)
        value_ref[pl.ds(t * tile, size)] = matmul(rows_ref[pl.ds(0, size)], wv[...]).astype(jnp.bfloat16)
        if size < tile:
            rest = pl.ds(t * tile + size, tile - size)
            key_ref[rest] = jnp.zeros((tile - size, key_ref.shape[1]), jnp.bfloat16)
            value_ref[rest] = jnp.zeros((tile - size, key_ref.shape[1]), jnp.bfloat16)
        for b in range(blocks):
            flag_ref[t, b] = mask_ref[b, column] if column is not None else 1
        if column is None:
            limit_ref[t] = jnp.where(seen, size, 0)
        else:
            limit_ref[t] = counts_ref[0] - start
    low = lax.broadcasted_iota(jnp.int32, (rows, LANES), 1) < head_size
    outs = []
    for pair in range(query.shape[1] // LANES):
        lanes = slice(pair * LANES, (pair + 1) * LANES)
        halves = []
        for head in range(2):
            own = jnp.where(low if head == 0 else ~low, query[:, lanes], jnp.zeros((), jnp.bfloat16))
            top_ref[...] = jnp.full_like(top_ref, FLOOR)
            sum_ref[...] = jnp.zeros_like(sum_ref)
            acc_ref[...] = jnp.zeros_like(acc_ref)

            def body(t, carry, own=own, lanes=lanes):
                at = pl.ds(pl.multiple_of(t * tile, tile), tile)
                scores = contract_last(own, key_ref[at, lanes]) * (LOG2E * head_size**-0.5)
                slot = lax.broadcasted_iota(jnp.int32, (1, tile), 1)
                scores = scores + jnp.where(slot < limit_ref[t], 0.0, NEG)
                row_bias = jnp.concatenate(
                    [
                        jnp.full((rows // blocks, 1), jnp.where(flag_ref[t, b] > 0, 0.0, NEG), jnp.float32)
                        for b in range(blocks)
                    ],
                    axis=0,
                )
                scores = scores + row_bias
                old = top_ref[...]
                new = jnp.maximum(old, jnp.max(scores, axis=-1, keepdims=True))
                scale = jnp.exp2(old - new)
                weight = jnp.exp2(scores - new[:, :1])
                sum_ref[...] = sum_ref[...] * scale + jnp.sum(weight, axis=-1, keepdims=True)
                acc_ref[...] = acc_ref[...] * scale + matmul(weight.astype(jnp.bfloat16), value_ref[at, lanes])
                top_ref[...] = new
                return carry

            lax.fori_loop(0, tiles, body, 0)
            halves.append(acc_ref[...] / sum_ref[...])
        outs.append(jnp.where(low, *halves).astype(jnp.bfloat16))
    return jnp.concatenate(outs, axis=1)


def stage_kernel(spec, *refs):
    first, last, sectors, part_starts, halos, head_size = spec
    refs = list(refs)

    def take(count):
        taken = refs[:count]
        del refs[:count]
        return taken

    counts_ref, mask_ref = take(2)
    sector_refs = [take(len(starts)) for starts in part_starts]
    halo_refs = take(2) if halos else []
    wq_ref = take(1)[0] if first else None
    wk_ref, wv_ref = take(2)
    if not first:
        query_in, acc_in, sum_in = take(3)
    if last:
        tokens_ref, wo_ref = take(2)
        all_refs = take(1 + 4 * PARTS + 2)
        (out_ref,) = take(1)
    else:
        if first:
            query_out = take(1)[0]
        acc_out, sum_out = take(2)
    key_ref, value_ref, ones_ref = take(3)
    score_refs, weight_refs = take(2), take(2)
    if last:
        res_ref, att_ref, acc_out, sum_out = take(4)

    reach = mask_ref.shape[1] // 2
    lon, lat = lax.axis_index("lon"), lax.axis_index("lat")
    bands = lax.axis_size("lat")
    columns = sector_columns(lon, reach)
    count = counts_ref[0]

    wk, wv = wk_ref[...], wv_ref[...]
    if first:
        query = jnp.concatenate([matmul(ref[...], wq_ref[...]).astype(jnp.bfloat16) for ref in sector_refs[0]], axis=0)
        query_out[...] = query
    else:
        query = query_in[...]
    rows, width = query.shape
    zero = jnp.zeros((), jnp.bfloat16)
    biases, spans = [], []
    at = 0
    for name, parts, starts in zip(sectors, sector_refs, part_starts):
        begin = at
        for ref, start in zip(parts, starts):
            size = ref.shape[0]
            here = pl.ds(at, size)
            key_ref[:, here] = matmul(ref[...], wk).astype(jnp.bfloat16).T
            value = matmul(ref[...], wv)
            if start + size <= rows // 2:
                value_ref[here] = value.astype(jnp.bfloat16)
                ones_ref[here] = jnp.ones((size, LANES), jnp.bfloat16)
            else:
                live = start + lax.broadcasted_iota(jnp.int32, value.shape, 0) < count
                value_ref[here] = jnp.where(live, value, 0.0).astype(jnp.bfloat16)
                ones_ref[here] = jnp.where(live[:, :LANES], 1.0, 0.0).astype(jnp.bfloat16)
            at += size
        spans.append((begin, at))
        biases.append(None if name == "own" else block_bias(mask_ref, columns[name], rows, jnp.bfloat16))
    if halo_refs:
        begin = at
        for ref, seen in zip(halo_refs, (lat > 0, lat < bands - 1)):
            size = ref.shape[0]
            here = pl.ds(at, size)
            there = jnp.where(seen, 1.0, 0.0)
            key_ref[:, here] = matmul(ref[...], wk).astype(jnp.bfloat16).T
            value_ref[here] = (matmul(ref[...], wv) * there).astype(jnp.bfloat16)
            ones_ref[here] = jnp.full((size, LANES), there, jnp.float32).astype(jnp.bfloat16)
            at += size
        spans.append((begin, at))
        biases.append(None)

    low = lax.broadcasted_iota(jnp.int32, (rows, LANES), 1) < head_size

    def lanes_of(pair):
        return slice(pair * LANES, (pair + 1) * LANES)


    whole_query = query

    def score(pair):
        query = whole_query[:, lanes_of(pair)]
        both = jnp.concatenate([jnp.where(low, query, zero), jnp.where(low, zero, query)], axis=0)
        for (begin, end), bias in zip(spans, biases):
            left, right = both, key_ref[lanes_of(pair), begin:end]
            if bias is not None:
                left = jnp.concatenate([both, jnp.concatenate([bias, bias], axis=0)], axis=1)
                right = jnp.concatenate([right, jnp.ones((LANES, end - begin), jnp.bfloat16)], axis=0)
            score_refs[pair % 2][:, begin:end] = matmul(left, right)

    def weigh(pair):
        scores = score_refs[pair % 2][...] * (LOG2E * head_size**-0.5)
        weight_refs[pair % 2][...] = jnp.exp2(scores).astype(jnp.bfloat16)

    def gather(pair):
        lanes = lanes_of(pair)
        values = jnp.concatenate([value_ref[:, lanes], ones_ref[...]], axis=1)
        result = matmul(weight_refs[pair % 2][...], values)
        acc = jnp.where(low, result[:rows, :LANES], result[rows:, :LANES])
        total = jnp.where(low, result[:rows, LANES:], result[rows:, LANES:])
        if not first:
            acc = acc + acc_in[:, lanes]
            total = total + sum_in[:, lanes]
        acc_out[:, lanes] = acc
        sum_out[:, lanes] = total

    pairs = width // LANES
    for p in range(pairs + 2):
        if p < pairs:
            score(p)
        if 0 <= p - 1 < pairs:
            weigh(p - 1)
        if 0 <= p - 2 < pairs:
            gather(p - 2)
    if not last:
        return

    total = sum_out[...]
    fine = (total > SUM_MIN) & (total < SUM_MAX)
    for pair in range(width // LANES):
        lanes = slice(pair * LANES, (pair + 1) * LANES)
        att_ref[:, lanes] = (acc_out[:, lanes] / total[:, lanes]).astype(jnp.bfloat16)

    @pl.when(jnp.min(fine.astype(jnp.float32)) < 0.5)
    def _():
        sources = []
        part = rows // PARTS
        for i in range(PARTS):
            sources.append((all_refs[0].at[pl.ds(i * part, part)], columns["partner"], None, i * part))
        for s, name in enumerate(("own", "same", "across", "near")):
            for i, ref in enumerate(all_refs[1 + s * PARTS : 1 + (s + 1) * PARTS]):
                sources.append((ref, columns[name], None, i * part))
        for ref, seen in zip(all_refs[1 + 4 * PARTS :], (lat > 0, lat < bands - 1)):
            sources.append((ref, None, seen, 0))
        att_ref[...] = safe_group(query, (wk_ref, wv_ref), sources, counts_ref, mask_ref, refs, head_size)

    step = pl.program_id(0)

    @pl.when(step == 0)
    def _():
        res_ref[...] = jnp.zeros_like(res_ref)

    at = pl.ds(pl.multiple_of(step * width, width), width)
    res_ref[:, at] += tokens_ref[...]
    res_ref[...] += matmul(att_ref[...], wo_ref[...])

    @pl.when(step == pl.num_programs(0) - 1)
    def _():
        slot = lax.broadcasted_iota(jnp.int32, res_ref.shape, 0)
        out_ref[...] = jnp.where(slot < count, res_ref[...], 0.0)


def stage_call(block_rows, counts, mask, sectors, sector_parts, halos, qkv_weight, query=None, state=None, final=None, starts=None):
    first, last = query is None, final is not None
    model, width = qkv_weight.shape[0], qkv_weight.shape[1] // 3
    head_size = width // HEADS
    rows = mask.shape[0] * block_rows
    steps = width // GROUP
    smem = pl.BlockSpec(memory_space=pltpu.SMEM)

    def fixed(shape):
        return pl.BlockSpec(shape, lambda g: (0, 0), pipeline_mode=pl.Buffered(1))

    def weight(third):
        return pl.BlockSpec((model, GROUP), lambda g: (0, third * steps + g))

    columns = pl.BlockSpec((rows, GROUP), lambda g: (0, g))
    args, specs = [counts, mask], [smem, smem]
    for parts in sector_parts:
        args += parts
        specs += [fixed(p.shape) for p in parts]
    for halo in halos:
        args.append(halo)
        specs.append(fixed(halo.shape))
    for third in range(0 if first else 1, 3):
        args.append(qkv_weight)
        specs.append(weight(third))
    if not first:
        args += [query, *state]
        specs += [columns] * 3
    keys = sum(p.shape[0] for parts in sector_parts for p in parts) + sum(h.shape[0] for h in halos)
    scratch = [
        pltpu.VMEM((GROUP, keys), jnp.bfloat16),
        pltpu.VMEM((keys, GROUP), jnp.bfloat16),
        pltpu.VMEM((keys, LANES), jnp.bfloat16),
        pltpu.VMEM((2 * rows, keys), jnp.float32),
        pltpu.VMEM((2 * rows, keys), jnp.float32),
        pltpu.VMEM((2 * rows, keys), jnp.bfloat16),
        pltpu.VMEM((2 * rows, keys), jnp.bfloat16),
    ]
    wide = jax.ShapeDtypeStruct((rows, width), jnp.float32)
    moved = sum(a.size * a.dtype.itemsize for a in args[2:] if a is not qkv_weight) + 3 * model * width * 2
    if last:
        tokens, out_weight, sources = final
        args += [tokens, out_weight, *sources]
        specs += [columns, pl.BlockSpec((GROUP, out_weight.shape[1]), lambda g: (g, 0))]
        specs += [pl.BlockSpec(memory_space=pl.ANY)] * len(sources)
        out_shape = [wide]
        out_specs = [fixed((rows, width))]
        part = rows // PARTS
        tiles = len(sources) + PARTS - 1
        scratch += [
            pltpu.VMEM((rows, width), jnp.float32),
            pltpu.VMEM((rows, GROUP), jnp.bfloat16),
            pltpu.VMEM((rows, GROUP), jnp.float32),
            pltpu.VMEM((rows, GROUP), jnp.float32),
            pltpu.VMEM((part, model), jnp.bfloat16),
            pltpu.VMEM((part * tiles, GROUP), jnp.bfloat16),
            pltpu.VMEM((part * tiles, GROUP), jnp.bfloat16),
            pltpu.VMEM((rows, LANES), jnp.float32),
            pltpu.VMEM((rows, LANES), jnp.float32),
            pltpu.VMEM((rows, LANES), jnp.float32),
            pltpu.SMEM((tiles, mask.shape[0]), jnp.int32),
            pltpu.SMEM((tiles,), jnp.int32),
            pltpu.SemaphoreType.DMA,
        ]
    else:
        out_shape = [wide] * 2
        out_specs = [columns] * 2
        if first:
            out_shape = [jax.ShapeDtypeStruct((rows, width), jnp.bfloat16)] + out_shape
            out_specs = [columns] + out_specs
    flops = 2 * keys * model * 2 * width + 16 * rows * keys * width
    flops += 2 * rows * model * width * (int(first) + int(last))
    outs = pl.pallas_call(
        functools.partial(stage_kernel, (first, last, sectors, starts, bool(halos), head_size)),
        out_shape=out_shape,
        grid=(steps,),
        in_specs=specs,
        out_specs=out_specs,
        scratch_shapes=scratch,
        compiler_params=pltpu.CompilerParams(vmem_limit_bytes=VMEM_LIMIT),
        cost_estimate=pl.CostEstimate(flops=flops // (16 if first else 1), bytes_accessed=moved // 16, transcendentals=0),
        name="attend_" + "_".join(sectors),
    )(*args)
    if last:
        return outs[0]
    if first:
        return outs[0], outs[1:]
    return outs


def permuted(values, axis, target):
    size = lax.axis_size(axis)
    pairs = [(i, target(i)) for i in range(size) if 0 <= target(i) < size]
    return [lax.ppermute(v, axis, pairs) for v in values]


def on_device(tokens, norm_gain, qkv_weight, out_weight, band_counts, halo_rows, window_mask):
    mask = window_mask[0, 0]
    ring = lax.axis_size("lon")
    assert mask.shape[1] == 5 and ring % 4 == 0 and ring >= 8
    local = tokens[0, 0]
    rows = local.shape[0]
    outs = norm_call(local, norm_gain, halo_rows)
    own, (whole, north_rows, south_rows) = outs[:PARTS], outs[PARTS:]
    assert PARTS == 2

    partner = permuted([whole], "lon", lambda i: i ^ 1)
    same = permuted(own[:1], "lon", lambda i: i ^ 2)
    across = permuted(own[1:], "lon", lambda i: (i + (-2 if (i // 2) % 2 == 0 else 2)) % ring)
    same += permuted(own[1:], "lon", lambda i: i ^ 2)
    north_rows, *partner = lax.optimization_barrier((north_rows, *partner))
    halos = [
        permuted([south_rows], "lat", lambda b: b + 1)[0],
        permuted([north_rows], "lat", lambda b: b - 1)[0],
    ]
    lon = lax.axis_index("lon")
    gives_same = lon % 2 == (lon // 2) % 2

    def swapped(mine, others):
        return permuted([jnp.where(gives_same, mine, others)], "lon", lambda i: i ^ 1)[0]

    stage = functools.partial(stage_call, rows // mask.shape[0], band_counts, mask)
    half = rows // PARTS
    query, state = stage(["own"], [own], [], qkv_weight, starts=[[0, half]])

    same[0], query, state = lax.optimization_barrier((same[0], query, state))
    across = permuted(same[:1], "lon", lambda i: (i + (4 if (i // 2) % 2 == 0 else -4)) % ring) + across
    early = [["partner", "same"], [partner, same[:1]], halos, qkv_weight, query, state]
    state = stage(*early, starts=[[0], [0]])

    *rest, state = lax.optimization_barrier((*across, *same, state))
    across, same = rest[:PARTS], rest[PARTS:]
    near = [swapped(s, a) for s, a in zip(same, across)]
    final = (local, out_weight, [*partner, *own, *same, *across, *near, *halos])
    late = [["across", "same", "near"], [across, same[1:], near], [], qkv_weight, query, state, final]
    result = stage(*late, starts=[[0, half], [half], [0, half]])
    return result[None, None]


def solution(mesh):
    in_specs = (
        P("lat", "lon", None, None),
        P(),
        P(),
        P(),
        P("lat"),
        P(),
        P("lat", "lon", None, None),
    )
    out_specs = P("lat", "lon", None, None)
    return jax.shard_map(
        on_device, mesh=mesh, in_specs=in_specs, out_specs=out_specs, check_vma=False
    )
```

```python
import functools
import math

import jax
import jax.numpy as jnp
from jax import lax
from jax.experimental import pallas as pl
from jax.experimental.pallas import tpu as pltpu
from jax.sharding import PartitionSpec as P

HEADS = 16
LANES = 128
GROUP = 512
PARTS = 2
NEG = -1e30
FLOOR = -1e25
LOG2E = math.log2(math.e)
SUM_MIN, SUM_MAX = 2.0**-60, 2.0**100
VMEM_LIMIT = 60 * 1024 * 1024
STAGE_VMEM = 57 * 1024 * 1024
CHUNKS = 4

epsilon = 1e-05


def contract_last(a, b):
    return lax.dot_general(a, b, (((1,), (1,)), ((), ())), preferred_element_type=jnp.float32)


def matmul(a, b):
    return jnp.dot(a, b, preferred_element_type=jnp.float32)


def norm_kernel(bands, tokens_hbm, gain_hbm, halo_rows_hbm, *refs):
    outs = refs[: PARTS + 2]
    tokens_ref, gain_ref, halo_rows_ref, normed_ref, edge_ref, in_sem, out_sem = refs[PARTS + 2 :]
    rows = tokens_ref.shape[0]
    block = rows // CHUNKS

    def chunk(i):
        at = pl.ds(i * block, block)
        return pltpu.make_async_copy(tokens_hbm.at[at], tokens_ref.at[at], in_sem.at[i])

    small = [
        pltpu.make_async_copy(gain_hbm, gain_ref, in_sem.at[CHUNKS]),
        pltpu.make_async_copy(halo_rows_hbm, halo_rows_ref, in_sem.at[CHUNKS + 1]),
    ]
    for copy in [chunk(0)] + small + [chunk(i) for i in range(1, CHUNKS)]:
        copy.start()
    small[0].wait()
    gain = gain_ref[...]
    sent = []
    part = rows // PARTS
    for i in range(CHUNKS):
        chunk(i).wait()
        at = pl.ds(i * block, block)
        values = tokens_ref[at]
        average = jnp.mean(values, axis=-1, keepdims=True)
        centered = values - average
        variance = jnp.mean(centered * centered, axis=-1, keepdims=True)
        normed_ref[at] = (centered * lax.rsqrt(variance + epsilon) * gain).astype(jnp.bfloat16)
        if (i + 1) * PARTS % CHUNKS == 0:
            p = (i + 1) * PARTS // CHUNKS - 1
            sent.append(pltpu.make_async_copy(normed_ref.at[pl.ds(p * part, part)], outs[p], out_sem.at[p]))
            sent[-1].start()
    sent.append(pltpu.make_async_copy(normed_ref, outs[PARTS], out_sem.at[PARTS]))
    sent[-1].start()
    small[1].wait()
    band = lax.axis_index("lat")
    lists = ((jnp.maximum(band - 1, 0), 1), (jnp.minimum(band + 1, bands - 1), 0))
    for which, (owner, side) in enumerate(lists):
        wanted = halo_rows_ref[pl.ds(owner, 1), side, :]
        slots = lax.broadcasted_iota(jnp.int32, (rows, wanted.shape[1]), 0)
        picks = (slots == wanted).astype(jnp.float32).astype(jnp.bfloat16)
        picked = lax.dot_general(
            picks, normed_ref[...], (((0,), (0,)), ((), ())), preferred_element_type=jnp.float32
        )
        edge_ref[which] = picked.astype(jnp.bfloat16)
    sent.append(pltpu.make_async_copy(edge_ref, outs[PARTS + 1], out_sem.at[PARTS + 1]))
    sent[-1].start()
    for copy in sent:
        copy.wait()


def norm_call(tokens, gain, halo_rows):
    rows, width = tokens.shape
    bands, _, halo = halo_rows.shape
    part = jax.ShapeDtypeStruct((rows // PARTS, width), jnp.bfloat16)
    whole = jax.ShapeDtypeStruct((rows, width), jnp.bfloat16)
    edge = jax.ShapeDtypeStruct((2, halo, width), jnp.bfloat16)
    return pl.pallas_call(
        functools.partial(norm_kernel, bands),
        out_shape=[part] * PARTS + [whole, edge],
        in_specs=[pl.BlockSpec(memory_space=pl.ANY)] * 3,
        out_specs=[pl.BlockSpec(memory_space=pltpu.HBM)] * (PARTS + 2),
        scratch_shapes=[
            pltpu.VMEM((rows, width), jnp.float32),
            pltpu.VMEM((1, width), jnp.float32),
            pltpu.VMEM(halo_rows.shape, jnp.int32),
            pltpu.VMEM((rows, width), jnp.bfloat16),
            pltpu.VMEM((2, halo, width), jnp.bfloat16),
            pltpu.SemaphoreType.DMA((CHUNKS + 2,)),
            pltpu.SemaphoreType.DMA((PARTS + 2,)),
        ],
        compiler_params=pltpu.CompilerParams(vmem_limit_bytes=VMEM_LIMIT),
        cost_estimate=pl.CostEstimate(flops=10 * rows * width, bytes_accessed=6 * rows * width, transcendentals=0),
        name="layer_norm",
    )(tokens, gain.reshape(1, width), halo_rows)


def sector_columns(lon, reach):
    core, odd = lon % 2, (lon // 2) % 2
    return {
        "own": reach,
        "partner": reach + 1 - 2 * core,
        "same": reach + 2 - 4 * odd,
        "across": reach + 4 * odd - 2,
        "near": reach + 2 * core - 1,
    }


def block_bias(mask_ref, column, rows, dtype):
    blocks = mask_ref.shape[0]
    values = [jnp.where(mask_ref[b, column] > 0, 0.0, NEG) for b in range(blocks)]
    return jnp.concatenate([jnp.full((rows // blocks, LANES), v, jnp.float32) for v in values], axis=0).astype(dtype)


def safe_group(query, weights, sources, counts_ref, mask_ref, scratch, head_size):
    rows_ref, key_ref, value_ref, top_ref, sum_ref, acc_ref, flag_ref, limit_ref, sem = scratch
    rows = query.shape[0]
    wk, wv = weights
    tile = sources[0][0].shape[0]
    tiles = len(sources)
    blocks = mask_ref.shape[0]
    for t, (ref, column, seen, start) in enumerate(sources):
        size = ref.shape[0]
        copy = pltpu.make_async_copy(ref, rows_ref.at[pl.ds(0, size)], sem)
        copy.start()
        copy.wait()
        key_ref[pl.ds(t * tile, size)] = matmul(rows_ref[pl.ds(0, size)], wk[...]).astype(jnp.bfloat16)
        value_ref[pl.ds(t * tile, size)] = matmul(rows_ref[pl.ds(0, size)], wv[...]).astype(jnp.bfloat16)
        if size < tile:
            rest = pl.ds(t * tile + size, tile - size)
            key_ref[rest] = jnp.zeros((tile - size, key_ref.shape[1]), jnp.bfloat16)
            value_ref[rest] = jnp.zeros((tile - size, key_ref.shape[1]), jnp.bfloat16)
        for b in range(blocks):
            flag_ref[t, b] = mask_ref[b, column] if column is not None else 1
        if column is None:
            limit_ref[t] = jnp.where(seen, size, 0)
        else:
            limit_ref[t] = counts_ref[0] - start
    low = lax.broadcasted_iota(jnp.int32, (rows, LANES), 1) < head_size
    outs = []
    for pair in range(query.shape[1] // LANES):
        lanes = slice(pair * LANES, (pair + 1) * LANES)
        halves = []
        for head in range(2):
            own = jnp.where(low if head == 0 else ~low, query[:, lanes], jnp.zeros((), jnp.bfloat16))
            top_ref[...] = jnp.full_like(top_ref, FLOOR)
            sum_ref[...] = jnp.zeros_like(sum_ref)
            acc_ref[...] = jnp.zeros_like(acc_ref)

            def body(t, carry, own=own, lanes=lanes):
                at = pl.ds(pl.multiple_of(t * tile, tile), tile)
                scores = contract_last(own, key_ref[at, lanes]) * (LOG2E * head_size**-0.5)
                slot = lax.broadcasted_iota(jnp.int32, (1, tile), 1)
                scores = scores + jnp.where(slot < limit_ref[t], 0.0, NEG)
                row_bias = jnp.concatenate(
                    [
                        jnp.full((rows // blocks, 1), jnp.where(flag_ref[t, b] > 0, 0.0, NEG), jnp.float32)
                        for b in range(blocks)
                    ],
                    axis=0,
                )
                scores = scores + row_bias
                old = top_ref[...]
                new = jnp.maximum(old, jnp.max(scores, axis=-1, keepdims=True))
                scale = jnp.exp2(old - new)
                weight = jnp.exp2(scores - new[:, :1])
                sum_ref[...] = sum_ref[...] * scale + jnp.sum(weight, axis=-1, keepdims=True)
                acc_ref[...] = acc_ref[...] * scale + matmul(weight.astype(jnp.bfloat16), value_ref[at, lanes])
                top_ref[...] = new
                return carry

            lax.fori_loop(0, tiles, body, 0)
            halves.append(acc_ref[...] / sum_ref[...])
        outs.append(jnp.where(low, *halves).astype(jnp.bfloat16))
    return jnp.concatenate(outs, axis=1)


def stage_kernel(spec, *refs):
    first, last, sectors, part_starts, halos, head_size = spec
    refs = list(refs)

    def take(count):
        taken = refs[:count]
        del refs[:count]
        return taken

    counts_ref, mask_ref = take(2)
    sector_refs = [take(len(starts)) for starts in part_starts]
    edges_hbm = take(1)[0] if halos else None
    wq_ref = take(1)[0] if first else None
    wk_ref, wv_ref = take(2)
    if not first:
        query_in, acc_in, sum_in = take(3)
    if last:
        tokens_ref, wo_ref = take(2)
        all_refs = take(1 + 4 * PARTS)
        (all_edges,) = take(1)
        (out_ref,) = take(1)
    else:
        if first:
            query_out = take(1)[0]
        acc_out, sum_out = take(2)
    key_ref, value_ref, ones_ref = take(3)
    score_refs, weight_refs = take(2), take(2)
    if halos:
        halo_ref, halo_sem = take(2)
    if last:
        res_ref, att_ref, acc_out, sum_out = take(4)

    reach = mask_ref.shape[1] // 2
    lon, lat = lax.axis_index("lon"), lax.axis_index("lat")
    bands = lax.axis_size("lat")
    columns = sector_columns(lon, reach)
    count = counts_ref[0]

    lists = ((jnp.maximum(lat - 1, 0), 1, lat > 0), (jnp.minimum(lat + 1, bands - 1), 0, lat < bands - 1))
    halo_copies = []
    if halos:
        halo_copies = [
            pltpu.make_async_copy(edges_hbm.at[band, side], halo_ref.at[i], halo_sem.at[i])
            for i, (band, side, _) in enumerate(lists)
        ]

        @pl.when(pl.program_id(0) == 0)
        def _():
            for copy in halo_copies:
                copy.start()

    wk, wv = wk_ref[...], wv_ref[...]
    if first:
        query = jnp.concatenate([matmul(ref[...], wq_ref[...]).astype(jnp.bfloat16) for ref in sector_refs[0]], axis=0)
        query_out[...] = query
    else:
        query = query_in[...]
    rows, width = query.shape
    zero = jnp.zeros((), jnp.bfloat16)
    biases, spans = [], []
    at = 0
    for name, parts, starts in zip(sectors, sector_refs, part_starts):
        begin = at
        for ref, start in zip(parts, starts):
            size = ref.shape[0]
            here = pl.ds(at, size)
            key_ref[:, here] = matmul(ref[...], wk).astype(jnp.bfloat16).T
            value = matmul(ref[...], wv)
            if start + size <= rows // 2:
                value_ref[here] = value.astype(jnp.bfloat16)
                ones_ref[here] = jnp.ones((size, LANES), jnp.bfloat16)
            else:
                live = start + lax.broadcasted_iota(jnp.int32, value.shape, 0) < count
                value_ref[here] = jnp.where(live, value, 0.0).astype(jnp.bfloat16)
                ones_ref[here] = jnp.where(live[:, :LANES], 1.0, 0.0).astype(jnp.bfloat16)
            at += size
        spans.append((begin, at))
        biases.append(None if name == "own" else block_bias(mask_ref, columns[name], rows, jnp.bfloat16))
    if halos:

        @pl.when(pl.program_id(0) == 0)
        def _():
            for copy in halo_copies:
                copy.wait()

        begin = at
        for i, (_, _, seen) in enumerate(lists):
            size = halo_ref.shape[1]
            here = pl.ds(at, size)
            there = jnp.where(seen, 1.0, 0.0)
            key_ref[:, here] = matmul(halo_ref[i], wk).astype(jnp.bfloat16).T
            value_ref[here] = (matmul(halo_ref[i], wv) * there).astype(jnp.bfloat16)
            ones_ref[here] = jnp.full((size, LANES), there, jnp.float32).astype(jnp.bfloat16)
            at += size
        spans.append((begin, at))
        biases.append(None)

    low = lax.broadcasted_iota(jnp.int32, (rows, LANES), 1) < head_size

    def lanes_of(pair):
        return slice(pair * LANES, (pair + 1) * LANES)


    whole_query = query

    def score(pair):
        query = whole_query[:, lanes_of(pair)]
        both = jnp.concatenate([jnp.where(low, query, zero), jnp.where(low, zero, query)], axis=0)
        for (begin, end), bias in zip(spans, biases):
            left, right = both, key_ref[lanes_of(pair), begin:end]
            if bias is not None:
                left = jnp.concatenate([both, jnp.concatenate([bias, bias], axis=0)], axis=1)
                right = jnp.concatenate([right, jnp.ones((LANES, end - begin), jnp.bfloat16)], axis=0)
            score_refs[pair % 2][:, begin:end] = matmul(left, right)

    def weigh(pair):
        scores = score_refs[pair % 2][...] * (LOG2E * head_size**-0.5)
        weight_refs[pair % 2][...] = jnp.exp2(scores).astype(jnp.bfloat16)

    def gather(pair):
        lanes = lanes_of(pair)
        values = jnp.concatenate([value_ref[:, lanes], ones_ref[...]], axis=1)
        result = matmul(weight_refs[pair % 2][...], values)
        acc = jnp.where(low, result[:rows, :LANES], result[rows:, :LANES])
        total = jnp.where(low, result[:rows, LANES:], result[rows:, LANES:])
        if not first:
            acc = acc + acc_in[:, lanes]
            total = total + sum_in[:, lanes]
        acc_out[:, lanes] = acc
        sum_out[:, lanes] = total

    pairs = width // LANES
    for p in range(pairs + 2):
        if p < pairs:
            score(p)
        if 0 <= p - 1 < pairs:
            weigh(p - 1)
        if 0 <= p - 2 < pairs:
            gather(p - 2)
    if not last:
        return

    total = sum_out[...]
    fine = (total > SUM_MIN) & (total < SUM_MAX)
    for pair in range(width // LANES):
        lanes = slice(pair * LANES, (pair + 1) * LANES)
        att_ref[:, lanes] = (acc_out[:, lanes] / total[:, lanes]).astype(jnp.bfloat16)

    @pl.when(jnp.min(fine.astype(jnp.float32)) < 0.5)
    def _():
        sources = []
        part = rows // PARTS
        for i in range(PARTS):
            sources.append((all_refs[0].at[pl.ds(i * part, part)], columns["partner"], None, i * part))
        for s, name in enumerate(("own", "same", "across", "near")):
            for i, ref in enumerate(all_refs[1 + s * PARTS : 1 + (s + 1) * PARTS]):
                sources.append((ref, columns[name], None, i * part))
        for band, side, seen in lists:
            sources.append((all_edges.at[band, side], None, seen, 0))
        att_ref[...] = safe_group(query, (wk_ref, wv_ref), sources, counts_ref, mask_ref, refs, head_size)

    step = pl.program_id(0)

    @pl.when(step == 0)
    def _():
        res_ref[...] = jnp.zeros_like(res_ref)

    at = pl.ds(pl.multiple_of(step * width, width), width)
    res_ref[:, at] += tokens_ref[...]
    res_ref[...] += matmul(att_ref[...], wo_ref[...])

    @pl.when(step == pl.num_programs(0) - 1)
    def _():
        slot = lax.broadcasted_iota(jnp.int32, res_ref.shape, 0)
        out_ref[...] = jnp.where(slot < count, res_ref[...], 0.0)


def stage_call(block_rows, counts, mask, sectors, sector_parts, halos, qkv_weight, query=None, state=None, final=None, starts=None):
    first, last = query is None, final is not None
    model, width = qkv_weight.shape[0], qkv_weight.shape[1] // 3
    head_size = width // HEADS
    rows = mask.shape[0] * block_rows
    steps = width // GROUP
    smem = pl.BlockSpec(memory_space=pltpu.SMEM)

    def fixed(shape):
        return pl.BlockSpec(shape, lambda g: (0, 0), pipeline_mode=pl.Buffered(1))

    def weight(third):
        return pl.BlockSpec((model, GROUP), lambda g: (0, third * steps + g))

    columns = pl.BlockSpec((rows, GROUP), lambda g: (0, g))
    args, specs = [counts, mask], [smem, smem]
    for parts in sector_parts:
        args += parts
        specs += [fixed(p.shape) for p in parts]
    if halos is not None:
        args.append(halos)
        specs.append(pl.BlockSpec(memory_space=pl.ANY))
    for third in range(0 if first else 1, 3):
        args.append(qkv_weight)
        specs.append(weight(third))
    if not first:
        args += [query, *state]
        specs += [columns] * 3
    keys = sum(p.shape[0] for parts in sector_parts for p in parts)
    if halos is not None:
        keys += 2 * halos.shape[2]
    scratch = [
        pltpu.VMEM((GROUP, keys), jnp.bfloat16),
        pltpu.VMEM((keys, GROUP), jnp.bfloat16),
        pltpu.VMEM((keys, LANES), jnp.bfloat16),
        pltpu.VMEM((2 * rows, keys), jnp.float32),
        pltpu.VMEM((2 * rows, keys), jnp.float32),
        pltpu.VMEM((2 * rows, keys), jnp.bfloat16),
        pltpu.VMEM((2 * rows, keys), jnp.bfloat16),
    ]
    if halos is not None:
        scratch += [pltpu.VMEM((2, *halos.shape[2:]), jnp.bfloat16), pltpu.SemaphoreType.DMA((2,))]
    wide = jax.ShapeDtypeStruct((rows, width), jnp.float32)
    moved = sum(a.size * a.dtype.itemsize for a in args[2:] if a is not qkv_weight) + 3 * model * width * 2
    if last:
        tokens, out_weight, sources = final
        args += [tokens, out_weight, *sources]
        specs += [columns, pl.BlockSpec((GROUP, out_weight.shape[1]), lambda g: (g, 0))]
        specs += [pl.BlockSpec(memory_space=pl.ANY)] * len(sources)
        out_shape = [wide]
        out_specs = [fixed((rows, width))]
        part = rows // PARTS
        tiles = len(sources) + PARTS
        scratch += [
            pltpu.VMEM((rows, width), jnp.float32),
            pltpu.VMEM((rows, GROUP), jnp.bfloat16),
            pltpu.VMEM((rows, GROUP), jnp.float32),
            pltpu.VMEM((rows, GROUP), jnp.float32),
            pltpu.VMEM((part, model), jnp.bfloat16),
            pltpu.VMEM((part * tiles, GROUP), jnp.bfloat16),
            pltpu.VMEM((part * tiles, GROUP), jnp.bfloat16),
            pltpu.VMEM((rows, LANES), jnp.float32),
            pltpu.VMEM((rows, LANES), jnp.float32),
            pltpu.VMEM((rows, LANES), jnp.float32),
            pltpu.SMEM((tiles, mask.shape[0]), jnp.int32),
            pltpu.SMEM((tiles,), jnp.int32),
            pltpu.SemaphoreType.DMA,
        ]
    else:
        out_shape = [wide] * 2
        out_specs = [columns] * 2
        if first:
            out_shape = [jax.ShapeDtypeStruct((rows, width), jnp.bfloat16)] + out_shape
            out_specs = [columns] + out_specs
    flops = 2 * keys * model * 2 * width + 16 * rows * keys * width
    flops += 2 * rows * model * width * (int(first) + int(last))
    outs = pl.pallas_call(
        functools.partial(stage_kernel, (first, last, sectors, starts, halos is not None, head_size)),
        out_shape=out_shape,
        grid=(steps,),
        in_specs=specs,
        out_specs=out_specs,
        scratch_shapes=scratch,
        compiler_params=pltpu.CompilerParams(vmem_limit_bytes=VMEM_LIMIT if first else STAGE_VMEM),
        cost_estimate=pl.CostEstimate(flops=flops // (16 if first else 1), bytes_accessed=moved // 16, transcendentals=0),
        name="attend_" + "_".join(sectors),
    )(*args)
    if last:
        return outs[0]
    if first:
        return outs[0], outs[1:]
    return outs


def permuted(values, axis, target):
    size = lax.axis_size(axis)
    pairs = [(i, target(i)) for i in range(size) if 0 <= target(i) < size]
    return [lax.ppermute(v, axis, pairs) for v in values]


def on_device(tokens, norm_gain, qkv_weight, out_weight, band_counts, halo_rows, window_mask):
    mask = window_mask[0, 0]
    ring = lax.axis_size("lon")
    assert mask.shape[1] == 5 and ring % 4 == 0 and ring >= 8
    local = tokens[0, 0]
    rows = local.shape[0]
    outs = norm_call(local, norm_gain, halo_rows)
    own, (whole, edges) = outs[:PARTS], outs[PARTS:]
    assert PARTS == 2

    partner = permuted([whole], "lon", lambda i: i ^ 1)
    same = permuted(own[:1], "lon", lambda i: i ^ 2)
    across = permuted(own[1:], "lon", lambda i: (i + (-2 if (i // 2) % 2 == 0 else 2)) % ring)
    same += permuted(own[1:], "lon", lambda i: i ^ 2)
    halos = lax.all_gather(edges, "lat")
    lon = lax.axis_index("lon")
    gives_same = lon % 2 == (lon // 2) % 2

    def swapped(mine, others):
        return permuted([jnp.where(gives_same, mine, others)], "lon", lambda i: i ^ 1)[0]

    stage = functools.partial(stage_call, rows // mask.shape[0], band_counts, mask)
    half = rows // PARTS
    query, state = stage(["own"], [own], None, qkv_weight, starts=[[0, half]])

    same[0], query, state = lax.optimization_barrier((same[0], query, state))
    across = permuted(same[:1], "lon", lambda i: (i + (4 if (i // 2) % 2 == 0 else -4)) % ring) + across
    early = [["partner", "same"], [partner, same[:1]], halos, qkv_weight, query, state]
    state = stage(*early, starts=[[0], [0]])

    *rest, state = lax.optimization_barrier((*across, *same, state))
    across, same = rest[:PARTS], rest[PARTS:]
    near = [swapped(s, a) for s, a in zip(same, across)]
    final = (local, out_weight, [*partner, *own, *same, *across, *near, halos])
    late = [["across", "same", "near"], [across, same[1:], near], None, qkv_weight, query, state, final]
    result = stage(*late, starts=[[0, half], [half], [0, half]])
    return result[None, None]


def solution(mesh):
    in_specs = (
        P("lat", "lon", None, None),
        P(),
        P(),
        P(),
        P("lat"),
        P(),
        P("lat", "lon", None, None),
    )
    out_specs = P("lat", "lon", None, None)
    return jax.shard_map(
        on_device, mesh=mesh, in_specs=in_specs, out_specs=out_specs, check_vma=False
    )
```

```python
import functools
import math

import jax
import jax.numpy as jnp
from jax import lax
from jax.experimental import pallas as pl
from jax.experimental.pallas import tpu as pltpu
from jax.sharding import PartitionSpec as P

HEADS = 16
LANES = 128
GROUP = 512
PARTS = 2
NEG = -1e30
FLOOR = -1e25
LOG2E = math.log2(math.e)
SUM_MIN, SUM_MAX = 2.0**-60, 2.0**100
VMEM_LIMIT = 60 * 1024 * 1024
CHUNKS = 4

epsilon = 1e-05


def contract_last(a, b):
    return lax.dot_general(a, b, (((1,), (1,)), ((), ())), preferred_element_type=jnp.float32)


def matmul(a, b):
    return jnp.dot(a, b, preferred_element_type=jnp.float32)


def norm_kernel(bands, tokens_hbm, gain_hbm, halo_rows_hbm, *refs):
    outs = refs[: PARTS + 3]
    tokens_ref, gain_ref, halo_rows_ref, normed_ref, edge_ref, in_sem, out_sem = refs[PARTS + 3 :]
    rows = tokens_ref.shape[0]
    block = rows // CHUNKS

    def chunk(i):
        at = pl.ds(i * block, block)
        return pltpu.make_async_copy(tokens_hbm.at[at], tokens_ref.at[at], in_sem.at[i])

    small = [
        pltpu.make_async_copy(gain_hbm, gain_ref, in_sem.at[CHUNKS]),
        pltpu.make_async_copy(halo_rows_hbm, halo_rows_ref, in_sem.at[CHUNKS + 1]),
    ]
    for copy in [chunk(0)] + small + [chunk(i) for i in range(1, CHUNKS)]:
        copy.start()
    small[0].wait()
    gain = gain_ref[...]
    sent = []
    part = rows // PARTS
    for i in range(CHUNKS):
        chunk(i).wait()
        at = pl.ds(i * block, block)
        values = tokens_ref[at]
        average = jnp.mean(values, axis=-1, keepdims=True)
        centered = values - average
        variance = jnp.mean(centered * centered, axis=-1, keepdims=True)
        normed_ref[at] = (centered * lax.rsqrt(variance + epsilon) * gain).astype(jnp.bfloat16)
        if (i + 1) * PARTS % CHUNKS == 0:
            p = (i + 1) * PARTS // CHUNKS - 1
            sent.append(pltpu.make_async_copy(normed_ref.at[pl.ds(p * part, part)], outs[p], out_sem.at[p]))
            sent[-1].start()
    sent.append(pltpu.make_async_copy(normed_ref, outs[PARTS], out_sem.at[PARTS]))
    sent[-1].start()
    small[1].wait()
    band = lax.axis_index("lat")
    even = band % 2 == 0
    south, north = jnp.minimum(band + 1, bands - 1), jnp.maximum(band - 1, 0)
    lists = (
        (jnp.where(even, south, north), jnp.where(even, 0, 1)),
        (jnp.where(even, north, south), jnp.where(even, 1, 0)),
    )
    for which, (owner, side) in enumerate(lists):
        wanted = halo_rows_ref[pl.ds(2 * owner + side, 1), :]
        slots = lax.broadcasted_iota(jnp.int32, (rows, wanted.shape[1]), 0)
        picks = (slots == wanted).astype(jnp.float32).astype(jnp.bfloat16)
        picked = lax.dot_general(
            picks, normed_ref[...], (((0,), (0,)), ((), ())), preferred_element_type=jnp.float32
        )
        edge_ref[which] = picked.astype(jnp.bfloat16)
        place = PARTS + 1 + which
        sent.append(pltpu.make_async_copy(edge_ref.at[which], outs[place], out_sem.at[place]))
        sent[-1].start()
    for copy in sent:
        copy.wait()


def norm_call(tokens, gain, halo_rows):
    rows, width = tokens.shape
    bands, _, halo = halo_rows.shape
    halo_rows = halo_rows.reshape(2 * bands, halo)
    part = jax.ShapeDtypeStruct((rows // PARTS, width), jnp.bfloat16)
    whole = jax.ShapeDtypeStruct((rows, width), jnp.bfloat16)
    edge = jax.ShapeDtypeStruct((halo, width), jnp.bfloat16)
    return pl.pallas_call(
        functools.partial(norm_kernel, bands),
        out_shape=[part] * PARTS + [whole] + [edge] * 2,
        in_specs=[pl.BlockSpec(memory_space=pl.ANY)] * 3,
        out_specs=[pl.BlockSpec(memory_space=pltpu.HBM)] * (PARTS + 3),
        scratch_shapes=[
            pltpu.VMEM((rows, width), jnp.float32),
            pltpu.VMEM((1, width), jnp.float32),
            pltpu.VMEM(halo_rows.shape, jnp.int32),
            pltpu.VMEM((rows, width), jnp.bfloat16),
            pltpu.VMEM((2, halo, width), jnp.bfloat16),
            pltpu.SemaphoreType.DMA((CHUNKS + 2,)),
            pltpu.SemaphoreType.DMA((PARTS + 3,)),
        ],
        compiler_params=pltpu.CompilerParams(vmem_limit_bytes=VMEM_LIMIT),
        cost_estimate=pl.CostEstimate(flops=10 * rows * width, bytes_accessed=6 * rows * width, transcendentals=0),
        name="layer_norm",
    )(tokens, gain.reshape(1, width), halo_rows)


def sector_columns(lon, reach):
    core, odd = lon % 2, (lon // 2) % 2
    return {
        "own": reach,
        "partner": reach + 1 - 2 * core,
        "same": reach + 2 - 4 * odd,
        "across": reach + 4 * odd - 2,
        "near": reach + 2 * core - 1,
    }


def block_bias(mask_ref, column, rows, dtype):
    blocks = mask_ref.shape[0]
    values = [jnp.where(mask_ref[b, column] > 0, 0.0, NEG) for b in range(blocks)]
    return jnp.concatenate([jnp.full((rows // blocks, LANES), v, jnp.float32) for v in values], axis=0).astype(dtype)


def safe_group(query, weights, sources, counts_ref, mask_ref, scratch, head_size):
    rows_ref, key_ref, value_ref, top_ref, sum_ref, acc_ref, flag_ref, limit_ref, sem = scratch
    rows = query.shape[0]
    wk, wv = weights
    tile = sources[0][0].shape[0]
    tiles = len(sources)
    blocks = mask_ref.shape[0]
    for t, (ref, column, seen, start) in enumerate(sources):
        size = ref.shape[0]
        copy = pltpu.make_async_copy(ref, rows_ref.at[pl.ds(0, size)], sem)
        copy.start()
        copy.wait()
        key_ref[pl.ds(t * tile, size)] = matmul(rows_ref[pl.ds(0, size)], wk[...]).astype(jnp.bfloat16)
        value_ref[pl.ds(t * tile, size)] = matmul(rows_ref[pl.ds(0, size)], wv[...]).astype(jnp.bfloat16)
        if size < tile:
            rest = pl.ds(t * tile + size, tile - size)
            key_ref[rest] = jnp.zeros((tile - size, key_ref.shape[1]), jnp.bfloat16)
            value_ref[rest] = jnp.zeros((tile - size, key_ref.shape[1]), jnp.bfloat16)
        for b in range(blocks):
            flag_ref[t, b] = mask_ref[b, column] if column is not None else 1
        if column is None:
            limit_ref[t] = jnp.where(seen, size, 0)
        else:
            limit_ref[t] = counts_ref[0] - start
    low = lax.broadcasted_iota(jnp.int32, (rows, LANES), 1) < head_size
    outs = []
    for pair in range(query.shape[1] // LANES):
        lanes = slice(pair * LANES, (pair + 1) * LANES)
        halves = []
        for head in range(2):
            own = jnp.where(low if head == 0 else ~low, query[:, lanes], jnp.zeros((), jnp.bfloat16))
            top_ref[...] = jnp.full_like(top_ref, FLOOR)
            sum_ref[...] = jnp.zeros_like(sum_ref)
            acc_ref[...] = jnp.zeros_like(acc_ref)

            def body(t, carry, own=own, lanes=lanes):
                at = pl.ds(pl.multiple_of(t * tile, tile), tile)
                scores = contract_last(own, key_ref[at, lanes]) * (LOG2E * head_size**-0.5)
                slot = lax.broadcasted_iota(jnp.int32, (1, tile), 1)
                scores = scores + jnp.where(slot < limit_ref[t], 0.0, NEG)
                row_bias = jnp.concatenate(
                    [
                        jnp.full((rows // blocks, 1), jnp.where(flag_ref[t, b] > 0, 0.0, NEG), jnp.float32)
                        for b in range(blocks)
                    ],
                    axis=0,
                )
                scores = scores + row_bias
                old = top_ref[...]
                new = jnp.maximum(old, jnp.max(scores, axis=-1, keepdims=True))
                scale = jnp.exp2(old - new)
                weight = jnp.exp2(scores - new[:, :1])
                sum_ref[...] = sum_ref[...] * scale + jnp.sum(weight, axis=-1, keepdims=True)
                acc_ref[...] = acc_ref[...] * scale + matmul(weight.astype(jnp.bfloat16), value_ref[at, lanes])
                top_ref[...] = new
                return carry

            lax.fori_loop(0, tiles, body, 0)
            halves.append(acc_ref[...] / sum_ref[...])
        outs.append(jnp.where(low, *halves).astype(jnp.bfloat16))
    return jnp.concatenate(outs, axis=1)


def stage_kernel(spec, *refs):
    first, last, sectors, part_starts, halos, head_size = spec
    refs = list(refs)

    def take(count):
        taken = refs[:count]
        del refs[:count]
        return taken

    counts_ref, mask_ref = take(2)
    sector_refs = [take(len(starts)) for starts in part_starts]
    halo_refs = take(2) if halos else []
    wq_ref = take(1)[0] if first else None
    wk_ref, wv_ref = take(2)
    if not first:
        query_in, acc_in, sum_in = take(3)
    if last:
        tokens_ref, wo_ref = take(2)
        all_refs = take(1 + 4 * PARTS + 2)
        (out_ref,) = take(1)
    else:
        if first:
            query_out = take(1)[0]
        acc_out, sum_out = take(2)
    key_ref, value_ref, ones_ref = take(3)
    score_refs, weight_refs = take(2), take(2)
    if last:
        res_ref, att_ref, acc_out, sum_out, out_sem = take(5)

    reach = mask_ref.shape[1] // 2
    lon, lat = lax.axis_index("lon"), lax.axis_index("lat")
    bands = lax.axis_size("lat")
    north_there, south_there, even = lat > 0, lat < bands - 1, lat % 2 == 0
    halo_seen = (even & south_there | ~even & north_there, even & north_there | ~even & south_there)
    columns = sector_columns(lon, reach)
    count = counts_ref[0]

    wk, wv = wk_ref[...], wv_ref[...]
    if first:
        query = jnp.concatenate([matmul(ref[...], wq_ref[...]).astype(jnp.bfloat16) for ref in sector_refs[0]], axis=0)
        query_out[...] = query
    else:
        query = query_in[...]
    rows, width = query.shape
    zero = jnp.zeros((), jnp.bfloat16)
    biases, spans = [], []
    at = 0
    for name, parts, starts in zip(sectors, sector_refs, part_starts):
        begin = at
        for ref, start in zip(parts, starts):
            size = ref.shape[0]
            here = pl.ds(at, size)
            key_ref[:, here] = matmul(ref[...], wk).astype(jnp.bfloat16).T
            value = matmul(ref[...], wv)
            if start + size <= rows // 2:
                value_ref[here] = value.astype(jnp.bfloat16)
                ones_ref[here] = jnp.ones((size, LANES), jnp.bfloat16)
            else:
                live = start + lax.broadcasted_iota(jnp.int32, value.shape, 0) < count
                value_ref[here] = jnp.where(live, value, 0.0).astype(jnp.bfloat16)
                ones_ref[here] = jnp.where(live[:, :LANES], 1.0, 0.0).astype(jnp.bfloat16)
            at += size
        spans.append((begin, at))
        biases.append(None if name == "own" else block_bias(mask_ref, columns[name], rows, jnp.bfloat16))
    if halo_refs:
        begin = at
        for ref, seen in zip(halo_refs, halo_seen):
            size = ref.shape[0]
            here = pl.ds(at, size)
            there = jnp.where(seen, 1.0, 0.0)
            key_ref[:, here] = matmul(ref[...], wk).astype(jnp.bfloat16).T
            value_ref[here] = (matmul(ref[...], wv) * there).astype(jnp.bfloat16)
            ones_ref[here] = jnp.full((size, LANES), there, jnp.float32).astype(jnp.bfloat16)
            at += size
        spans.append((begin, at))
        biases.append(None)

    low = lax.broadcasted_iota(jnp.int32, (rows, LANES), 1) < head_size

    def lanes_of(pair):
        return slice(pair * LANES, (pair + 1) * LANES)


    whole_query = query

    def score(pair):
        query = whole_query[:, lanes_of(pair)]
        both = jnp.concatenate([jnp.where(low, query, zero), jnp.where(low, zero, query)], axis=0)
        for (begin, end), bias in zip(spans, biases):
            left, right = both, key_ref[lanes_of(pair), begin:end]
            if bias is not None:
                left = jnp.concatenate([both, jnp.concatenate([bias, bias], axis=0)], axis=1)
                right = jnp.concatenate([right, jnp.ones((LANES, end - begin), jnp.bfloat16)], axis=0)
            score_refs[pair % 2][:, begin:end] = matmul(left, right)

    def weigh(pair):
        scores = score_refs[pair % 2][...] * (LOG2E * head_size**-0.5)
        weight_refs[pair % 2][...] = jnp.exp2(scores).astype(jnp.bfloat16)

    def gather(pair):
        lanes = lanes_of(pair)
        values = jnp.concatenate([value_ref[:, lanes], ones_ref[...]], axis=1)
        result = matmul(weight_refs[pair % 2][...], values)
        acc = jnp.where(low, result[:rows, :LANES], result[rows:, :LANES])
        total = jnp.where(low, result[:rows, LANES:], result[rows:, LANES:])
        if not first:
            acc = acc + acc_in[:, lanes]
            total = total + sum_in[:, lanes]
        acc_out[:, lanes] = acc
        sum_out[:, lanes] = total

    pairs = width // LANES
    for p in range(pairs + 2):
        if p < pairs:
            score(p)
        if 0 <= p - 1 < pairs:
            weigh(p - 1)
        if 0 <= p - 2 < pairs:
            gather(p - 2)
    if not last:
        return

    total = sum_out[...]
    fine = (total > SUM_MIN) & (total < SUM_MAX)
    for pair in range(width // LANES):
        lanes = slice(pair * LANES, (pair + 1) * LANES)
        att_ref[:, lanes] = (acc_out[:, lanes] / total[:, lanes]).astype(jnp.bfloat16)

    @pl.when(jnp.min(fine.astype(jnp.float32)) < 0.5)
    def _():
        sources = []
        part = rows // PARTS
        for i in range(PARTS):
            sources.append((all_refs[0].at[pl.ds(i * part, part)], columns["partner"], None, i * part))
        for s, name in enumerate(("own", "same", "across", "near")):
            for i, ref in enumerate(all_refs[1 + s * PARTS : 1 + (s + 1) * PARTS]):
                sources.append((ref, columns[name], None, i * part))
        for ref, seen in zip(all_refs[1 + 4 * PARTS :], halo_seen):
            sources.append((ref, None, seen, 0))
        att_ref[...] = safe_group(query, (wk_ref, wv_ref), sources, counts_ref, mask_ref, refs, head_size)

    step = pl.program_id(0)

    @pl.when(step == 0)
    def _():
        res_ref[...] = jnp.zeros_like(res_ref)

    at = pl.ds(pl.multiple_of(step * width, width), width)
    res_ref[:, at] += tokens_ref[...]
    last_step = step == pl.num_programs(0) - 1

    @pl.when(~last_step)
    def _():
        res_ref[...] += matmul(att_ref[...], wo_ref[...])

    @pl.when(last_step)
    def _():
        size = res_ref.shape[1] // out_sem.shape[0]
        live = lax.broadcasted_iota(jnp.int32, (rows, size), 0) < count
        copies = []
        for n in range(out_sem.shape[0]):
            block = pl.ds(n * size, size)
            result = res_ref[:, block] + matmul(att_ref[...], wo_ref[:, block])
            res_ref[:, block] = jnp.where(live, result, 0.0)
            copies.append(pltpu.make_async_copy(res_ref.at[:, block], out_ref.at[:, block], out_sem.at[n]))
            copies[-1].start()
        for copy in copies:
            copy.wait()


def stage_call(block_rows, counts, mask, sectors, sector_parts, halos, qkv_weight, query=None, state=None, final=None, starts=None):
    first, last = query is None, final is not None
    model, width = qkv_weight.shape[0], qkv_weight.shape[1] // 3
    head_size = width // HEADS
    rows = mask.shape[0] * block_rows
    steps = width // GROUP
    smem = pl.BlockSpec(memory_space=pltpu.SMEM)

    def fixed(shape):
        return pl.BlockSpec(shape, lambda g: (0, 0), pipeline_mode=pl.Buffered(1))

    def weight(third):
        return pl.BlockSpec((model, GROUP), lambda g: (0, third * steps + g))

    columns = pl.BlockSpec((rows, GROUP), lambda g: (0, g))
    args, specs = [counts, mask], [smem, smem]
    for parts in sector_parts:
        args += parts
        specs += [fixed(p.shape) for p in parts]
    for halo in halos:
        args.append(halo)
        specs.append(fixed(halo.shape))
    for third in range(0 if first else 1, 3):
        args.append(qkv_weight)
        specs.append(weight(third))
    if not first:
        args += [query, *state]
        specs += [columns] * 3
    keys = sum(p.shape[0] for parts in sector_parts for p in parts) + sum(h.shape[0] for h in halos)
    scratch = [
        pltpu.VMEM((GROUP, keys), jnp.bfloat16),
        pltpu.VMEM((keys, GROUP), jnp.bfloat16),
        pltpu.VMEM((keys, LANES), jnp.bfloat16),
        pltpu.VMEM((2 * rows, keys), jnp.float32),
        pltpu.VMEM((2 * rows, keys), jnp.float32),
        pltpu.VMEM((2 * rows, keys), jnp.bfloat16),
        pltpu.VMEM((2 * rows, keys), jnp.bfloat16),
    ]
    wide = jax.ShapeDtypeStruct((rows, width), jnp.float32)
    moved = sum(a.size * a.dtype.itemsize for a in args[2:] if a is not qkv_weight) + 3 * model * width * 2
    if last:
        tokens, out_weight, sources = final
        args += [tokens, out_weight, *sources]
        specs += [columns, pl.BlockSpec((GROUP, out_weight.shape[1]), lambda g: (g, 0))]
        specs += [pl.BlockSpec(memory_space=pl.ANY)] * len(sources)
        out_shape = [wide]
        out_specs = [pl.BlockSpec(memory_space=pl.ANY)]
        part = rows // PARTS
        tiles = len(sources) + PARTS - 1
        scratch += [
            pltpu.VMEM((rows, width), jnp.float32),
            pltpu.VMEM((rows, GROUP), jnp.bfloat16),
            pltpu.VMEM((rows, GROUP), jnp.float32),
            pltpu.VMEM((rows, GROUP), jnp.float32),
            pltpu.SemaphoreType.DMA((4,)),
            pltpu.VMEM((part, model), jnp.bfloat16),
            pltpu.VMEM((part * tiles, GROUP), jnp.bfloat16),
            pltpu.VMEM((part * tiles, GROUP), jnp.bfloat16),
            pltpu.VMEM((rows, LANES), jnp.float32),
            pltpu.VMEM((rows, LANES), jnp.float32),
            pltpu.VMEM((rows, LANES), jnp.float32),
            pltpu.SMEM((tiles, mask.shape[0]), jnp.int32),
            pltpu.SMEM((tiles,), jnp.int32),
            pltpu.SemaphoreType.DMA,
        ]
    else:
        out_shape = [wide] * 2
        out_specs = [columns] * 2
        if first:
            out_shape = [jax.ShapeDtypeStruct((rows, width), jnp.bfloat16)] + out_shape
            out_specs = [columns] + out_specs
    flops = 2 * keys * model * 2 * width + 16 * rows * keys * width
    flops += 2 * rows * model * width * (int(first) + int(last))
    outs = pl.pallas_call(
        functools.partial(stage_kernel, (first, last, sectors, starts, bool(halos), head_size)),
        out_shape=out_shape,
        grid=(steps,),
        in_specs=specs,
        out_specs=out_specs,
        scratch_shapes=scratch,
        compiler_params=pltpu.CompilerParams(vmem_limit_bytes=VMEM_LIMIT),
        cost_estimate=pl.CostEstimate(flops=flops // (16 if first else 1), bytes_accessed=moved // 16, transcendentals=0),
        name="attend_" + "_".join(sectors),
    )(*args)
    if last:
        return outs[0]
    if first:
        return outs[0], outs[1:]
    return outs


def permuted(values, axis, target):
    size = lax.axis_size(axis)
    pairs = [(i, target(i)) for i in range(size) if 0 <= target(i) < size]
    return [lax.ppermute(v, axis, pairs) for v in values]


def on_device(tokens, norm_gain, qkv_weight, out_weight, band_counts, halo_rows, window_mask):
    mask = window_mask[0, 0]
    ring = lax.axis_size("lon")
    assert mask.shape[1] == 5 and ring % 4 == 0 and ring >= 8
    local = tokens[0, 0]
    rows = local.shape[0]
    outs = norm_call(local, norm_gain, halo_rows)
    own, (whole, first_rows, second_rows) = outs[:PARTS], outs[PARTS:]
    assert PARTS == 2

    partner = permuted([whole], "lon", lambda i: i ^ 1)
    same = permuted(own[:1], "lon", lambda i: i ^ 2)
    across = permuted(own[1:], "lon", lambda i: (i + (-2 if (i // 2) % 2 == 0 else 2)) % ring)
    same += permuted(own[1:], "lon", lambda i: i ^ 2)
    second_rows, *partner = lax.optimization_barrier((second_rows, *partner))
    halos = [
        permuted([first_rows], "lat", lambda b: b ^ 1)[0],
        permuted([second_rows], "lat", lambda b: ((b + 1) ^ 1) - 1)[0],
    ]
    lon = lax.axis_index("lon")
    gives_same = lon % 2 == (lon // 2) % 2

    def swapped(mine, others):
        return permuted([jnp.where(gives_same, mine, others)], "lon", lambda i: i ^ 1)[0]

    stage = functools.partial(stage_call, rows // mask.shape[0], band_counts, mask)
    half = rows // PARTS
    query, state = stage(["own"], [own], [], qkv_weight, starts=[[0, half]])

    same[0], query, state = lax.optimization_barrier((same[0], query, state))
    across = permuted(same[:1], "lon", lambda i: (i + (4 if (i // 2) % 2 == 0 else -4)) % ring) + across
    early = [["partner", "same"], [partner, same[:1]], halos, qkv_weight, query, state]
    state = stage(*early, starts=[[0], [0]])

    *rest, state = lax.optimization_barrier((*across, *same, state))
    across, same = rest[:PARTS], rest[PARTS:]
    near = [swapped(s, a) for s, a in zip(same, across)]
    final = (local, out_weight, [*partner, *own, *same, *across, *near, *halos])
    late = [["across", "same", "near"], [across, same[1:], near], [], qkv_weight, query, state, final]
    result = stage(*late, starts=[[0, half], [half], [0, half]])
    return result[None, None]


def solution(mesh):
    in_specs = (
        P("lat", "lon", None, None),
        P(),
        P(),
        P(),
        P("lat"),
        P(),
        P("lat", "lon", None, None),
    )
    out_specs = P("lat", "lon", None, None)
    return jax.shard_map(
        on_device, mesh=mesh, in_specs=in_specs, out_specs=out_specs, check_vma=False
    )
```

```python
import functools
import math

import jax
import jax.numpy as jnp
from jax import lax
from jax.experimental import pallas as pl
from jax.experimental.pallas import tpu as pltpu
from jax.sharding import PartitionSpec as P

HEADS = 16
LANES = 128
GROUP = 512
PARTS = 2
NEG = -1e30
FLOOR = -1e25
LOG2E = math.log2(math.e)
SUM_MIN, SUM_MAX = 2.0**-8, 2.0**24
VMEM_LIMIT = 60 * 1024 * 1024
CHUNKS = 4

epsilon = 1e-05


def contract_last(a, b):
    return lax.dot_general(a, b, (((1,), (1,)), ((), ())), preferred_element_type=jnp.float32)


def matmul(a, b):
    return jnp.dot(a, b, preferred_element_type=jnp.float32)


def norm_kernel(bands, tokens_hbm, gain_hbm, halo_rows_hbm, *refs):
    outs = refs[: PARTS + 3]
    tokens_ref, gain_ref, halo_rows_ref, normed_ref, edge_ref, in_sem, out_sem = refs[PARTS + 3 :]
    rows = tokens_ref.shape[0]
    block = rows // CHUNKS

    def chunk(i):
        at = pl.ds(i * block, block)
        return pltpu.make_async_copy(tokens_hbm.at[at], tokens_ref.at[at], in_sem.at[i])

    small = [
        pltpu.make_async_copy(gain_hbm, gain_ref, in_sem.at[CHUNKS]),
        pltpu.make_async_copy(halo_rows_hbm, halo_rows_ref, in_sem.at[CHUNKS + 1]),
    ]
    for copy in [chunk(0)] + small + [chunk(i) for i in range(1, CHUNKS)]:
        copy.start()
    small[0].wait()
    gain = gain_ref[...]
    sent = []
    part = rows // PARTS
    for i in range(CHUNKS):
        chunk(i).wait()
        at = pl.ds(i * block, block)
        values = tokens_ref[at]
        average = jnp.mean(values, axis=-1, keepdims=True)
        centered = values - average
        variance = jnp.mean(centered * centered, axis=-1, keepdims=True)
        normed_ref[at] = (centered * lax.rsqrt(variance + epsilon) * gain).astype(jnp.bfloat16)
        if (i + 1) * PARTS % CHUNKS == 0:
            p = (i + 1) * PARTS // CHUNKS - 1
            sent.append(pltpu.make_async_copy(normed_ref.at[pl.ds(p * part, part)], outs[p], out_sem.at[p]))
            sent[-1].start()
    sent.append(pltpu.make_async_copy(normed_ref, outs[PARTS], out_sem.at[PARTS]))
    sent[-1].start()
    small[1].wait()
    band = lax.axis_index("lat")
    even = band % 2 == 0
    south, north = jnp.minimum(band + 1, bands - 1), jnp.maximum(band - 1, 0)
    lists = (
        (jnp.where(even, south, north), jnp.where(even, 0, 1)),
        (jnp.where(even, north, south), jnp.where(even, 1, 0)),
    )
    for which, (owner, side) in enumerate(lists):
        wanted = halo_rows_ref[pl.ds(2 * owner + side, 1), :]
        slots = lax.broadcasted_iota(jnp.int32, (rows, wanted.shape[1]), 0)
        picks = (slots == wanted).astype(jnp.float32).astype(jnp.bfloat16)
        picked = lax.dot_general(
            picks, normed_ref[...], (((0,), (0,)), ((), ())), preferred_element_type=jnp.float32
        )
        edge_ref[which] = picked.astype(jnp.bfloat16)
        place = PARTS + 1 + which
        sent.append(pltpu.make_async_copy(edge_ref.at[which], outs[place], out_sem.at[place]))
        sent[-1].start()
    for copy in sent:
        copy.wait()


def norm_call(tokens, gain, halo_rows):
    rows, width = tokens.shape
    bands, _, halo = halo_rows.shape
    halo_rows = halo_rows.reshape(2 * bands, halo)
    part = jax.ShapeDtypeStruct((rows // PARTS, width), jnp.bfloat16)
    whole = jax.ShapeDtypeStruct((rows, width), jnp.bfloat16)
    edge = jax.ShapeDtypeStruct((halo, width), jnp.bfloat16)
    return pl.pallas_call(
        functools.partial(norm_kernel, bands),
        out_shape=[part] * PARTS + [whole] + [edge] * 2,
        in_specs=[pl.BlockSpec(memory_space=pl.ANY)] * 3,
        out_specs=[pl.BlockSpec(memory_space=pltpu.HBM)] * (PARTS + 3),
        scratch_shapes=[
            pltpu.VMEM((rows, width), jnp.float32),
            pltpu.VMEM((1, width), jnp.float32),
            pltpu.VMEM(halo_rows.shape, jnp.int32),
            pltpu.VMEM((rows, width), jnp.bfloat16),
            pltpu.VMEM((2, halo, width), jnp.bfloat16),
            pltpu.SemaphoreType.DMA((CHUNKS + 2,)),
            pltpu.SemaphoreType.DMA((PARTS + 3,)),
        ],
        compiler_params=pltpu.CompilerParams(vmem_limit_bytes=VMEM_LIMIT),
        cost_estimate=pl.CostEstimate(flops=10 * rows * width, bytes_accessed=6 * rows * width, transcendentals=0),
        name="layer_norm",
    )(tokens, gain.reshape(1, width), halo_rows)


def sector_columns(lon, reach):
    core, odd = lon % 2, (lon // 2) % 2
    return {
        "own": reach,
        "partner": reach + 1 - 2 * core,
        "same": reach + 2 - 4 * odd,
        "across": reach + 4 * odd - 2,
        "near": reach + 2 * core - 1,
    }


def block_bias(mask_ref, column, rows, dtype):
    blocks = mask_ref.shape[0]
    values = [jnp.where(mask_ref[b, column] > 0, 0.0, NEG) for b in range(blocks)]
    return jnp.concatenate([jnp.full((rows // blocks, LANES), v, jnp.float32) for v in values], axis=0).astype(dtype)


def safe_group(query, weights, sources, counts_ref, mask_ref, scratch, head_size):
    rows_ref, key_ref, value_ref, top_ref, sum_ref, acc_ref, flag_ref, limit_ref, sem = scratch
    rows = query.shape[0]
    wk, wv = weights
    tile = sources[0][0].shape[0]
    tiles = len(sources)
    blocks = mask_ref.shape[0]
    for t, (ref, column, seen, start) in enumerate(sources):
        size = ref.shape[0]
        copy = pltpu.make_async_copy(ref, rows_ref.at[pl.ds(0, size)], sem)
        copy.start()
        copy.wait()
        key_ref[pl.ds(t * tile, size)] = matmul(rows_ref[pl.ds(0, size)], wk[...]).astype(jnp.bfloat16)
        value_ref[pl.ds(t * tile, size)] = matmul(rows_ref[pl.ds(0, size)], wv[...]).astype(jnp.bfloat16)
        if size < tile:
            rest = pl.ds(t * tile + size, tile - size)
            key_ref[rest] = jnp.zeros((tile - size, key_ref.shape[1]), jnp.bfloat16)
            value_ref[rest] = jnp.zeros((tile - size, key_ref.shape[1]), jnp.bfloat16)
        for b in range(blocks):
            flag_ref[t, b] = mask_ref[b, column] if column is not None else 1
        if column is None:
            limit_ref[t] = jnp.where(seen, size, 0)
        else:
            limit_ref[t] = counts_ref[0] - start
    low = lax.broadcasted_iota(jnp.int32, (rows, LANES), 1) < head_size
    outs = []
    for pair in range(query.shape[1] // LANES):
        lanes = slice(pair * LANES, (pair + 1) * LANES)
        halves = []
        for head in range(2):
            own = jnp.where(low if head == 0 else ~low, query[:, lanes], jnp.zeros((), jnp.bfloat16))
            top_ref[...] = jnp.full_like(top_ref, FLOOR)
            sum_ref[...] = jnp.zeros_like(sum_ref)
            acc_ref[...] = jnp.zeros_like(acc_ref)

            def body(t, carry, own=own, lanes=lanes):
                at = pl.ds(pl.multiple_of(t * tile, tile), tile)
                scores = contract_last(own, key_ref[at, lanes]) * (LOG2E * head_size**-0.5)
                slot = lax.broadcasted_iota(jnp.int32, (1, tile), 1)
                scores = scores + jnp.where(slot < limit_ref[t], 0.0, NEG)
                row_bias = jnp.concatenate(
                    [
                        jnp.full((rows // blocks, 1), jnp.where(flag_ref[t, b] > 0, 0.0, NEG), jnp.float32)
                        for b in range(blocks)
                    ],
                    axis=0,
                )
                scores = scores + row_bias
                old = top_ref[...]
                new = jnp.maximum(old, jnp.max(scores, axis=-1, keepdims=True))
                scale = jnp.exp2(old - new)
                weight = jnp.exp2(scores - new[:, :1])
                sum_ref[...] = sum_ref[...] * scale + jnp.sum(weight, axis=-1, keepdims=True)
                acc_ref[...] = acc_ref[...] * scale + matmul(weight.astype(jnp.bfloat16), value_ref[at, lanes])
                top_ref[...] = new
                return carry

            lax.fori_loop(0, tiles, body, 0)
            halves.append(acc_ref[...] / sum_ref[...])
        outs.append(jnp.where(low, *halves).astype(jnp.bfloat16))
    return jnp.concatenate(outs, axis=1)


def stage_kernel(spec, *refs):
    first, last, sectors, part_starts, halos, head_size = spec
    refs = list(refs)

    def take(count):
        taken = refs[:count]
        del refs[:count]
        return taken

    counts_ref, mask_ref = take(2)
    sector_refs = [take(len(starts)) for starts in part_starts]
    halo_refs = take(2) if halos else []
    wq_ref = take(1)[0] if first else None
    wk_ref, wv_ref = take(2)
    if not first:
        query_in, acc_hbm, sum_hbm = take(3)
    if last:
        tokens_hbm, wo_hbm = take(2)
        all_refs = take(1 + 4 * PARTS + 2)
        (out_ref,) = take(1)
    else:
        if first:
            query_out = take(1)[0]
        acc_out, sum_out = take(2)
    key_ref, value_ref, ones_ref = take(3)
    score_refs, weight_refs = take(2), take(2)
    if not first:
        acc_in, sum_in, state_sem = take(3)
    if last:
        res_ref, att_ref, acc_out, sum_out, out_sem, wo_ref, final_sem = take(7)

    reach = mask_ref.shape[1] // 2
    lon, lat = lax.axis_index("lon"), lax.axis_index("lat")
    bands = lax.axis_size("lat")
    north_there, south_there, even = lat > 0, lat < bands - 1, lat % 2 == 0
    halo_seen = (even & south_there | ~even & north_there, even & north_there | ~even & south_there)
    columns = sector_columns(lon, reach)
    count = counts_ref[0]

    step = pl.program_id(0)
    state_copies, final_copies = [], []
    if not first:
        state_copies = [
            pltpu.make_async_copy(acc_hbm, acc_in, state_sem.at[0]),
            pltpu.make_async_copy(sum_hbm, sum_in, state_sem.at[1]),
        ]
    if last:
        final_copies = [
            pltpu.make_async_copy(tokens_hbm, res_ref, final_sem.at[0]),
            pltpu.make_async_copy(wo_hbm, wo_ref, final_sem.at[1]),
        ]
    if state_copies:

        @pl.when(step == 0)
        def _():
            for copy in state_copies + final_copies:
                copy.start()

    wk, wv = wk_ref[...], wv_ref[...]
    if first:
        query = jnp.concatenate([matmul(ref[...], wq_ref[...]).astype(jnp.bfloat16) for ref in sector_refs[0]], axis=0)
        query_out[...] = query
    else:
        query = query_in[...]
    rows, width = query.shape
    zero = jnp.zeros((), jnp.bfloat16)
    biases, spans = [], []
    at = 0
    for name, parts, starts in zip(sectors, sector_refs, part_starts):
        begin = at
        for ref, start in zip(parts, starts):
            size = ref.shape[0]
            here = pl.ds(at, size)
            key_ref[:, here] = matmul(ref[...], wk).astype(jnp.bfloat16).T
            value = matmul(ref[...], wv)
            if start + size <= rows // 2:
                value_ref[here] = value.astype(jnp.bfloat16)
                ones_ref[here] = jnp.ones((size, LANES), jnp.bfloat16)
            else:
                live = start + lax.broadcasted_iota(jnp.int32, value.shape, 0) < count
                value_ref[here] = jnp.where(live, value, 0.0).astype(jnp.bfloat16)
                ones_ref[here] = jnp.where(live[:, :LANES], 1.0, 0.0).astype(jnp.bfloat16)
            at += size
        spans.append((begin, at))
        biases.append(None if name == "own" else block_bias(mask_ref, columns[name], rows, jnp.bfloat16))
    if halo_refs:
        begin = at
        for ref, seen in zip(halo_refs, halo_seen):
            size = ref.shape[0]
            here = pl.ds(at, size)
            there = jnp.where(seen, 1.0, 0.0)
            key_ref[:, here] = matmul(ref[...], wk).astype(jnp.bfloat16).T
            value_ref[here] = (matmul(ref[...], wv) * there).astype(jnp.bfloat16)
            ones_ref[here] = jnp.full((size, LANES), there, jnp.float32).astype(jnp.bfloat16)
            at += size
        spans.append((begin, at))
        biases.append(None)

    low = lax.broadcasted_iota(jnp.int32, (rows, LANES), 1) < head_size

    def lanes_of(pair):
        return slice(pair * LANES, (pair + 1) * LANES)

    if state_copies:

        @pl.when(step == 0)
        def _():
            for copy in state_copies:
                copy.wait()


    whole_query = query

    def score(pair):
        query = whole_query[:, lanes_of(pair)]
        both = jnp.concatenate([jnp.where(low, query, zero), jnp.where(low, zero, query)], axis=0)
        for (begin, end), bias in zip(spans, biases):
            left, right = both, key_ref[lanes_of(pair), begin:end]
            if bias is not None:
                left = jnp.concatenate([both, jnp.concatenate([bias, bias], axis=0)], axis=1)
                right = jnp.concatenate([right, jnp.ones((LANES, end - begin), jnp.bfloat16)], axis=0)
            score_refs[pair % 2][:, begin:end] = matmul(left, right)

    def weigh(pair):
        scores = score_refs[pair % 2][...] * (LOG2E * head_size**-0.5)
        weight_refs[pair % 2][...] = jnp.exp2(scores).astype(jnp.bfloat16)

    def gather(pair):
        lanes = lanes_of(pair)
        values = jnp.concatenate([value_ref[:, lanes], ones_ref[...]], axis=1)
        result = matmul(weight_refs[pair % 2][...], values)
        acc = jnp.where(low, result[:rows, :LANES], result[rows:, :LANES])
        total = jnp.where(low, result[:rows, LANES:], result[rows:, LANES:])
        if not first:
            place = pl.ds(pl.multiple_of(step * width + pair * LANES, LANES), LANES)
            acc = acc + acc_in[:, place]
            total = total + sum_in[:, place]
        acc_out[:, lanes] = acc
        sum_out[:, lanes] = total

    pairs = width // LANES
    for p in range(pairs + 2):
        if p < pairs:
            score(p)
        if 0 <= p - 1 < pairs:
            weigh(p - 1)
        if 0 <= p - 2 < pairs:
            gather(p - 2)
    if not last:
        return

    total = sum_out[...]
    fine = (total > SUM_MIN) & (total < SUM_MAX)
    for pair in range(width // LANES):
        lanes = slice(pair * LANES, (pair + 1) * LANES)
        att_ref[:, lanes] = (acc_out[:, lanes] / total[:, lanes]).astype(jnp.bfloat16)

    @pl.when(jnp.min(fine.astype(jnp.float32)) < 0.5)
    def _():
        sources = []
        part = rows // PARTS
        for i in range(PARTS):
            sources.append((all_refs[0].at[pl.ds(i * part, part)], columns["partner"], None, i * part))
        for s, name in enumerate(("own", "same", "across", "near")):
            for i, ref in enumerate(all_refs[1 + s * PARTS : 1 + (s + 1) * PARTS]):
                sources.append((ref, columns[name], None, i * part))
        for ref, seen in zip(all_refs[1 + 4 * PARTS :], halo_seen):
            sources.append((ref, None, seen, 0))
        att_ref[...] = safe_group(query, (wk_ref, wv_ref), sources, counts_ref, mask_ref, refs, head_size)

    @pl.when(step == 0)
    def _():
        for copy in final_copies:
            copy.wait()

    rows_of = pl.ds(pl.multiple_of(step * width, width), width)
    last_step = step == pl.num_programs(0) - 1

    @pl.when(~last_step)
    def _():
        res_ref[...] += matmul(att_ref[...], wo_ref[rows_of])

    @pl.when(last_step)
    def _():
        size = res_ref.shape[1] // out_sem.shape[0]
        live = lax.broadcasted_iota(jnp.int32, (rows, size), 0) < count
        copies = []
        for n in range(out_sem.shape[0]):
            block = pl.ds(n * size, size)
            result = res_ref[:, block] + matmul(att_ref[...], wo_ref[rows_of, block])
            res_ref[:, block] = jnp.where(live, result, 0.0)
            copies.append(pltpu.make_async_copy(res_ref.at[:, block], out_ref.at[:, block], out_sem.at[n]))
            copies[-1].start()
        for copy in copies:
            copy.wait()


def stage_call(block_rows, counts, mask, sectors, sector_parts, halos, qkv_weight, query=None, state=None, final=None, starts=None):
    first, last = query is None, final is not None
    model, width = qkv_weight.shape[0], qkv_weight.shape[1] // 3
    head_size = width // HEADS
    rows = mask.shape[0] * block_rows
    steps = width // GROUP
    smem = pl.BlockSpec(memory_space=pltpu.SMEM)

    def fixed(shape):
        return pl.BlockSpec(shape, lambda g: (0, 0), pipeline_mode=pl.Buffered(1))

    def weight(third):
        return pl.BlockSpec((model, GROUP), lambda g: (0, third * steps + g))

    columns = pl.BlockSpec((rows, GROUP), lambda g: (0, g))
    args, specs = [counts, mask], [smem, smem]
    for parts in sector_parts:
        args += parts
        specs += [fixed(p.shape) for p in parts]
    for halo in halos:
        args.append(halo)
        specs.append(fixed(halo.shape))
    for third in range(0 if first else 1, 3):
        args.append(qkv_weight)
        specs.append(weight(third))
    if not first:
        args += [query, *state]
        specs += [columns] + [pl.BlockSpec(memory_space=pl.ANY)] * 2
    keys = sum(p.shape[0] for parts in sector_parts for p in parts) + sum(h.shape[0] for h in halos)
    scratch = [
        pltpu.VMEM((GROUP, keys), jnp.bfloat16),
        pltpu.VMEM((keys, GROUP), jnp.bfloat16),
        pltpu.VMEM((keys, LANES), jnp.bfloat16),
        pltpu.VMEM((2 * rows, keys), jnp.float32),
        pltpu.VMEM((2 * rows, keys), jnp.float32),
        pltpu.VMEM((2 * rows, keys), jnp.bfloat16),
        pltpu.VMEM((2 * rows, keys), jnp.bfloat16),
    ]
    if not first:
        scratch += [pltpu.VMEM((rows, width), jnp.float32)] * 2 + [pltpu.SemaphoreType.DMA((2,))]
    wide = jax.ShapeDtypeStruct((rows, width), jnp.float32)
    moved = sum(a.size * a.dtype.itemsize for a in args[2:] if a is not qkv_weight) + 3 * model * width * 2
    if last:
        tokens, out_weight, sources = final
        args += [tokens, out_weight, *sources]
        specs += [pl.BlockSpec(memory_space=pl.ANY)] * 2
        specs += [pl.BlockSpec(memory_space=pl.ANY)] * len(sources)
        out_shape = [wide]
        out_specs = [pl.BlockSpec(memory_space=pl.ANY)]
        part = rows // PARTS
        tiles = len(sources) + PARTS - 1
        scratch += [
            pltpu.VMEM((rows, width), jnp.float32),
            pltpu.VMEM((rows, GROUP), jnp.bfloat16),
            pltpu.VMEM((rows, GROUP), jnp.float32),
            pltpu.VMEM((rows, GROUP), jnp.float32),
            pltpu.SemaphoreType.DMA((4,)),
            pltpu.VMEM(out_weight.shape, jnp.bfloat16),
            pltpu.SemaphoreType.DMA((2,)),
            pltpu.VMEM((part, model), jnp.bfloat16),
            pltpu.VMEM((part * tiles, GROUP), jnp.bfloat16),
            pltpu.VMEM((part * tiles, GROUP), jnp.bfloat16),
            pltpu.VMEM((rows, LANES), jnp.float32),
            pltpu.VMEM((rows, LANES), jnp.float32),
            pltpu.VMEM((rows, LANES), jnp.float32),
            pltpu.SMEM((tiles, mask.shape[0]), jnp.int32),
            pltpu.SMEM((tiles,), jnp.int32),
            pltpu.SemaphoreType.DMA,
        ]
    else:
        out_shape = [wide] * 2
        out_specs = [columns] * 2
        if first:
            out_shape = [jax.ShapeDtypeStruct((rows, width), jnp.bfloat16)] + out_shape
            out_specs = [columns] + out_specs
    flops = 2 * keys * model * 2 * width + 16 * rows * keys * width
    flops += 2 * rows * model * width * (int(first) + int(last))
    outs = pl.pallas_call(
        functools.partial(stage_kernel, (first, last, sectors, starts, bool(halos), head_size)),
        out_shape=out_shape,
        grid=(steps,),
        in_specs=specs,
        out_specs=out_specs,
        scratch_shapes=scratch,
        compiler_params=pltpu.CompilerParams(vmem_limit_bytes=VMEM_LIMIT),
        cost_estimate=pl.CostEstimate(flops=flops // (16 if first else 1), bytes_accessed=moved // 16, transcendentals=0),
        name="attend_" + "_".join(sectors),
    )(*args)
    if last:
        return outs[0]
    if first:
        return outs[0], outs[1:]
    return outs


def permuted(values, axis, target):
    size = lax.axis_size(axis)
    pairs = [(i, target(i)) for i in range(size) if 0 <= target(i) < size]
    return [lax.ppermute(v, axis, pairs) for v in values]


def on_device(tokens, norm_gain, qkv_weight, out_weight, band_counts, halo_rows, window_mask):
    mask = window_mask[0, 0]
    ring = lax.axis_size("lon")
    assert mask.shape[1] == 5 and ring % 4 == 0 and ring >= 8
    local = tokens[0, 0]
    rows = local.shape[0]
    outs = norm_call(local, norm_gain, halo_rows)
    own, (whole, first_rows, second_rows) = outs[:PARTS], outs[PARTS:]
    assert PARTS == 2

    partner = permuted([whole], "lon", lambda i: i ^ 1)
    same = permuted(own[:1], "lon", lambda i: i ^ 2)
    across = permuted(own[1:], "lon", lambda i: (i + (-2 if (i // 2) % 2 == 0 else 2)) % ring)
    same += permuted(own[1:], "lon", lambda i: i ^ 2)
    second_rows, *partner = lax.optimization_barrier((second_rows, *partner))
    halos = [
        permuted([first_rows], "lat", lambda b: b ^ 1)[0],
        permuted([second_rows], "lat", lambda b: ((b + 1) ^ 1) - 1)[0],
    ]
    lon = lax.axis_index("lon")
    gives_same = lon % 2 == (lon // 2) % 2

    def swapped(mine, others):
        return permuted([jnp.where(gives_same, mine, others)], "lon", lambda i: i ^ 1)[0]

    stage = functools.partial(stage_call, rows // mask.shape[0], band_counts, mask)
    half = rows // PARTS
    query, state = stage(["own"], [own], [], qkv_weight, starts=[[0, half]])

    same[0], query, state = lax.optimization_barrier((same[0], query, state))
    across = permuted(same[:1], "lon", lambda i: (i + (4 if (i // 2) % 2 == 0 else -4)) % ring) + across
    early = [["partner", "same"], [partner, same[:1]], halos, qkv_weight, query, state]
    state = stage(*early, starts=[[0], [0]])

    *rest, state = lax.optimization_barrier((*across, *same, state))
    across, same = rest[:PARTS], rest[PARTS:]
    near = [swapped(s, a) for s, a in zip(same, across)]
    final = (local, out_weight, [*partner, *own, *same, *across, *near, *halos])
    late = [["across", "same", "near"], [across, same[1:], near], [], qkv_weight, query, state, final]
    result = stage(*late, starts=[[0, half], [half], [0, half]])
    return result[None, None]


def solution(mesh):
    in_specs = (
        P("lat", "lon", None, None),
        P(),
        P(),
        P(),
        P("lat"),
        P(),
        P("lat", "lon", None, None),
    )
    out_specs = P("lat", "lon", None, None)
    return jax.shard_map(
        on_device, mesh=mesh, in_specs=in_specs, out_specs=out_specs, check_vma=False
    )
```

```python
import functools
import math

import jax
import jax.numpy as jnp
from jax import lax
from jax.experimental import pallas as pl
from jax.experimental.pallas import tpu as pltpu
from jax.sharding import PartitionSpec as P

HEADS = 16
LANES = 128
GROUP = 512
PARTS = 2
NEG = -1e30
FLOOR = -1e25
LOG2E = math.log2(math.e)
SUM_MIN, SUM_MAX = 2.0**-8, 2.0**24
VMEM_LIMIT = 60 * 1024 * 1024
CHUNKS = 4

epsilon = 1e-05


def contract_last(a, b):
    return lax.dot_general(a, b, (((1,), (1,)), ((), ())), preferred_element_type=jnp.float32)


def matmul(a, b):
    return jnp.dot(a, b, preferred_element_type=jnp.float32)


def norm_kernel(bands, tokens_hbm, gain_hbm, halo_rows_hbm, *refs):
    outs = refs[: PARTS + 3]
    tokens_ref, gain_ref, halo_rows_ref, normed_ref, edge_ref, in_sem, out_sem = refs[PARTS + 3 :]
    rows = tokens_ref.shape[0]
    block = rows // CHUNKS

    def chunk(i):
        at = pl.ds(i * block, block)
        return pltpu.make_async_copy(tokens_hbm.at[at], tokens_ref.at[at], in_sem.at[i])

    small = [
        pltpu.make_async_copy(gain_hbm, gain_ref, in_sem.at[CHUNKS]),
        pltpu.make_async_copy(halo_rows_hbm, halo_rows_ref, in_sem.at[CHUNKS + 1]),
    ]
    for copy in [chunk(0)] + small + [chunk(i) for i in range(1, CHUNKS)]:
        copy.start()
    small[0].wait()
    gain = gain_ref[...]
    sent = []
    part = rows // PARTS
    for i in range(CHUNKS):
        chunk(i).wait()
        at = pl.ds(i * block, block)
        values = tokens_ref[at]
        average = jnp.mean(values, axis=-1, keepdims=True)
        centered = values - average
        variance = jnp.mean(centered * centered, axis=-1, keepdims=True)
        normed_ref[at] = (centered * lax.rsqrt(variance + epsilon) * gain).astype(jnp.bfloat16)
        if (i + 1) * PARTS % CHUNKS == 0:
            p = (i + 1) * PARTS // CHUNKS - 1
            sent.append(pltpu.make_async_copy(normed_ref.at[pl.ds(p * part, part)], outs[p], out_sem.at[p]))
            sent[-1].start()
    sent.append(pltpu.make_async_copy(normed_ref, outs[PARTS], out_sem.at[PARTS]))
    sent[-1].start()
    small[1].wait()
    band = lax.axis_index("lat")
    even = band % 2 == 0
    south, north = jnp.minimum(band + 1, bands - 1), jnp.maximum(band - 1, 0)
    lists = (
        (jnp.where(even, south, north), jnp.where(even, 0, 1)),
        (jnp.where(even, north, south), jnp.where(even, 1, 0)),
    )
    for which, (owner, side) in enumerate(lists):
        wanted = halo_rows_ref[pl.ds(2 * owner + side, 1), :]
        slots = lax.broadcasted_iota(jnp.int32, (rows, wanted.shape[1]), 0)
        picks = (slots == wanted).astype(jnp.float32).astype(jnp.bfloat16)
        picked = lax.dot_general(
            picks, normed_ref[...], (((0,), (0,)), ((), ())), preferred_element_type=jnp.float32
        )
        edge_ref[which] = picked.astype(jnp.bfloat16)
        place = PARTS + 1 + which
        sent.append(pltpu.make_async_copy(edge_ref.at[which], outs[place], out_sem.at[place]))
        sent[-1].start()
    for copy in sent:
        copy.wait()


def norm_call(tokens, gain, halo_rows):
    rows, width = tokens.shape
    bands, _, halo = halo_rows.shape
    halo_rows = halo_rows.reshape(2 * bands, halo)
    part = jax.ShapeDtypeStruct((rows // PARTS, width), jnp.bfloat16)
    whole = jax.ShapeDtypeStruct((rows, width), jnp.bfloat16)
    edge = jax.ShapeDtypeStruct((halo, width), jnp.bfloat16)
    return pl.pallas_call(
        functools.partial(norm_kernel, bands),
        out_shape=[part] * PARTS + [whole] + [edge] * 2,
        in_specs=[pl.BlockSpec(memory_space=pl.ANY)] * 3,
        out_specs=[pl.BlockSpec(memory_space=pltpu.HBM)] * (PARTS + 3),
        scratch_shapes=[
            pltpu.VMEM((rows, width), jnp.float32),
            pltpu.VMEM((1, width), jnp.float32),
            pltpu.VMEM(halo_rows.shape, jnp.int32),
            pltpu.VMEM((rows, width), jnp.bfloat16),
            pltpu.VMEM((2, halo, width), jnp.bfloat16),
            pltpu.SemaphoreType.DMA((CHUNKS + 2,)),
            pltpu.SemaphoreType.DMA((PARTS + 3,)),
        ],
        compiler_params=pltpu.CompilerParams(vmem_limit_bytes=VMEM_LIMIT),
        cost_estimate=pl.CostEstimate(flops=10 * rows * width, bytes_accessed=6 * rows * width, transcendentals=0),
        name="layer_norm",
    )(tokens, gain.reshape(1, width), halo_rows)


def sector_columns(lon, reach):
    core, odd = lon % 2, (lon // 2) % 2
    return {
        "own": reach,
        "partner": reach + 1 - 2 * core,
        "same": reach + 2 - 4 * odd,
        "across": reach + 4 * odd - 2,
        "near": reach + 2 * core - 1,
    }


def block_bias(mask_ref, column, rows, dtype):
    blocks = mask_ref.shape[0]
    values = [jnp.where(mask_ref[b, column] > 0, 0.0, NEG) for b in range(blocks)]
    return jnp.concatenate([jnp.full((rows // blocks, LANES), v, jnp.float32) for v in values], axis=0).astype(dtype)


def safe_group(query, weights, sources, counts_ref, mask_ref, scratch, head_size):
    rows_ref, key_ref, value_ref, top_ref, sum_ref, acc_ref, flag_ref, limit_ref, sem = scratch
    rows = query.shape[0]
    wk, wv = weights
    tile = sources[0][0].shape[0]
    tiles = len(sources)
    blocks = mask_ref.shape[0]
    for t, (ref, column, seen, start) in enumerate(sources):
        size = ref.shape[0]
        copy = pltpu.make_async_copy(ref, rows_ref.at[pl.ds(0, size)], sem)
        copy.start()
        copy.wait()
        key_ref[pl.ds(t * tile, size)] = matmul(rows_ref[pl.ds(0, size)], wk[...]).astype(jnp.bfloat16)
        value_ref[pl.ds(t * tile, size)] = matmul(rows_ref[pl.ds(0, size)], wv[...]).astype(jnp.bfloat16)
        if size < tile:
            rest = pl.ds(t * tile + size, tile - size)
            key_ref[rest] = jnp.zeros((tile - size, key_ref.shape[1]), jnp.bfloat16)
            value_ref[rest] = jnp.zeros((tile - size, key_ref.shape[1]), jnp.bfloat16)
        for b in range(blocks):
            flag_ref[t, b] = mask_ref[b, column] if column is not None else 1
        if column is None:
            limit_ref[t] = jnp.where(seen, size, 0)
        else:
            limit_ref[t] = counts_ref[0] - start
    low = lax.broadcasted_iota(jnp.int32, (rows, LANES), 1) < head_size
    outs = []
    for pair in range(query.shape[1] // LANES):
        lanes = slice(pair * LANES, (pair + 1) * LANES)
        halves = []
        for head in range(2):
            own = jnp.where(low if head == 0 else ~low, query[:, lanes], jnp.zeros((), jnp.bfloat16))
            top_ref[...] = jnp.full_like(top_ref, FLOOR)
            sum_ref[...] = jnp.zeros_like(sum_ref)
            acc_ref[...] = jnp.zeros_like(acc_ref)

            def body(t, carry, own=own, lanes=lanes):
                at = pl.ds(pl.multiple_of(t * tile, tile), tile)
                scores = contract_last(own, key_ref[at, lanes]) * (LOG2E * head_size**-0.5)
                slot = lax.broadcasted_iota(jnp.int32, (1, tile), 1)
                scores = scores + jnp.where(slot < limit_ref[t], 0.0, NEG)
                row_bias = jnp.concatenate(
                    [
                        jnp.full((rows // blocks, 1), jnp.where(flag_ref[t, b] > 0, 0.0, NEG), jnp.float32)
                        for b in range(blocks)
                    ],
                    axis=0,
                )
                scores = scores + row_bias
                old = top_ref[...]
                new = jnp.maximum(old, jnp.max(scores, axis=-1, keepdims=True))
                scale = jnp.exp2(old - new)
                weight = jnp.exp2(scores - new[:, :1])
                sum_ref[...] = sum_ref[...] * scale + jnp.sum(weight, axis=-1, keepdims=True)
                acc_ref[...] = acc_ref[...] * scale + matmul(weight.astype(jnp.bfloat16), value_ref[at, lanes])
                top_ref[...] = new
                return carry

            lax.fori_loop(0, tiles, body, 0)
            halves.append(acc_ref[...] / sum_ref[...])
        outs.append(jnp.where(low, *halves).astype(jnp.bfloat16))
    return jnp.concatenate(outs, axis=1)


def stage_kernel(spec, *refs):
    first, last, sectors, part_starts, halos, head_size = spec
    refs = list(refs)

    def take(count):
        taken = refs[:count]
        del refs[:count]
        return taken

    counts_ref, mask_ref = take(2)
    sector_refs = [take(len(starts)) for starts in part_starts]
    halo_refs = take(2) if halos else []
    wq_ref = take(1)[0] if first else None
    wk_ref, wv_ref = take(2)
    if not first:
        query_in, acc_in, sum_in = take(3)
    if last:
        tokens_hbm, wo_hbm = take(2)
        all_refs = take(1 + 4 * PARTS + 2)
        (out_ref,) = take(1)
    else:
        if first:
            query_out = take(1)[0]
        acc_out, sum_out = take(2)
    key_ref, value_ref, ones_ref = take(3)
    score_refs, weight_refs = take(2), take(2)
    if last:
        res_ref, att_ref, acc_out, sum_out, out_sem, wo_ref, final_sem = take(7)

    reach = mask_ref.shape[1] // 2
    lon, lat = lax.axis_index("lon"), lax.axis_index("lat")
    bands = lax.axis_size("lat")
    north_there, south_there, even = lat > 0, lat < bands - 1, lat % 2 == 0
    halo_seen = (even & south_there | ~even & north_there, even & north_there | ~even & south_there)
    columns = sector_columns(lon, reach)
    count = counts_ref[0]

    step = pl.program_id(0)
    if last:
        final_copies = [
            pltpu.make_async_copy(tokens_hbm, res_ref, final_sem.at[0]),
            pltpu.make_async_copy(wo_hbm, wo_ref, final_sem.at[1]),
        ]

        @pl.when(step == 0)
        def _():
            for copy in final_copies:
                copy.start()

    wk, wv = wk_ref[...], wv_ref[...]
    if first:
        query = jnp.concatenate([matmul(ref[...], wq_ref[...]).astype(jnp.bfloat16) for ref in sector_refs[0]], axis=0)
        query_out[...] = query
    else:
        query = query_in[...]
    rows, width = query.shape
    zero = jnp.zeros((), jnp.bfloat16)
    biases, spans = [], []
    at = 0
    for name, parts, starts in zip(sectors, sector_refs, part_starts):
        begin = at
        for ref, start in zip(parts, starts):
            size = ref.shape[0]
            here = pl.ds(at, size)
            key_ref[:, here] = matmul(ref[...], wk).astype(jnp.bfloat16).T
            value = matmul(ref[...], wv)
            if start + size <= rows // 2:
                value_ref[here] = value.astype(jnp.bfloat16)
                ones_ref[here] = jnp.ones((size, LANES), jnp.bfloat16)
            else:
                live = start + lax.broadcasted_iota(jnp.int32, value.shape, 0) < count
                value_ref[here] = jnp.where(live, value, 0.0).astype(jnp.bfloat16)
                ones_ref[here] = jnp.where(live[:, :LANES], 1.0, 0.0).astype(jnp.bfloat16)
            at += size
        spans.append((begin, at))
        biases.append(None if name == "own" else block_bias(mask_ref, columns[name], rows, jnp.bfloat16))
    if halo_refs:
        begin = at
        for ref, seen in zip(halo_refs, halo_seen):
            size = ref.shape[0]
            here = pl.ds(at, size)
            there = jnp.where(seen, 1.0, 0.0)
            key_ref[:, here] = matmul(ref[...], wk).astype(jnp.bfloat16).T
            value_ref[here] = (matmul(ref[...], wv) * there).astype(jnp.bfloat16)
            ones_ref[here] = jnp.full((size, LANES), there, jnp.float32).astype(jnp.bfloat16)
            at += size
        spans.append((begin, at))
        biases.append(None)

    low = lax.broadcasted_iota(jnp.int32, (rows, LANES), 1) < head_size

    def lanes_of(pair):
        return slice(pair * LANES, (pair + 1) * LANES)


    whole_query = query

    def score(pair):
        query = whole_query[:, lanes_of(pair)]
        both = jnp.concatenate([jnp.where(low, query, zero), jnp.where(low, zero, query)], axis=0)
        for (begin, end), bias in zip(spans, biases):
            left, right = both, key_ref[lanes_of(pair), begin:end]
            if bias is not None:
                left = jnp.concatenate([both, jnp.concatenate([bias, bias], axis=0)], axis=1)
                right = jnp.concatenate([right, jnp.ones((LANES, end - begin), jnp.bfloat16)], axis=0)
            score_refs[pair % 2][:, begin:end] = matmul(left, right)

    def weigh(pair):
        scores = score_refs[pair % 2][...] * (LOG2E * head_size**-0.5)
        weight_refs[pair % 2][...] = jnp.exp2(scores).astype(jnp.bfloat16)

    def gather(pair):
        lanes = lanes_of(pair)
        values = jnp.concatenate([value_ref[:, lanes], ones_ref[...]], axis=1)
        result = matmul(weight_refs[pair % 2][...], values)
        acc = jnp.where(low, result[:rows, :LANES], result[rows:, :LANES])
        total = jnp.where(low, result[:rows, LANES:], result[rows:, LANES:])
        if not first:
            acc = acc + acc_in[:, lanes]
            total = total + sum_in[:, lanes]
        acc_out[:, lanes] = acc
        sum_out[:, lanes] = total

    pairs = width // LANES
    for p in range(pairs + 2):
        if p < pairs:
            score(p)
        if 0 <= p - 1 < pairs:
            weigh(p - 1)
        if 0 <= p - 2 < pairs:
            gather(p - 2)
    if not last:
        return

    total = sum_out[...]
    fine = (total > SUM_MIN) & (total < SUM_MAX)
    for pair in range(width // LANES):
        lanes = slice(pair * LANES, (pair + 1) * LANES)
        att_ref[:, lanes] = (acc_out[:, lanes] / total[:, lanes]).astype(jnp.bfloat16)

    @pl.when(jnp.min(fine.astype(jnp.float32)) < 0.5)
    def _():
        sources = []
        part = rows // PARTS
        for i in range(PARTS):
            sources.append((all_refs[0].at[pl.ds(i * part, part)], columns["partner"], None, i * part))
        for s, name in enumerate(("own", "same", "across", "near")):
            for i, ref in enumerate(all_refs[1 + s * PARTS : 1 + (s + 1) * PARTS]):
                sources.append((ref, columns[name], None, i * part))
        for ref, seen in zip(all_refs[1 + 4 * PARTS :], halo_seen):
            sources.append((ref, None, seen, 0))
        att_ref[...] = safe_group(query, (wk_ref, wv_ref), sources, counts_ref, mask_ref, refs, head_size)

    @pl.when(step == 0)
    def _():
        for copy in final_copies:
            copy.wait()

    rows_of = pl.ds(pl.multiple_of(step * width, width), width)
    last_step = step == pl.num_programs(0) - 1

    @pl.when(~last_step)
    def _():
        res_ref[...] += matmul(att_ref[...], wo_ref[rows_of])

    @pl.when(last_step)
    def _():
        size = res_ref.shape[1] // out_sem.shape[0]
        live = lax.broadcasted_iota(jnp.int32, (rows, size), 0) < count
        copies = []
        for n in range(out_sem.shape[0]):
            block = pl.ds(n * size, size)
            result = res_ref[:, block] + matmul(att_ref[...], wo_ref[rows_of, block])
            res_ref[:, block] = jnp.where(live, result, 0.0)
            copies.append(pltpu.make_async_copy(res_ref.at[:, block], out_ref.at[:, block], out_sem.at[n]))
            copies[-1].start()
        for copy in copies:
            copy.wait()


def stage_call(block_rows, counts, mask, sectors, sector_parts, halos, qkv_weight, query=None, state=None, final=None, starts=None):
    first, last = query is None, final is not None
    model, width = qkv_weight.shape[0], qkv_weight.shape[1] // 3
    head_size = width // HEADS
    rows = mask.shape[0] * block_rows
    steps = width // GROUP
    smem = pl.BlockSpec(memory_space=pltpu.SMEM)

    def fixed(shape):
        return pl.BlockSpec(shape, lambda g: (0, 0), pipeline_mode=pl.Buffered(1))

    def weight(third):
        return pl.BlockSpec((model, GROUP), lambda g: (0, third * steps + g))

    columns = pl.BlockSpec((rows, GROUP), lambda g: (0, g))
    args, specs = [counts, mask], [smem, smem]
    for parts in sector_parts:
        args += parts
        specs += [fixed(p.shape) for p in parts]
    for halo in halos:
        args.append(halo)
        specs.append(fixed(halo.shape))
    for third in range(0 if first else 1, 3):
        args.append(qkv_weight)
        specs.append(weight(third))
    if not first:
        args += [query, *state]
        specs += [columns] * 3
    keys = sum(p.shape[0] for parts in sector_parts for p in parts) + sum(h.shape[0] for h in halos)
    scratch = [
        pltpu.VMEM((GROUP, keys), jnp.bfloat16),
        pltpu.VMEM((keys, GROUP), jnp.bfloat16),
        pltpu.VMEM((keys, LANES), jnp.bfloat16),
        pltpu.VMEM((2 * rows, keys), jnp.float32),
        pltpu.VMEM((2 * rows, keys), jnp.float32),
        pltpu.VMEM((2 * rows, keys), jnp.bfloat16),
        pltpu.VMEM((2 * rows, keys), jnp.bfloat16),
    ]
    wide = jax.ShapeDtypeStruct((rows, width), jnp.float32)
    moved = sum(a.size * a.dtype.itemsize for a in args[2:] if a is not qkv_weight) + 3 * model * width * 2
    if last:
        tokens, out_weight, sources = final
        args += [tokens, out_weight, *sources]
        specs += [pl.BlockSpec(memory_space=pl.ANY)] * 2
        specs += [pl.BlockSpec(memory_space=pl.ANY)] * len(sources)
        out_shape = [wide]
        out_specs = [pl.BlockSpec(memory_space=pl.ANY)]
        part = rows // PARTS
        tiles = len(sources) + PARTS - 1
        scratch += [
            pltpu.VMEM((rows, width), jnp.float32),
            pltpu.VMEM((rows, GROUP), jnp.bfloat16),
            pltpu.VMEM((rows, GROUP), jnp.float32),
            pltpu.VMEM((rows, GROUP), jnp.float32),
            pltpu.SemaphoreType.DMA((4,)),
            pltpu.VMEM(out_weight.shape, jnp.bfloat16),
            pltpu.SemaphoreType.DMA((2,)),
            pltpu.VMEM((part, model), jnp.bfloat16),
            pltpu.VMEM((part * tiles, GROUP), jnp.bfloat16),
            pltpu.VMEM((part * tiles, GROUP), jnp.bfloat16),
            pltpu.VMEM((rows, LANES), jnp.float32),
            pltpu.VMEM((rows, LANES), jnp.float32),
            pltpu.VMEM((rows, LANES), jnp.float32),
            pltpu.SMEM((tiles, mask.shape[0]), jnp.int32),
            pltpu.SMEM((tiles,), jnp.int32),
            pltpu.SemaphoreType.DMA,
        ]
    else:
        out_shape = [wide] * 2
        out_specs = [columns] * 2
        if first:
            out_shape = [jax.ShapeDtypeStruct((rows, width), jnp.bfloat16)] + out_shape
            out_specs = [columns] + out_specs
    flops = 2 * keys * model * 2 * width + 16 * rows * keys * width
    flops += 2 * rows * model * width * (int(first) + int(last))
    outs = pl.pallas_call(
        functools.partial(stage_kernel, (first, last, sectors, starts, bool(halos), head_size)),
        out_shape=out_shape,
        grid=(steps,),
        in_specs=specs,
        out_specs=out_specs,
        scratch_shapes=scratch,
        compiler_params=pltpu.CompilerParams(vmem_limit_bytes=VMEM_LIMIT),
        cost_estimate=pl.CostEstimate(flops=flops // (16 if first else 1), bytes_accessed=moved // 16, transcendentals=0),
        name="attend_" + "_".join(sectors),
    )(*args)
    if last:
        return outs[0]
    if first:
        return outs[0], outs[1:]
    return outs


def permuted(values, axis, target):
    size = lax.axis_size(axis)
    pairs = [(i, target(i)) for i in range(size) if 0 <= target(i) < size]
    return [lax.ppermute(v, axis, pairs) for v in values]


def on_device(tokens, norm_gain, qkv_weight, out_weight, band_counts, halo_rows, window_mask):
    mask = window_mask[0, 0]
    ring = lax.axis_size("lon")
    assert mask.shape[1] == 5 and ring % 4 == 0 and ring >= 8
    local = tokens[0, 0]
    rows = local.shape[0]
    outs = norm_call(local, norm_gain, halo_rows)
    own, (whole, first_rows, second_rows) = outs[:PARTS], outs[PARTS:]
    assert PARTS == 2

    partner = permuted([whole], "lon", lambda i: i ^ 1)
    same = permuted(own[:1], "lon", lambda i: i ^ 2)
    across = permuted(own[1:], "lon", lambda i: (i + (-2 if (i // 2) % 2 == 0 else 2)) % ring)
    same += permuted(own[1:], "lon", lambda i: i ^ 2)
    second_rows, *partner = lax.optimization_barrier((second_rows, *partner))
    halos = [
        permuted([first_rows], "lat", lambda b: b ^ 1)[0],
        permuted([second_rows], "lat", lambda b: ((b + 1) ^ 1) - 1)[0],
    ]
    lon = lax.axis_index("lon")
    gives_same = lon % 2 == (lon // 2) % 2

    def swapped(mine, others):
        return permuted([jnp.where(gives_same, mine, others)], "lon", lambda i: i ^ 1)[0]

    stage = functools.partial(stage_call, rows // mask.shape[0], band_counts, mask)
    half = rows // PARTS
    query, state = stage(["own"], [own], [], qkv_weight, starts=[[0, half]])

    same[0], query, state = lax.optimization_barrier((same[0], query, state))
    across = permuted(same[:1], "lon", lambda i: (i + (4 if (i // 2) % 2 == 0 else -4)) % ring) + across
    early = [["partner", "same"], [partner, same[:1]], halos, qkv_weight, query, state]
    state = stage(*early, starts=[[0], [0]])

    *rest, state = lax.optimization_barrier((*across, *same, state))
    across, same = rest[:PARTS], rest[PARTS:]
    near = [swapped(s, a) for s, a in zip(same, across)]
    final = (local, out_weight, [*partner, *own, *same, *across, *near, *halos])
    late = [["across", "same", "near"], [across, same[1:], near], [], qkv_weight, query, state, final]
    result = stage(*late, starts=[[0, half], [half], [0, half]])
    return result[None, None]


def solution(mesh):
    in_specs = (
        P("lat", "lon", None, None),
        P(),
        P(),
        P(),
        P("lat"),
        P(),
        P("lat", "lon", None, None),
    )
    out_specs = P("lat", "lon", None, None)
    return jax.shard_map(
        on_device, mesh=mesh, in_specs=in_specs, out_specs=out_specs, check_vma=False
    )
```

```python
import functools
import math

import jax
import jax.numpy as jnp
from jax import lax
from jax.experimental import pallas as pl
from jax.experimental.pallas import tpu as pltpu
from jax.sharding import PartitionSpec as P

HEADS = 16
LANES = 128
GROUP = 512
PARTS = 2
NEG = -1e30
FLOOR = -1e25
LOG2E = math.log2(math.e)
SUM_MIN, SUM_MAX = 2.0**-8, 2.0**24
VMEM_LIMIT = 60 * 1024 * 1024
CHUNKS = 4

epsilon = 1e-05


def contract_last(a, b):
    return lax.dot_general(a, b, (((1,), (1,)), ((), ())), preferred_element_type=jnp.float32)


def matmul(a, b):
    return jnp.dot(a, b, preferred_element_type=jnp.float32)


def norm_kernel(bands, tokens_hbm, gain_hbm, halo_rows_hbm, *refs):
    outs = refs[: PARTS + 3]
    tokens_ref, gain_ref, halo_rows_ref, normed_ref, edge_ref, in_sem, out_sem = refs[PARTS + 3 :]
    rows = tokens_ref.shape[0]
    block = rows // CHUNKS

    def chunk(i):
        at = pl.ds(i * block, block)
        return pltpu.make_async_copy(tokens_hbm.at[at], tokens_ref.at[at], in_sem.at[i])

    small = [
        pltpu.make_async_copy(gain_hbm, gain_ref, in_sem.at[CHUNKS]),
        pltpu.make_async_copy(halo_rows_hbm, halo_rows_ref, in_sem.at[CHUNKS + 1]),
    ]
    for copy in [chunk(0)] + small + [chunk(i) for i in range(1, CHUNKS)]:
        copy.start()
    small[0].wait()
    gain = gain_ref[...]
    sent = []
    part = rows // PARTS
    for i in range(CHUNKS):
        chunk(i).wait()
        at = pl.ds(i * block, block)
        values = tokens_ref[at]
        average = jnp.mean(values, axis=-1, keepdims=True)
        centered = values - average
        variance = jnp.mean(centered * centered, axis=-1, keepdims=True)
        normed_ref[at] = (centered * lax.rsqrt(variance + epsilon) * gain).astype(jnp.bfloat16)
        if (i + 1) * PARTS % CHUNKS == 0:
            p = (i + 1) * PARTS // CHUNKS - 1
            sent.append(pltpu.make_async_copy(normed_ref.at[pl.ds(p * part, part)], outs[p], out_sem.at[p]))
            sent[-1].start()
    sent.append(pltpu.make_async_copy(normed_ref, outs[PARTS], out_sem.at[PARTS]))
    sent[-1].start()
    small[1].wait()
    band = lax.axis_index("lat")
    even = band % 2 == 0
    south, north = jnp.minimum(band + 1, bands - 1), jnp.maximum(band - 1, 0)
    lists = (
        (jnp.where(even, south, north), jnp.where(even, 0, 1)),
        (jnp.where(even, north, south), jnp.where(even, 1, 0)),
    )
    for which, (owner, side) in enumerate(lists):
        wanted = halo_rows_ref[pl.ds(2 * owner + side, 1), :]
        slots = lax.broadcasted_iota(jnp.int32, (rows, wanted.shape[1]), 0)
        picks = (slots == wanted).astype(jnp.float32).astype(jnp.bfloat16)
        picked = lax.dot_general(
            picks, normed_ref[...], (((0,), (0,)), ((), ())), preferred_element_type=jnp.float32
        )
        edge_ref[which] = picked.astype(jnp.bfloat16)
        place = PARTS + 1 + which
        sent.append(pltpu.make_async_copy(edge_ref.at[which], outs[place], out_sem.at[place]))
        sent[-1].start()
    for copy in sent:
        copy.wait()


def norm_call(tokens, gain, halo_rows):
    rows, width = tokens.shape
    bands, _, halo = halo_rows.shape
    halo_rows = halo_rows.reshape(2 * bands, halo)
    part = jax.ShapeDtypeStruct((rows // PARTS, width), jnp.bfloat16)
    whole = jax.ShapeDtypeStruct((rows, width), jnp.bfloat16)
    edge = jax.ShapeDtypeStruct((halo, width), jnp.bfloat16)
    return pl.pallas_call(
        functools.partial(norm_kernel, bands),
        out_shape=[part] * PARTS + [whole] + [edge] * 2,
        in_specs=[pl.BlockSpec(memory_space=pl.ANY)] * 3,
        out_specs=[pl.BlockSpec(memory_space=pltpu.HBM)] * (PARTS + 3),
        scratch_shapes=[
            pltpu.VMEM((rows, width), jnp.float32),
            pltpu.VMEM((1, width), jnp.float32),
            pltpu.VMEM(halo_rows.shape, jnp.int32),
            pltpu.VMEM((rows, width), jnp.bfloat16),
            pltpu.VMEM((2, halo, width), jnp.bfloat16),
            pltpu.SemaphoreType.DMA((CHUNKS + 2,)),
            pltpu.SemaphoreType.DMA((PARTS + 3,)),
        ],
        compiler_params=pltpu.CompilerParams(vmem_limit_bytes=VMEM_LIMIT),
        cost_estimate=pl.CostEstimate(flops=10 * rows * width, bytes_accessed=6 * rows * width, transcendentals=0),
        name="layer_norm",
    )(tokens, gain.reshape(1, width), halo_rows)


def sector_columns(lon, reach):
    core, odd = lon % 2, (lon // 2) % 2
    return {
        "own": reach,
        "partner": reach + 1 - 2 * core,
        "same": reach + 2 - 4 * odd,
        "across": reach + 4 * odd - 2,
        "near": reach + 2 * core - 1,
    }


def block_bias(mask_ref, column, rows, dtype):
    blocks = mask_ref.shape[0]
    values = [jnp.where(mask_ref[b, column] > 0, 0.0, NEG) for b in range(blocks)]
    return jnp.concatenate([jnp.full((rows // blocks, LANES), v, jnp.float32) for v in values], axis=0).astype(dtype)


def safe_group(query, weights, sources, counts_ref, mask_ref, scratch, head_size):
    rows_ref, key_ref, value_ref, top_ref, sum_ref, acc_ref, flag_ref, limit_ref, sem = scratch
    rows = query.shape[0]
    wk, wv = weights
    tile = sources[0][0].shape[0]
    tiles = len(sources)
    blocks = mask_ref.shape[0]
    for t, (ref, column, seen, start) in enumerate(sources):
        size = ref.shape[0]
        copy = pltpu.make_async_copy(ref, rows_ref.at[pl.ds(0, size)], sem)
        copy.start()
        copy.wait()
        key_ref[pl.ds(t * tile, size)] = matmul(rows_ref[pl.ds(0, size)], wk[...]).astype(jnp.bfloat16)
        value_ref[pl.ds(t * tile, size)] = matmul(rows_ref[pl.ds(0, size)], wv[...]).astype(jnp.bfloat16)
        if size < tile:
            rest = pl.ds(t * tile + size, tile - size)
            key_ref[rest] = jnp.zeros((tile - size, key_ref.shape[1]), jnp.bfloat16)
            value_ref[rest] = jnp.zeros((tile - size, key_ref.shape[1]), jnp.bfloat16)
        for b in range(blocks):
            flag_ref[t, b] = mask_ref[b, column] if column is not None else 1
        if column is None:
            limit_ref[t] = jnp.where(seen, size, 0)
        else:
            limit_ref[t] = counts_ref[0] - start
    low = lax.broadcasted_iota(jnp.int32, (rows, LANES), 1) < head_size
    outs = []
    for pair in range(query.shape[1] // LANES):
        lanes = slice(pair * LANES, (pair + 1) * LANES)
        halves = []
        for head in range(2):
            own = jnp.where(low if head == 0 else ~low, query[:, lanes], jnp.zeros((), jnp.bfloat16))
            top_ref[...] = jnp.full_like(top_ref, FLOOR)
            sum_ref[...] = jnp.zeros_like(sum_ref)
            acc_ref[...] = jnp.zeros_like(acc_ref)

            def body(t, carry, own=own, lanes=lanes):
                at = pl.ds(pl.multiple_of(t * tile, tile), tile)
                scores = contract_last(own, key_ref[at, lanes]) * (LOG2E * head_size**-0.5)
                slot = lax.broadcasted_iota(jnp.int32, (1, tile), 1)
                scores = scores + jnp.where(slot < limit_ref[t], 0.0, NEG)
                row_bias = jnp.concatenate(
                    [
                        jnp.full((rows // blocks, 1), jnp.where(flag_ref[t, b] > 0, 0.0, NEG), jnp.float32)
                        for b in range(blocks)
                    ],
                    axis=0,
                )
                scores = scores + row_bias
                old = top_ref[...]
                new = jnp.maximum(old, jnp.max(scores, axis=-1, keepdims=True))
                scale = jnp.exp2(old - new)
                weight = jnp.exp2(scores - new[:, :1])
                sum_ref[...] = sum_ref[...] * scale + jnp.sum(weight, axis=-1, keepdims=True)
                acc_ref[...] = acc_ref[...] * scale + matmul(weight.astype(jnp.bfloat16), value_ref[at, lanes])
                top_ref[...] = new
                return carry

            lax.fori_loop(0, tiles, body, 0)
            halves.append(acc_ref[...] / sum_ref[...])
        outs.append(jnp.where(low, *halves).astype(jnp.bfloat16))
    return jnp.concatenate(outs, axis=1)


def stage_kernel(spec, *refs):
    first, last, sectors, part_starts, halos, head_size = spec
    refs = list(refs)

    def take(count):
        taken = refs[:count]
        del refs[:count]
        return taken

    counts_ref, mask_ref = take(2)
    sector_refs = [take(len(starts)) for starts in part_starts]
    halo_refs = take(2) if halos else []
    wq_ref = take(1)[0] if first else None
    wk_ref, wv_ref = take(2)
    if not first:
        query_in, acc_in, sum_in = take(3)
    if last:
        tokens_hbm, wo_hbm = take(2)
        all_refs = take(1 + 4 * PARTS + 2)
        (out_ref,) = take(1)
    else:
        if first:
            query_out = take(1)[0]
        acc_out, sum_out = take(2)
    key_ref, value_ref, ones_ref = take(3)
    score_refs, weight_refs = take(2), take(2)
    if last:
        acc_hbm, sum_hbm = acc_in, sum_in
        acc_in, sum_in, state_sem = take(3)
        res_ref, att_ref, acc_out, sum_out, out_sem, wo_ref, final_sem = take(7)

    reach = mask_ref.shape[1] // 2
    lon, lat = lax.axis_index("lon"), lax.axis_index("lat")
    bands = lax.axis_size("lat")
    north_there, south_there, even = lat > 0, lat < bands - 1, lat % 2 == 0
    halo_seen = (even & south_there | ~even & north_there, even & north_there | ~even & south_there)
    columns = sector_columns(lon, reach)
    count = counts_ref[0]

    step = pl.program_id(0)
    state_copies, final_copies = [], []
    if last:
        state_copies = [
            pltpu.make_async_copy(acc_hbm, acc_in, state_sem.at[0]),
            pltpu.make_async_copy(sum_hbm, sum_in, state_sem.at[1]),
        ]
    if last:
        final_copies = [
            pltpu.make_async_copy(tokens_hbm, res_ref, final_sem.at[0]),
            pltpu.make_async_copy(wo_hbm, wo_ref, final_sem.at[1]),
        ]
    if state_copies:

        @pl.when(step == 0)
        def _():
            for copy in state_copies + final_copies:
                copy.start()

    wk, wv = wk_ref[...], wv_ref[...]
    if first:
        query = jnp.concatenate([matmul(ref[...], wq_ref[...]).astype(jnp.bfloat16) for ref in sector_refs[0]], axis=0)
        query_out[...] = query
    else:
        query = query_in[...]
    rows, width = query.shape
    zero = jnp.zeros((), jnp.bfloat16)
    biases, spans = [], []
    at = 0
    for name, parts, starts in zip(sectors, sector_refs, part_starts):
        begin = at
        for ref, start in zip(parts, starts):
            size = ref.shape[0]
            here = pl.ds(at, size)
            key_ref[:, here] = matmul(ref[...], wk).astype(jnp.bfloat16).T
            value = matmul(ref[...], wv)
            if start + size <= rows // 2:
                value_ref[here] = value.astype(jnp.bfloat16)
                ones_ref[here] = jnp.ones((size, LANES), jnp.bfloat16)
            else:
                live = start + lax.broadcasted_iota(jnp.int32, value.shape, 0) < count
                value_ref[here] = jnp.where(live, value, 0.0).astype(jnp.bfloat16)
                ones_ref[here] = jnp.where(live[:, :LANES], 1.0, 0.0).astype(jnp.bfloat16)
            at += size
        spans.append((begin, at))
        biases.append(None if name == "own" else block_bias(mask_ref, columns[name], rows, jnp.bfloat16))
    if halo_refs:
        begin = at
        for ref, seen in zip(halo_refs, halo_seen):
            size = ref.shape[0]
            here = pl.ds(at, size)
            there = jnp.where(seen, 1.0, 0.0)
            key_ref[:, here] = matmul(ref[...], wk).astype(jnp.bfloat16).T
            value_ref[here] = (matmul(ref[...], wv) * there).astype(jnp.bfloat16)
            ones_ref[here] = jnp.full((size, LANES), there, jnp.float32).astype(jnp.bfloat16)
            at += size
        spans.append((begin, at))
        biases.append(None)

    low = lax.broadcasted_iota(jnp.int32, (rows, LANES), 1) < head_size

    def lanes_of(pair):
        return slice(pair * LANES, (pair + 1) * LANES)

    if state_copies:

        @pl.when(step == 0)
        def _():
            for copy in state_copies:
                copy.wait()


    whole_query = query

    def score(pair):
        query = whole_query[:, lanes_of(pair)]
        both = jnp.concatenate([jnp.where(low, query, zero), jnp.where(low, zero, query)], axis=0)
        for (begin, end), bias in zip(spans, biases):
            left, right = both, key_ref[lanes_of(pair), begin:end]
            if bias is not None:
                left = jnp.concatenate([both, jnp.concatenate([bias, bias], axis=0)], axis=1)
                right = jnp.concatenate([right, jnp.ones((LANES, end - begin), jnp.bfloat16)], axis=0)
            score_refs[pair % 2][:, begin:end] = matmul(left, right)

    def weigh(pair):
        scores = score_refs[pair % 2][...] * (LOG2E * head_size**-0.5)
        weight_refs[pair % 2][...] = jnp.exp2(scores).astype(jnp.bfloat16)

    def gather(pair):
        lanes = lanes_of(pair)
        values = jnp.concatenate([value_ref[:, lanes], ones_ref[...]], axis=1)
        result = matmul(weight_refs[pair % 2][...], values)
        acc = jnp.where(low, result[:rows, :LANES], result[rows:, :LANES])
        total = jnp.where(low, result[:rows, LANES:], result[rows:, LANES:])
        if not first:
            place = pl.ds(pl.multiple_of(step * width + pair * LANES, LANES), LANES) if last else lanes
            acc = acc + acc_in[:, place]
            total = total + sum_in[:, place]
        acc_out[:, lanes] = acc
        sum_out[:, lanes] = total

    pairs = width // LANES
    for p in range(pairs + 2):
        if p < pairs:
            score(p)
        if 0 <= p - 1 < pairs:
            weigh(p - 1)
        if 0 <= p - 2 < pairs:
            gather(p - 2)
    if not last:
        return

    total = sum_out[...]
    fine = (total > SUM_MIN) & (total < SUM_MAX)
    for pair in range(width // LANES):
        lanes = slice(pair * LANES, (pair + 1) * LANES)
        att_ref[:, lanes] = (acc_out[:, lanes] / total[:, lanes]).astype(jnp.bfloat16)

    @pl.when(jnp.min(fine.astype(jnp.float32)) < 0.5)
    def _():
        sources = []
        part = rows // PARTS
        for i in range(PARTS):
            sources.append((all_refs[0].at[pl.ds(i * part, part)], columns["partner"], None, i * part))
        for s, name in enumerate(("own", "same", "across", "near")):
            for i, ref in enumerate(all_refs[1 + s * PARTS : 1 + (s + 1) * PARTS]):
                sources.append((ref, columns[name], None, i * part))
        for ref, seen in zip(all_refs[1 + 4 * PARTS :], halo_seen):
            sources.append((ref, None, seen, 0))
        att_ref[...] = safe_group(query, (wk_ref, wv_ref), sources, counts_ref, mask_ref, refs, head_size)

    @pl.when(step == 0)
    def _():
        for copy in final_copies:
            copy.wait()

    rows_of = pl.ds(pl.multiple_of(step * width, width), width)
    last_step = step == pl.num_programs(0) - 1

    @pl.when(~last_step)
    def _():
        res_ref[...] += matmul(att_ref[...], wo_ref[rows_of])

    @pl.when(last_step)
    def _():
        size = res_ref.shape[1] // out_sem.shape[0]
        live = lax.broadcasted_iota(jnp.int32, (rows, size), 0) < count
        copies = []
        for n in range(out_sem.shape[0]):
            block = pl.ds(n * size, size)
            result = res_ref[:, block] + matmul(att_ref[...], wo_ref[rows_of, block])
            res_ref[:, block] = jnp.where(live, result, 0.0)
            copies.append(pltpu.make_async_copy(res_ref.at[:, block], out_ref.at[:, block], out_sem.at[n]))
            copies[-1].start()
        for copy in copies:
            copy.wait()


def stage_call(block_rows, counts, mask, sectors, sector_parts, halos, qkv_weight, query=None, state=None, final=None, starts=None):
    first, last = query is None, final is not None
    model, width = qkv_weight.shape[0], qkv_weight.shape[1] // 3
    head_size = width // HEADS
    rows = mask.shape[0] * block_rows
    steps = width // GROUP
    smem = pl.BlockSpec(memory_space=pltpu.SMEM)

    def fixed(shape):
        return pl.BlockSpec(shape, lambda g: (0, 0), pipeline_mode=pl.Buffered(1))

    def weight(third):
        return pl.BlockSpec((model, GROUP), lambda g: (0, third * steps + g))

    columns = pl.BlockSpec((rows, GROUP), lambda g: (0, g))
    args, specs = [counts, mask], [smem, smem]
    for parts in sector_parts:
        args += parts
        specs += [fixed(p.shape) for p in parts]
    for halo in halos:
        args.append(halo)
        specs.append(fixed(halo.shape))
    for third in range(0 if first else 1, 3):
        args.append(qkv_weight)
        specs.append(weight(third))
    if not first:
        args += [query, *state]
        specs += [columns] + [pl.BlockSpec(memory_space=pl.ANY) if last else columns] * 2
    keys = sum(p.shape[0] for parts in sector_parts for p in parts) + sum(h.shape[0] for h in halos)
    scratch = [
        pltpu.VMEM((GROUP, keys), jnp.bfloat16),
        pltpu.VMEM((keys, GROUP), jnp.bfloat16),
        pltpu.VMEM((keys, LANES), jnp.bfloat16),
        pltpu.VMEM((2 * rows, keys), jnp.float32),
        pltpu.VMEM((2 * rows, keys), jnp.float32),
        pltpu.VMEM((2 * rows, keys), jnp.bfloat16),
        pltpu.VMEM((2 * rows, keys), jnp.bfloat16),
    ]
    if last:
        scratch += [pltpu.VMEM((rows, width), jnp.float32)] * 2 + [pltpu.SemaphoreType.DMA((2,))]
    wide = jax.ShapeDtypeStruct((rows, width), jnp.float32)
    moved = sum(a.size * a.dtype.itemsize for a in args[2:] if a is not qkv_weight) + 3 * model * width * 2
    if last:
        tokens, out_weight, sources = final
        args += [tokens, out_weight, *sources]
        specs += [pl.BlockSpec(memory_space=pl.ANY)] * 2
        specs += [pl.BlockSpec(memory_space=pl.ANY)] * len(sources)
        out_shape = [wide]
        out_specs = [pl.BlockSpec(memory_space=pl.ANY)]
        part = rows // PARTS
        tiles = len(sources) + PARTS - 1
        scratch += [
            pltpu.VMEM((rows, width), jnp.float32),
            pltpu.VMEM((rows, GROUP), jnp.bfloat16),
            pltpu.VMEM((rows, GROUP), jnp.float32),
            pltpu.VMEM((rows, GROUP), jnp.float32),
            pltpu.SemaphoreType.DMA((4,)),
            pltpu.VMEM(out_weight.shape, jnp.bfloat16),
            pltpu.SemaphoreType.DMA((2,)),
            pltpu.VMEM((part, model), jnp.bfloat16),
            pltpu.VMEM((part * tiles, GROUP), jnp.bfloat16),
            pltpu.VMEM((part * tiles, GROUP), jnp.bfloat16),
            pltpu.VMEM((rows, LANES), jnp.float32),
            pltpu.VMEM((rows, LANES), jnp.float32),
            pltpu.VMEM((rows, LANES), jnp.float32),
            pltpu.SMEM((tiles, mask.shape[0]), jnp.int32),
            pltpu.SMEM((tiles,), jnp.int32),
            pltpu.SemaphoreType.DMA,
        ]
    else:
        out_shape = [wide] * 2
        out_specs = [columns] * 2
        if first:
            out_shape = [jax.ShapeDtypeStruct((rows, width), jnp.bfloat16)] + out_shape
            out_specs = [columns] + out_specs
    flops = 2 * keys * model * 2 * width + 16 * rows * keys * width
    flops += 2 * rows * model * width * (int(first) + int(last))
    outs = pl.pallas_call(
        functools.partial(stage_kernel, (first, last, sectors, starts, bool(halos), head_size)),
        out_shape=out_shape,
        grid=(steps,),
        in_specs=specs,
        out_specs=out_specs,
        scratch_shapes=scratch,
        compiler_params=pltpu.CompilerParams(vmem_limit_bytes=VMEM_LIMIT),
        cost_estimate=pl.CostEstimate(flops=flops // (16 if first else 1), bytes_accessed=moved // 16, transcendentals=0),
        name="attend_" + "_".join(sectors),
    )(*args)
    if last:
        return outs[0]
    if first:
        return outs[0], outs[1:]
    return outs


def permuted(values, axis, target):
    size = lax.axis_size(axis)
    pairs = [(i, target(i)) for i in range(size) if 0 <= target(i) < size]
    return [lax.ppermute(v, axis, pairs) for v in values]


def on_device(tokens, norm_gain, qkv_weight, out_weight, band_counts, halo_rows, window_mask):
    mask = window_mask[0, 0]
    ring = lax.axis_size("lon")
    assert mask.shape[1] == 5 and ring % 4 == 0 and ring >= 8
    local = tokens[0, 0]
    rows = local.shape[0]
    outs = norm_call(local, norm_gain, halo_rows)
    own, (whole, first_rows, second_rows) = outs[:PARTS], outs[PARTS:]
    assert PARTS == 2

    partner = permuted([whole], "lon", lambda i: i ^ 1)
    same = permuted(own[:1], "lon", lambda i: i ^ 2)
    across = permuted(own[1:], "lon", lambda i: (i + (-2 if (i // 2) % 2 == 0 else 2)) % ring)
    same += permuted(own[1:], "lon", lambda i: i ^ 2)
    second_rows, *partner = lax.optimization_barrier((second_rows, *partner))
    halos = [
        permuted([first_rows], "lat", lambda b: b ^ 1)[0],
        permuted([second_rows], "lat", lambda b: ((b + 1) ^ 1) - 1)[0],
    ]
    lon = lax.axis_index("lon")
    gives_same = lon % 2 == (lon // 2) % 2

    def swapped(mine, others):
        return permuted([jnp.where(gives_same, mine, others)], "lon", lambda i: i ^ 1)[0]

    stage = functools.partial(stage_call, rows // mask.shape[0], band_counts, mask)
    half = rows // PARTS
    query, state = stage(["own"], [own], [], qkv_weight, starts=[[0, half]])

    same[0], query, state = lax.optimization_barrier((same[0], query, state))
    across = permuted(same[:1], "lon", lambda i: (i + (4 if (i // 2) % 2 == 0 else -4)) % ring) + across
    early = [["partner", "same"], [partner, same[:1]], halos, qkv_weight, query, state]
    state = stage(*early, starts=[[0], [0]])

    *rest, state = lax.optimization_barrier((*across, *same, state))
    across, same = rest[:PARTS], rest[PARTS:]
    near = [swapped(s, a) for s, a in zip(same, across)]
    final = (local, out_weight, [*partner, *own, *same, *across, *near, *halos])
    late = [["across", "same", "near"], [across, same[1:], near], [], qkv_weight, query, state, final]
    result = stage(*late, starts=[[0, half], [half], [0, half]])
    return result[None, None]


def solution(mesh):
    in_specs = (
        P("lat", "lon", None, None),
        P(),
        P(),
        P(),
        P("lat"),
        P(),
        P("lat", "lon", None, None),
    )
    out_specs = P("lat", "lon", None, None)
    return jax.shard_map(
        on_device, mesh=mesh, in_specs=in_specs, out_specs=out_specs, check_vma=False
    )
```
